32 devices in a mesh: ctx: 16 (over z, y, x), vid: 2 (over core).
Axes of the slice: x: 2, y: 2, z: 4, core: 2. Of those that a mesh axis runs over, the one named last changes fastest.
Arguments:
- features: bfloat16 [2, 32, 8, 32, 256], P('vid', 'ctx'), may hold values from -6 to 6
- grad_out: bfloat16 [2, 32, 8, 32, 128], P('vid', 'ctx'), may hold values from -6 to 6
- mean_saved: float32 [2, 32], P('vid'), may hold values from -3 to 3
- rstd_saved: float32 [2, 32], P('vid'), may hold values from 0.5 to 2
- latent: float32 [2, 8, 16, 16], P('vid'), may hold values from -6 to 6
- gamma: float32 [256], replicated, may hold values from 0.5 to 1.5
- beta: float32 [256], replicated, may hold values from -3 to 3
- w_scale: float32 [16, 256], replicated, may hold values from -1.5 to 1.5
- b_scale: float32 [256], replicated, may hold values from -3 to 3
- w_shift: float32 [16, 256], replicated, may hold values from -1.5 to 1.5
- b_shift: float32 [256], replicated, may hold values from -3 to 3
- kernel: bfloat16 [6912, 128], replicated, may hold values from -0.078125 to 0.078125
Outputs:
- features_grad: bfloat16 [2, 32, 8, 32, 256], P('vid', 'ctx')
- kernel_grad: float32 [6912, 128], P('ctx', 'vid')
- mod_grads: float32 [2, 16, 256], replicated
- vector_grads: float32 [4, 256], replicated
- latent_grad: float32 [2, 16, 16, 8], P('vid', 'ctx')
The draws below stay inside these ranges and needn't reach their ends.
All inputs are finite; a program needn't handle non-finite values.
Results may differ from the reference program's by a relative error of at most 0.0029.
Values may be sent and summed in bfloat16 or wider, within the bound.
No kernel may reach another device: no remote copies, remote signals or barrier semaphores. Data moves between devices by JAX's collectives and lax.ppermute only.
A program may use at most 64 MiB of HBM per device.

```python
import math
import jax
import jax.numpy as jnp
from jax import lax

H = 8
W = 32
C = 256
CO = 128
CZ = 16
G = 32
VIDEOS = 2
FRAMES = 32
LATENT = 8
LP = 16


def block_levels(own_key, extent, cuts, smallest, largest):
    loudness, own = 1.0, jax.random.fold_in(own_key, 6)
    for position, parts in cuts:
        steps = jnp.exp(jax.random.uniform(jax.random.fold_in(own, position), (parts,), jnp.float32, smallest / len(cuts), largest / len(cuts)))
        loudness = loudness * jnp.repeat(steps, extent[position] // parts).reshape([-1 if axis == position else 1 for axis in range(len(extent))])
    return loudness


def bell_draw(rng, dims, width, reach, cuts=(), kind=jnp.bfloat16):
    drawn = jax.random.normal(rng, dims, jnp.float32) * width
    if len(cuts) > 0:
        drawn = block_levels(rng, dims, cuts, -0.22, 0.18) * drawn
    return jnp.clip(drawn, min=-reach, max=reach).astype(kind)


def setup_inputs(seed: int = 0) -> dict:
    keys = jax.random.split(jax.random.key(seed), 13)
    features = bell_draw(keys[0], (VIDEOS, FRAMES, H, W, C), 1.0, 6.0, ((0, 2), (1, 16)))
    grad_out = bell_draw(keys[1], (VIDEOS, FRAMES, H, W, CO), 1.0, 6.0, ((0, 2), (1, 16)))
    mean_saved = bell_draw(keys[2], (VIDEOS, G), 0.4, 3.0, ((0, 2),), jnp.float32)
    rstd_saved = jnp.clip(jnp.exp(math.log(2.0) - 1.3862944 * jax.random.uniform(keys[3], (VIDEOS, G), jnp.float32) ** block_levels(keys[3], (VIDEOS, G), ((0, 2),), -0.2, 0.2)), 0.5, 2.0)
    latent = bell_draw(keys[4], (VIDEOS, LATENT, CZ, LP), 1.0, 6.0, ((0, 2),), jnp.float32)
    gamma = jnp.clip(jax.random.uniform(keys[5], (C,), jnp.float32, 0.5, 1.5), 0.5, 1.5)
    beta = bell_draw(keys[6], (C,), 0.5, 3.0, (), jnp.float32)
    w_scale = bell_draw(keys[7], (CZ, C), CZ ** -0.5, 1.5, (), jnp.float32)
    b_scale = bell_draw(keys[8], (C,), 0.5, 3.0, (), jnp.float32)
    w_shift = bell_draw(keys[9], (CZ, C), CZ ** -0.5, 1.5, (), jnp.float32)
    b_shift = bell_draw(keys[10], (C,), 0.5, 3.0, (), jnp.float32)
    kernel = bell_draw(keys[11], (27 * C, CO), (27 * C) ** -0.5, 0.078125)
    return dict(features=features, grad_out=grad_out, mean_saved=mean_saved, rstd_saved=rstd_saved, latent=latent, gamma=gamma, beta=beta, w_scale=w_scale, b_scale=b_scale, w_shift=w_shift, b_shift=b_shift, kernel=kernel)


highest = lax.Precision.HIGHEST


def spread(table):
    count = table.shape[0]
    grid = table.reshape(count, H // 4, W // 4, C)
    wide = jnp.broadcast_to(grid[:, None, :, None, :, None, :], (count, 4, H // 4, 4, W // 4, 4, C))
    return wide.reshape(count * 4, H, W, C)


def pool_blocks(field):
    count = field.shape[0] // 4
    return field.reshape(count, 4, H // 4, 4, W // 4, 4, C).sum(axis=(1, 3, 5)).reshape(count, LP, C)


def reference(features, grad_out, mean_saved, rstd_saved, latent, gamma, beta, w_scale, b_scale, w_shift, b_shift, kernel):
    tap_weights = kernel.reshape(3, 3, 3, C, CO)

    def one_video(operands):
        frames_in, grads_in, mean_row, rstd_row, latent_row = operands
        mean_chan = jnp.broadcast_to(mean_row[:, None], (G, C // G)).reshape(C)
        rstd_chan = jnp.broadcast_to(rstd_row[:, None], (G, C // G)).reshape(C)
        normed = (frames_in.astype(jnp.float32) - mean_chan) * rstd_chan
        scale_tab = jnp.einsum('tzp,zc->tpc', latent_row, w_scale, precision=highest) + b_scale
        shift_tab = jnp.einsum('tzp,zc->tpc', latent_row, w_shift, precision=highest) + b_shift
        scale_map = spread(scale_tab)
        shift_map = spread(shift_tab)
        base_map = normed * gamma + beta
        modulated = base_map * scale_map + shift_map
        squashed = jax.nn.sigmoid(modulated)
        activated = (modulated * squashed).astype(jnp.bfloat16)
        padded = jnp.concatenate([activated[:1], activated[:1], activated], 0)
        padded = jnp.pad(padded, ((0, 0), (1, 1), (1, 1), (0, 0)))
        grads_rows = grads_in.reshape(FRAMES * H * W, CO)
        grad_pad = jnp.pad(grads_in, ((2, 2), (1, 1), (1, 1), (0, 0)))
        extended = jnp.zeros(((FRAMES + 2) * H * W, C), jnp.float32)
        pieces = []
        for frame_tap in range(3):
            for row_tap in range(3):
                for col_tap in range(3):
                    window = padded[frame_tap:frame_tap + FRAMES, row_tap:row_tap + H, col_tap:col_tap + W].reshape(FRAMES * H * W, C)
                    pieces.append(lax.dot_general(window, grads_rows, (((0,), (0,)), ((), ())), preferred_element_type=jnp.float32))
                    source = grad_pad[2 - frame_tap:4 - frame_tap + FRAMES, 2 - row_tap:2 - row_tap + H, 2 - col_tap:2 - col_tap + W].reshape((FRAMES + 2) * H * W, CO)
                    extended = extended + lax.dot_general(source, tap_weights[frame_tap, row_tap, col_tap], (((1,), (1,)), ((), ())), preferred_element_type=jnp.float32)
        kernel_part = jnp.stack(pieces).reshape(27 * C, CO)
        extended = extended.reshape(FRAMES + 2, H, W, C)
        act_grad = extended[2:].at[0].add(extended[0] + extended[1])
        pre_grad = act_grad * squashed * (1.0 + modulated * (1.0 - squashed))
        features_grad = (pre_grad * scale_map * gamma * rstd_chan).astype(jnp.bfloat16)
        scale_pool = pool_blocks(pre_grad * base_map)
        shift_pool = pool_blocks(pre_grad)
        mod_part = jnp.stack([jnp.einsum('tzp,tpc->zc', latent_row, scale_pool, precision=highest),
                              jnp.einsum('tzp,tpc->zc', latent_row, shift_pool, precision=highest)])
        vec_part = jnp.stack([jnp.sum(pre_grad * scale_map * normed, axis=(0, 1, 2)),
                              jnp.sum(pre_grad * scale_map, axis=(0, 1, 2)),
                              jnp.sum(scale_pool, axis=(0, 1)),
                              jnp.sum(shift_pool, axis=(0, 1))])
        latent_sum = jnp.einsum('zc,tpc->tzp', w_scale, scale_pool, precision=highest) + jnp.einsum('zc,tpc->tzp', w_shift, shift_pool, precision=highest)
        latent_part = latent_sum.reshape(LATENT, CZ, 2, LP // 2).transpose(0, 2, 1, 3).reshape(2 * LATENT, CZ, LP // 2)
        return features_grad, kernel_part, mod_part, vec_part, latent_part

    results = lax.map(one_video, (features, grad_out, mean_saved, rstd_saved, latent))
    return (results[0], results[1].sum(axis=0), results[2].sum(axis=0), results[3].sum(axis=0), results[4])
```

```python
import math

import jax
import jax.numpy as jnp
from jax import lax
from jax.sharding import PartitionSpec as P

FR_DEV = 2
H = 8
W = 32
C = 256
CO = 128
G = 32
LP = 16
NEAR = 4


highest = lax.Precision.HIGHEST


def passed_along(value, axis, steps):
    count = lax.axis_size(axis)
    leading, last = (max(0, -steps), min(count, count - steps))
    return lax.ppermute(value, axis, [(source, source + steps) for source in range(leading, last)])


def swapped(value, axis, apart):
    mask = 2**apart
    pairs = [(source, source ^ mask) for source in range(lax.axis_size(axis))]
    return lax.ppermute(value, axis, pairs)


def rotated(value, turn, axis):
    count = lax.axis_size(axis)
    return lax.ppermute(value, axis, [(source, (source + turn) % count) for source in range(count)])


def near_groups(count):
    near = math.gcd(count, NEAR)
    base = [source - source % near for source in range(count)]
    return near, lambda source, turn: base[source] + (source + turn) % near


def far_groups(count):
    near = math.gcd(count, NEAR)
    return count // near, lambda source, turn: (source + turn * near) % count


def exchange_sum(value, axis, groups):
    count = lax.axis_size(axis)
    size, target = groups(count)
    total = value
    for turn in range(1, size):
        total = total + lax.ppermute(value, axis, [(s, target(s, turn)) for s in range(count)])
    return total


def scatter_sum(blocks, place, groups):
    count = lax.axis_size("ctx")
    size, target = groups(count)
    total = lax.dynamic_index_in_dim(blocks, place, 0, keepdims=False)
    narrow = blocks.astype(jnp.bfloat16)
    for turn in range(1, size):
        sent = lax.dynamic_index_in_dim(narrow, (place + turn) % size, 0, keepdims=False)
        got = lax.ppermute(sent, "ctx", [(s, target(s, turn)) for s in range(count)])
        total = total + got.astype(jnp.float32)
    return total


def spread_frame(table):
    grid = table.reshape(H // 4, W // 4, C)
    wide = jnp.broadcast_to(grid[:, None, :, None, :], (H // 4, 4, W // 4, 4, C))
    return wide.reshape(1, H, W, C)


def pool_frames(field):
    frames = field.shape[0]
    return field.reshape(frames, H // 4, 4, W // 4, 4, C).sum(axis=(0, 2, 4)).reshape(LP, C)


def transpose_conv(grad_pad, tap_weights, frames):
    total = jnp.zeros((frames * H * W, C), jnp.float32)
    for frame_tap in range(3):
        for row_tap in range(3):
            for col_tap in range(3):
                source = grad_pad[
                    2 - frame_tap : 2 - frame_tap + frames,
                    2 - row_tap : 2 - row_tap + H,
                    2 - col_tap : 2 - col_tap + W,
                ].reshape(frames * H * W, CO)
                total = total + lax.dot_general(
                    source,
                    tap_weights[frame_tap, row_tap, col_tap],
                    (((1,), (1,)), ((), ())),
                    preferred_element_type=jnp.float32,
                )
    return total.reshape(frames, H, W, C)


def local(
    features,
    grad_out,
    mean_saved,
    rstd_saved,
    latent,
    gamma,
    beta,
    w_scale,
    b_scale,
    w_shift,
    b_shift,
    kernel,
):
    device = lax.axis_index("ctx")
    frames_in = features[0]
    grads_in = grad_out[0]
    mean_chan = jnp.broadcast_to(mean_saved[0][:, None], (G, C // G)).reshape(C)
    rstd_chan = jnp.broadcast_to(rstd_saved[0][:, None], (G, C // G)).reshape(C)
    normed = (frames_in.astype(jnp.float32) - mean_chan) * rstd_chan
    latent_frame = lax.dynamic_index_in_dim(latent[0], device // 2, 0, keepdims=False)
    scale_tab = jnp.einsum("zp,zc->pc", latent_frame, w_scale, precision=highest) + b_scale
    shift_tab = jnp.einsum("zp,zc->pc", latent_frame, w_shift, precision=highest) + b_shift
    scale_map = spread_frame(scale_tab)
    shift_map = spread_frame(shift_tab)
    base_map = normed * gamma + beta
    modulated = base_map * scale_map + shift_map
    squashed = jax.nn.sigmoid(modulated)
    activated = (modulated * squashed).astype(jnp.bfloat16)
    before = passed_along(activated, "ctx", 1)
    leading = jnp.broadcast_to(activated[:1], before.shape)
    before = jnp.where(device == 0, leading, before)
    padded = jnp.pad(jnp.concatenate([before, activated], 0), ((0, 0), (1, 1), (1, 1), (0, 0)))
    tap_weights = kernel.reshape(3, 3, 3, C, CO)
    grads_rows = grads_in.reshape(FR_DEV * H * W, CO)
    pieces = []
    for frame_tap in range(3):
        for row_tap in range(3):
            for col_tap in range(3):
                window = padded[
                    frame_tap : frame_tap + FR_DEV, row_tap : row_tap + H, col_tap : col_tap + W
                ].reshape(FR_DEV * H * W, C)
                pieces.append(
                    lax.dot_general(
                        window,
                        grads_rows,
                        (((0,), (0,)), ((), ())),
                        preferred_element_type=jnp.float32,
                    )
                )
    kernel_term = jnp.stack(pieces).reshape(27 * C, CO)
    beyond = passed_along(grads_in, "ctx", -1)
    grad_pad = jnp.pad(jnp.concatenate([grads_in, beyond], 0), ((2, 0), (1, 1), (1, 1), (0, 0)))
    extended = transpose_conv(grad_pad, tap_weights, FR_DEV + 2)
    act_grad = extended[2:]
    virtual = jnp.where(device == 0, extended[0] + extended[1], 0.0)
    act_grad = act_grad.at[0].add(virtual)
    pre_grad = act_grad * squashed * (1.0 + modulated * (1.0 - squashed))
    features_grad = (pre_grad * scale_map * gamma * rstd_chan).astype(jnp.bfloat16)
    scale_pool = pool_frames(pre_grad * base_map)
    shift_pool = pool_frames(pre_grad)
    mod_part = jnp.stack(
        [
            jnp.einsum("zp,pc->zc", latent_frame, scale_pool, precision=highest),
            jnp.einsum("zp,pc->zc", latent_frame, shift_pool, precision=highest),
        ]
    )
    vec_part = jnp.stack(
        [
            jnp.sum(pre_grad * scale_map * normed, axis=(0, 1, 2)),
            jnp.sum(pre_grad * scale_map, axis=(0, 1, 2)),
            jnp.sum(scale_pool, axis=0),
            jnp.sum(shift_pool, axis=0),
        ]
    )
    latent_sum = jnp.einsum("zc,pc->zp", w_scale, scale_pool, precision=highest) + jnp.einsum(
        "zc,pc->zp", w_shift, shift_pool, precision=highest
    )
    half_len = LP // 2
    parity = device % 2
    own_half = lax.dynamic_slice_in_dim(latent_sum, parity * half_len, half_len, 1)
    far_half = lax.dynamic_slice_in_dim(latent_sum, (1 - parity) * half_len, half_len, 1)
    received = swapped(far_half, "ctx", 0)
    latent_grad = (own_half + received)[None, None]
    small = jnp.concatenate([mod_part.reshape(-1, C), vec_part], 0)
    small = small + rotated(small, 1, "vid")
    small = exchange_sum(small, "ctx", near_groups)
    small = exchange_sum(small, "ctx", far_groups)
    mod_grads = small[: 2 * latent.shape[2]].reshape(2, latent.shape[2], C)
    vector_grads = small[2 * latent.shape[2] :]

    videos = lax.axis_size("vid")
    count = lax.axis_size("ctx")
    near = math.gcd(count, NEAR)
    far = count // near
    rows, cols = 27 * C // count, CO // videos
    piece = -(-rows // (16 * videos)) * 16
    blocks = kernel_term.reshape(count, rows, videos, cols)
    blocks = jnp.pad(blocks, ((0, 0), (0, videos * piece - rows), (0, 0), (0, 0)))
    blocks = blocks.reshape(count, videos, piece, videos, cols)
    blocks = blocks.transpose(3, 0, 2, 1, 4).reshape(videos, count, piece, CO)
    here = lax.axis_index("vid")
    total = lax.dynamic_index_in_dim(blocks, here, 0, keepdims=False)
    for turn in range(1, videos):
        sent = lax.dynamic_index_in_dim(blocks, (here + turn) % videos, 0, keepdims=False)
        total = total + rotated(sent, turn, "vid")
    blocks = total.reshape(far, near, piece, CO).transpose(1, 0, 2, 3)
    total = scatter_sum(blocks, device % near, near_groups)
    total = scatter_sum(total, device // near, far_groups)
    kernel_grad = total.reshape(piece, videos, cols).transpose(1, 0, 2).reshape(videos * piece, cols)[:rows]
    return (features_grad[None], kernel_grad, mod_grads, vector_grads, latent_grad)


def solution(mesh):
    placed = (
        P("vid", "ctx", None, None, None),
        P("vid", "ctx", None, None, None),
        P("vid", None),
        P("vid", None),
        P("vid", None, None, None),
        P(),
        P(),
        P(),
        P(),
        P(),
        P(),
        P(),
    )
    return jax.shard_map(
        local,
        mesh=mesh,
        in_specs=placed,
        out_specs=(
            P("vid", "ctx", None, None, None),
            P("ctx", "vid"),
            P(),
            P(),
            P("vid", "ctx", None, None),
        ),
        check_vma=False,
    )
```

```python
import functools
import math

import jax
import jax.numpy as jnp
from jax import lax
from jax.experimental import pallas as pl
from jax.experimental.pallas import tpu as pltpu
from jax.sharding import PartitionSpec as P

NEAR = 4
CELL = 4
TAPS = 3
TILE = 16

f32 = jnp.float32
bf16 = jnp.bfloat16
dot = functools.partial(lax.dot_general, preferred_element_type=f32)
exact = functools.partial(dot, precision=lax.Precision.HIGHEST)
ROWS_COLS = (((1,), (0,)), ((), ()))
ROWS_ROWS = (((1,), (1,)), ((), ()))
COLS_COLS = (((0,), (0,)), ((), ()))


def call(body, outs, scratch=(), name=None):
    return pl.pallas_call(
        body,
        out_shape=outs,
        scratch_shapes=list(scratch),
        name=name,
        compiler_params=pltpu.CompilerParams(vmem_limit_bytes=50 * 2**20),
    )


def shaped(shape, kind=f32):
    return jax.ShapeDtypeStruct(shape, kind)


def paired(place, turn, size):
    return place ^ turn if size & (size - 1) == 0 else (place + turn) % size


def cell_matrix(height, width, cells):
    pixel = lax.broadcasted_iota(jnp.int32, (height * width, cells), 0)
    cell = lax.broadcasted_iota(jnp.int32, (height * width, cells), 1)
    place = (pixel // width) // CELL * (width // CELL) + pixel % width // CELL
    return jnp.where(place == cell, 1.0, 0.0).astype(f32)


def modulate_body(frames, height, width, feats, mean, rstd, latent, gamma, beta, ws, bs, wt, bt,
                  act_t, slope, normed_out, gain_out, tab_out):
    chans = feats.shape[1]
    groups = mean.shape[1]
    pixels = height * width
    lat = latent[0, lax.axis_index("ctx") * frames // CELL]
    group = lax.broadcasted_iota(jnp.int32, (groups, chans), 0)
    chan = lax.broadcasted_iota(jnp.int32, (groups, chans), 1)
    member = jnp.where(chan // (chans // groups) == group, 1.0, 0.0).astype(f32)
    mean_chan = exact(mean[...], member, ROWS_COLS)
    rstd_chan = exact(rstd[...], member, ROWS_COLS)
    scale_tab = exact(lat, ws[...], COLS_COLS) + bs[...]
    shift_tab = exact(lat, wt[...], COLS_COLS) + bt[...]
    tab_out[...] = scale_tab
    cells = cell_matrix(height, width, lat.shape[1])
    scale_map = exact(cells, scale_tab, ROWS_COLS)
    shift_map = exact(cells, shift_tab, ROWS_COLS)
    gain_out[...] = scale_map * (gamma[...] * rstd_chan)
    for frame in range(frames):
        at = pl.ds(frame * pixels, pixels)
        normed = (feats[at, :].astype(f32) - mean_chan) * rstd_chan
        modulated = (normed * gamma[...] + beta[...]) * scale_map + shift_map
        squashed = jax.nn.sigmoid(modulated)
        normed_out[at, :] = normed
        slope[at, :] = squashed * (1.0 + modulated * (1.0 - squashed))
        act_t[:, at] = (modulated * squashed).T.astype(bf16)


def column_shifts(value, width):
    column = lax.broadcasted_iota(jnp.int32, value.shape, 0) % width
    rows = value.shape[0]
    return (
        jnp.where(column == width - 1, 0.0, pltpu.roll(value, rows - 1, 0)),
        value,
        jnp.where(column == 0, 0.0, pltpu.roll(value, 1, 0)),
    )


def clear_borders(padded, width):
    lead = padded.shape[:-2]
    length, lanes = padded.shape[-2:]
    edge = jnp.zeros(lead + (width, lanes), padded.dtype)
    every = (slice(None),) * len(lead)
    padded[every + (slice(0, width),)] = edge
    padded[every + (slice(length - width, length),)] = edge


def input_grad_body(frames, height, width, grads, beyond, weights, slope, normed, gain, tab, latent,
                    ws, wt, gamma, beta, feats_grad, small, lat_own, lat_far, shifted, total):
    pixels = height * width
    chans = gain.shape[1]
    device = lax.axis_index("ctx")
    clear_borders(shifted, width)
    for half, source in enumerate((grads, beyond)):
        for col, value in enumerate(column_shifts(source[...].astype(f32), width)):
            for frame in range(frames):
                shifted[col, half * frames + frame, width:width + pixels] = (
                    value[frame * pixels:(frame + 1) * pixels].astype(bf16))

    def window(frame, row, col):
        start = (TAPS - 1 - row) * width
        return shifted[col, frame, start:start + pixels]

    def filters(step):
        return jnp.concatenate(
            [weights[(step * TAPS * TAPS + k) * chans:(step * TAPS * TAPS + k + 1) * chans, :]
             for k in range(TAPS * TAPS)], axis=1)

    def windows(frame_list):
        return jnp.concatenate(
            [jnp.concatenate([window(frame, k // TAPS, k % TAPS) for k in range(TAPS * TAPS)], axis=1)
             for frame in frame_list], axis=0)

    for step in range(TAPS):
        term = dot(windows([t + TAPS - 1 - step for t in range(frames)]), filters(step), ROWS_ROWS)
        total[...] = term if step == 0 else total[...] + term

    @pl.when(device == 0)
    def _():
        for step in range(TAPS - 1):
            for frame in range(TAPS - 1 - step):
                total[0:pixels] += dot(windows([frame]), filters(step), ROWS_ROWS)

    pooled_shift = jnp.zeros((pixels, chans), f32)
    pooled_norm = jnp.zeros((pixels, chans), f32)
    for frame in range(frames):
        at = pl.ds(frame * pixels, pixels)
        pre = total[at, :] * slope[at, :]
        feats_grad[at, :] = (pre * gain[...]).astype(bf16)
        pooled_shift += pre
        pooled_norm += pre * normed[at, :]
    lat = latent[0, device * frames // CELL]
    depth, length = lat.shape
    cells = cell_matrix(height, width, length)
    shift_pool = exact(cells, pooled_shift, COLS_COLS)
    norm_pool = exact(cells, pooled_norm, COLS_COLS)
    scale_pool = norm_pool * gamma[...] + shift_pool * beta[...]
    small[0:depth] = exact(lat, scale_pool, ROWS_COLS)
    small[depth:2 * depth] = exact(lat, shift_pool, ROWS_COLS)
    for row, field in enumerate((norm_pool * tab[...], shift_pool * tab[...], scale_pool, shift_pool)):
        small[2 * depth + row:2 * depth + row + 1] = jnp.sum(field, axis=0, keepdims=True)
    latent_sum = exact(ws[...], scale_pool, ROWS_ROWS) + exact(wt[...], shift_pool, ROWS_ROWS)
    first, second = latent_sum[:, :length // 2], latent_sum[:, length // 2:]
    even = device % 2 == 0
    lat_own[...] = jnp.where(even, first, second)
    lat_far[...] = jnp.where(even, second, first)


def filter_grad_body(frames, height, width, videos, near, piece, *refs):
    acts, refs = refs[:videos], refs[videos:]
    grads, refs = refs[:videos], refs[videos:]
    beyond, refs = refs[:videos], refs[videos:]
    smalls, refs = refs[:videos], refs[videos:]
    own, sends, small_out, packs, blocks = refs[0], refs[1:near], refs[near], refs[near + 1], refs[near + 2]
    pixels = height * width
    chans = acts[0].shape[0]
    lanes = grads[0].shape[1]
    cols = lanes // videos
    device = lax.axis_index("ctx")
    here = lax.axis_index("vid")
    per = min(videos, TAPS)
    banks = -(-TAPS // per)
    lane = lax.broadcasted_iota(jnp.int32, (1, lanes), 1)
    small_out[...] = functools.reduce(lambda a, b: a + b, [ref[...] for ref in smalls])

    clear_borders(packs, width)
    for video in range(videos):
        for half, source in enumerate((grads[video], beyond[video])):
            value = pltpu.roll(source[...].astype(f32), lax.rem(lanes - here * cols, lanes), 1)
            moved = column_shifts(value, width)
            for bank in range(banks):
                packed = moved[bank * per]
                for k in range(1, min(per, TAPS - bank * per)):
                    packed = jnp.where(lane >= k * cols, pltpu.roll(moved[bank * per + k], k * cols, 1), packed)
                packed = packed.astype(bf16)
                for frame in range(frames):
                    packs[video, bank, half * frames + frame, width:width + pixels] = (
                        packed[frame * pixels:(frame + 1) * pixels])

    def window(video, frame, row, bank):
        start = (TAPS - 1 - row) * width
        return packs[video, bank, frame, start:start + pixels]

    slots = [(row, bank) for row in range(TAPS) for bank in range(banks)]

    def windows(video, frame):
        return jnp.concatenate([window(video, frame, row, bank) for row, bank in slots], axis=1)

    far, rows = blocks.shape[0], TAPS**3 * chans // (blocks.shape[0] * near)
    every = jnp.concatenate([ref[...] for ref in acts], axis=1)
    firsts = jnp.concatenate([ref[:, 0:pixels] for ref in acts], axis=1)
    if piece * videos > rows:
        blocks[:, :, piece - TILE:] = jnp.zeros((far, near, TILE, lanes), f32)

    for step in range(TAPS):
        right = jnp.concatenate(
            [windows(video, t + TAPS - 1 - step) for video in range(videos) for t in range(frames)], axis=0)
        result = dot(every, right, ROWS_COLS)

        def put(result, add, step=step):
            for place, (row, bank) in enumerate(slots):
                tile = result[:, place * lanes:(place + 1) * lanes]
                for k in range(min(per, TAPS - bank * per)):
                    tap = (step * TAPS + row) * TAPS + bank * per + k
                    done = 0
                    while done < chans:
                        index = tap * chans + done
                        owner, inside = index // rows, index % rows
                        part, at = inside // piece, inside % piece
                        length = min(chans - done, rows - inside, piece - at)
                        turn = (part - k) * cols % lanes
                        value = tile[done:done + length]
                        if turn:
                            value = pltpu.roll(value, turn, 1)
                        dest = blocks.at[owner // near, owner % near, at:at + length, part * cols:(part + 1) * cols]
                        value = value[:, part * cols:(part + 1) * cols]
                        dest[...] = dest[...] + value if add else value
                        done += length

        put(result, False)
        if step < TAPS - 1:
            @pl.when(device == 0)
            def _(step=step, put=put):
                right = jnp.concatenate([windows(video, 0) for video in range(videos)], axis=0)
                extra = dot(firsts, right, ROWS_COLS)
                for frame in range(1, TAPS - 1 - step):
                    right = jnp.concatenate([windows(video, frame) for video in range(videos)], axis=0)
                    extra = extra + dot(firsts, right, ROWS_COLS)
                put(extra, True)

    me = device % near
    own[...] = blocks[:, me]
    for turn, send in enumerate(sends, 1):
        send[...] = blocks[:, paired(me, turn, near)].astype(bf16)


def plane_sum_body(near, far, *refs):
    own, got, refs = refs[0], refs[1:near], refs[near:]
    smalls, refs = refs[:far], refs[far:]
    kept, sends, small_out, total = refs[0], refs[1:far], refs[far], refs[far + 1]
    total[...] = functools.reduce(lambda a, b: a + b[...].astype(f32), got, own[...])
    small_out[...] = functools.reduce(lambda a, b: a + b, [ref[...] for ref in smalls])
    me = lax.axis_index("ctx") // near
    kept[...] = total[me]
    for turn, send in enumerate(sends, 1):
        send[...] = total[paired(me, turn, far)].astype(bf16)


def line_sum_body(near, far, *refs):
    kept, got, refs = refs[0], refs[1:far], refs[far:]
    smalls, refs = refs[:near], refs[near:]
    lat_own, lat_got, filter_grad, mod_grads, vector_grads, latent_grad = refs
    total = functools.reduce(lambda a, b: a + b[...].astype(f32), got, kept[...])
    rows, cols = filter_grad.shape
    piece, lanes = total.shape
    for part in range(lanes // cols):
        first, last = part * piece, min(rows, (part + 1) * piece)
        if first < last:
            filter_grad[first:last] = total[:last - first, part * cols:(part + 1) * cols]
    small = functools.reduce(lambda a, b: a + b, [ref[...] for ref in smalls])
    mod_grads[...] = small[:mod_grads.shape[0]]
    vector_grads[...] = small[mod_grads.shape[0]:]
    latent_grad[...] = lat_own[...] + lat_got[...]


def local(features, grad_out, mean, rstd, latent, gamma, beta, ws, bs, wt, bt, kernel):
    _, frames, height, width, chans = features.shape
    outs = grad_out.shape[-1]
    depth, length = latent.shape[2:]
    count, videos = lax.axis_size("ctx"), lax.axis_size("vid")
    near = math.gcd(count, NEAR)
    far = count // near
    pixels = height * width
    size = frames * pixels
    rows, cols = TAPS**3 * chans // count, outs // videos
    piece = -(-rows // (TILE * videos)) * TILE
    gamma, beta, bs, bt = (value.reshape(1, chans) for value in (gamma, beta, bs, bt))
    feats = features.reshape(size, chans)
    grads = grad_out.reshape(size, outs)

    def along_ctx(value, target):
        return lax.ppermute(value, "ctx", [(s, target(s)) for s in range(count)])

    def others(value):
        return [value] + [
            lax.ppermute(value, "vid", [(s, (s + turn) % videos) for s in range(videos)])
            for turn in range(1, videos)]

    def near_got(values):
        return [along_ctx(value, lambda s: s - s % near + paired(s % near, turn, near))
                for turn, value in enumerate(values, 1)]

    def far_got(values):
        return [along_ctx(value, lambda s: paired(s // near, turn, far) * near + s % near)
                for turn, value in enumerate(values, 1)]

    beyond = lax.ppermute(grads, "ctx", [(s, s - 1) for s in range(1, count)])
    act_t, slope, normed, gain, tab = call(
        functools.partial(modulate_body, frames, height, width),
        (shaped((chans, size), bf16), shaped((size, chans)), shaped((size, chans)), shaped((pixels, chans)),
         shaped((length, chans))),
        name="modulate",
    )(feats, mean, rstd, latent, gamma, beta, ws, bs, wt, bt)
    grads_all, acts_all, beyond_all = others(grads), others(act_t), others(beyond)
    small_rows = 2 * depth + 4
    feats_grad, small, lat_own, lat_far = call(
        functools.partial(input_grad_body, frames, height, width),
        (shaped((size, chans), bf16), shaped((small_rows, chans)), shaped((depth, length // 2)),
         shaped((depth, length // 2))),
        (pltpu.VMEM((TAPS, 2 * frames, (height + 2) * width, outs), bf16), pltpu.VMEM((size, chans), f32)),
        name="input_grad",
    )(grads, beyond, kernel, slope, normed, gain, tab, latent, ws, wt, gamma, beta)
    lat_got = along_ctx(lat_far, lambda s: s ^ 1)
    banks = -(-TAPS // min(videos, TAPS))
    own, *sends = call(
        functools.partial(filter_grad_body, frames, height, width, videos, near, piece),
        [shaped((far, piece, outs))] + [shaped((far, piece, outs), bf16)] * (near - 1)
        + [shaped((small_rows, chans))],
        (pltpu.VMEM((videos, banks, 2 * frames, (height + 2) * width, outs), bf16),
         pltpu.VMEM((far, near, piece, outs), f32)),
        name="filter_grad",
    )(*acts_all, *grads_all, *beyond_all, *others(small))
    small = sends.pop()
    kept, *sends = call(
        functools.partial(plane_sum_body, near, far),
        [shaped((piece, outs))] + [shaped((piece, outs), bf16)] * (far - 1) + [shaped((small_rows, chans))],
        (pltpu.VMEM((far, piece, outs), f32),),
        name="plane_sum",
    )(own, *near_got(sends), small, *far_got([small] * (far - 1)))
    small = sends.pop()
    filter_grad, mod_grads, vector_grads, latent_grad = call(
        functools.partial(line_sum_body, near, far),
        (shaped((rows, cols)), shaped((2 * depth, chans)), shaped((4, chans)), shaped((depth, length // 2))),
        name="line_sum",
    )(kept, *far_got(sends), small, *near_got([small] * (near - 1)), lat_own, lat_got)
    return (
        feats_grad.reshape(features.shape),
        filter_grad,
        mod_grads.reshape(2, depth, chans),
        vector_grads,
        latent_grad[None, None],
    )


def solution(mesh):
    split = P("vid", "ctx", None, None, None)
    return jax.shard_map(
        local,
        mesh=mesh,
        in_specs=(split, split, P("vid", None), P("vid", None), P("vid", None, None, None)) + (P(),) * 7,
        out_specs=(split, P("ctx", "vid"), P(), P(), P("vid", "ctx", None, None)),
        check_vma=False,
    )
```

```python
import functools
import math

import jax
import jax.numpy as jnp
from jax import lax
from jax.experimental import pallas as pl
from jax.experimental.pallas import tpu as pltpu
from jax.sharding import PartitionSpec as P

NEAR = 4
CELL = 4
TAPS = 3
TILE = 16

f32 = jnp.float32
bf16 = jnp.bfloat16
dot = functools.partial(lax.dot_general, preferred_element_type=f32)
exact = functools.partial(dot, precision=lax.Precision.HIGHEST)
ROWS_COLS = (((1,), (0,)), ((), ()))
ROWS_ROWS = (((1,), (1,)), ((), ()))
COLS_COLS = (((0,), (0,)), ((), ()))


def call(body, outs, scratch=(), name=None, far_args=()):
    def run(*args):
        args = [pltpu.with_memory_space_constraint(arg, pltpu.HBM) if k in far_args else arg
                for k, arg in enumerate(args)]

        def full(*refs):
            refs = list(refs)
            sems = refs.pop()
            buffers = [refs.pop() for _ in far_args][::-1]
            moves = [pltpu.make_async_copy(refs[at], buffer, sems.at[k])
                     for k, (at, buffer) in enumerate(zip(far_args, buffers))]
            for move in moves:
                move.start()
            for at, buffer in zip(far_args, buffers):
                refs[at] = buffer
            for move in moves:
                move.wait()
            body(*refs)

        return pl.pallas_call(
            full if far_args else body,
            out_shape=outs,
            in_specs=[pl.BlockSpec(memory_space=pltpu.HBM if k in far_args else pltpu.VMEM) for k in range(len(args))],
            scratch_shapes=list(scratch) + [pltpu.VMEM(args[k].shape, args[k].dtype) for k in far_args]
            + ([pltpu.SemaphoreType.DMA((len(far_args),))] if far_args else []),
            name=name,
            compiler_params=pltpu.CompilerParams(vmem_limit_bytes=50 * 2**20),
        )(*args)

    return run


def halves(value):
    top = value.astype(bf16)
    return top, (value - top.astype(f32)).astype(bf16)


def shaped(shape, kind=f32):
    return jax.ShapeDtypeStruct(shape, kind)


def paired(place, turn, size):
    return place ^ turn if size & (size - 1) == 0 else (place + turn) % size


def cell_matrix(height, width, cells):
    pixel = lax.broadcasted_iota(jnp.int32, (height * width, cells), 0)
    cell = lax.broadcasted_iota(jnp.int32, (height * width, cells), 1)
    place = (pixel // width) // CELL * (width // CELL) + pixel % width // CELL
    return jnp.where(place == cell, 1.0, 0.0).astype(f32)


def modulate_body(frames, height, width, feats, mean, rstd, latent, gamma, beta, ws, bs, wt, bt,
                  act_t, slope, normed_out, gain_out, tab_out):
    chans = feats.shape[1]
    groups = mean.shape[1]
    pixels = height * width
    lat = latent[0, lax.axis_index("ctx") * frames // CELL]
    group = lax.broadcasted_iota(jnp.int32, (groups, chans), 0)
    chan = lax.broadcasted_iota(jnp.int32, (groups, chans), 1)
    member = jnp.where(chan // (chans // groups) == group, 1.0, 0.0).astype(f32)
    mean_chan = exact(mean[...], member, ROWS_COLS)
    rstd_chan = exact(rstd[...], member, ROWS_COLS)
    scale_tab = exact(lat, ws[...], COLS_COLS) + bs[...]
    shift_tab = exact(lat, wt[...], COLS_COLS) + bt[...]
    tab_out[...] = scale_tab
    cells = cell_matrix(height, width, lat.shape[1])
    scale_map = exact(cells, scale_tab, ROWS_COLS)
    shift_map = exact(cells, shift_tab, ROWS_COLS)
    gain_out[...] = scale_map * (gamma[...] * rstd_chan)
    for frame in range(frames):
        at = pl.ds(frame * pixels, pixels)
        normed = (feats[at, :].astype(f32) - mean_chan) * rstd_chan
        modulated = (normed * gamma[...] + beta[...]) * scale_map + shift_map
        squashed = jax.nn.sigmoid(modulated)
        normed_out[at, :] = normed
        slope[at, :] = squashed * (1.0 + modulated * (1.0 - squashed))
        act_t[:, at] = (modulated * squashed).T.astype(bf16)


def column_shifts(value, width):
    column = lax.broadcasted_iota(jnp.int32, value.shape, 0) % width
    rows = value.shape[0]
    return (
        jnp.where(column == width - 1, 0.0, pltpu.roll(value, rows - 1, 0)),
        value,
        jnp.where(column == 0, 0.0, pltpu.roll(value, 1, 0)),
    )


def clear_borders(padded, width):
    lead = padded.shape[:-2]
    length, lanes = padded.shape[-2:]
    edge = jnp.zeros(lead + (width, lanes), padded.dtype)
    every = (slice(None),) * len(lead)
    padded[every + (slice(0, width),)] = edge
    padded[every + (slice(length - width, length),)] = edge


def input_grad_body(frames, height, width, grads, beyond, weights, slope, normed, gain, tab, latent,
                    ws, wt, gamma, beta, feats_grad, small, lat_own, lat_far, shifted, total):
    pixels = height * width
    chans = gain.shape[1]
    device = lax.axis_index("ctx")
    clear_borders(shifted, width)
    for half, source in enumerate((grads, beyond)):
        for col, value in enumerate(column_shifts(source[...].astype(f32), width)):
            for frame in range(frames):
                shifted[col, half * frames + frame, width:width + pixels] = (
                    value[frame * pixels:(frame + 1) * pixels].astype(bf16))

    def window(frame, row, col):
        start = (TAPS - 1 - row) * width
        return shifted[col, frame, start:start + pixels]

    def filters(step):
        return jnp.concatenate(
            [weights[(step * TAPS * TAPS + k) * chans:(step * TAPS * TAPS + k + 1) * chans, :]
             for k in range(TAPS * TAPS)], axis=1)

    def windows(frame_list):
        return jnp.concatenate(
            [jnp.concatenate([window(frame, k // TAPS, k % TAPS) for k in range(TAPS * TAPS)], axis=1)
             for frame in frame_list], axis=0)

    for step in range(TAPS):
        term = dot(windows([t + TAPS - 1 - step for t in range(frames)]), filters(step), ROWS_ROWS)
        total[...] = term if step == 0 else total[...] + term

    @pl.when(device == 0)
    def _():
        for step in range(TAPS - 1):
            for frame in range(TAPS - 1 - step):
                total[0:pixels] += dot(windows([frame]), filters(step), ROWS_ROWS)

    pooled_shift = jnp.zeros((pixels, chans), f32)
    pooled_norm = jnp.zeros((pixels, chans), f32)
    for frame in range(frames):
        at = pl.ds(frame * pixels, pixels)
        pre = total[at, :] * slope[at, :]
        feats_grad[at, :] = (pre * gain[...]).astype(bf16)
        pooled_shift += pre
        pooled_norm += pre * normed[at, :]
    lat = latent[0, device * frames // CELL]
    depth, length = lat.shape
    cells = cell_matrix(height, width, length)
    shift_pool = exact(cells, pooled_shift, COLS_COLS)
    norm_pool = exact(cells, pooled_norm, COLS_COLS)
    scale_pool = norm_pool * gamma[...] + shift_pool * beta[...]
    small[0:depth] = exact(lat, scale_pool, ROWS_COLS)
    small[depth:2 * depth] = exact(lat, shift_pool, ROWS_COLS)
    for row, field in enumerate((norm_pool * tab[...], shift_pool * tab[...], scale_pool, shift_pool)):
        small[2 * depth + row:2 * depth + row + 1] = jnp.sum(field, axis=0, keepdims=True)
    latent_sum = exact(scale_pool, ws[...], ROWS_ROWS) + exact(shift_pool, wt[...], ROWS_ROWS)
    first, second = latent_sum[:length // 2], latent_sum[length // 2:]
    even = device % 2 == 0
    lat_own[...] = jnp.where(even, first, second)
    lat_far[...] = jnp.where(even, second, first)


def filter_grad_body(frames, height, width, videos, near, piece, *refs):
    acts, refs = refs[:videos], refs[videos:]
    grads, refs = refs[:videos], refs[videos:]
    beyond, refs = refs[:videos], refs[videos:]
    smalls, refs = refs[:videos], refs[videos:]
    lat_far, own, refs = refs[0], refs[1], refs[2:]
    sends, small_out, packs, blocks = refs[:near - 1], refs[near - 1], refs[near], refs[near + 1]
    pixels = height * width
    chans = acts[0].shape[0]
    lanes = grads[0].shape[1]
    cols = lanes // videos
    device = lax.axis_index("ctx")
    here = lax.axis_index("vid")
    per = min(videos, TAPS)
    banks = -(-TAPS // per)
    lane = lax.broadcasted_iota(jnp.int32, (1, lanes), 1)
    small = functools.reduce(lambda a, b: a + b, [ref[...] for ref in smalls])
    small_out[...] = jnp.zeros_like(small_out)
    for k in range(chans // lanes):
        small_out[k * small.shape[0]:(k + 1) * small.shape[0]] = small[:, k * lanes:(k + 1) * lanes]

    clear_borders(packs, width)
    for video in range(videos):
        for half, source in enumerate((grads[video], beyond[video])):
            value = pltpu.roll(source[...].astype(f32), lax.rem(lanes - here * cols, lanes), 1)
            moved = column_shifts(value, width)
            for bank in range(banks):
                packed = moved[bank * per]
                for k in range(1, min(per, TAPS - bank * per)):
                    packed = jnp.where(lane >= k * cols, pltpu.roll(moved[bank * per + k], k * cols, 1), packed)
                packed = packed.astype(bf16)
                for frame in range(frames):
                    packs[video, bank, half * frames + frame, width:width + pixels] = (
                        packed[frame * pixels:(frame + 1) * pixels])

    def window(video, frame, row, bank):
        start = (TAPS - 1 - row) * width
        return packs[video, bank, frame, start:start + pixels]

    slots = [(row, bank) for row in range(TAPS) for bank in range(banks)]

    def windows(video, frame):
        return jnp.concatenate([window(video, frame, row, bank) for row, bank in slots], axis=1)

    far, rows = blocks.shape[0], TAPS**3 * chans // (blocks.shape[0] * near)
    every = jnp.concatenate([ref[...] for ref in acts], axis=1)
    firsts = jnp.concatenate([ref[:, 0:pixels] for ref in acts], axis=1)
    if piece * videos > rows:
        blocks[:, :, piece - TILE:] = jnp.zeros((far, near, TILE, lanes), f32)

    for step in range(TAPS):
        right = jnp.concatenate(
            [windows(video, t + TAPS - 1 - step) for video in range(videos) for t in range(frames)], axis=0)
        result = dot(every, right, ROWS_COLS)

        def put(result, add, step=step):
            for place, (row, bank) in enumerate(slots):
                tile = result[:, place * lanes:(place + 1) * lanes]
                for k in range(min(per, TAPS - bank * per)):
                    tap = (step * TAPS + row) * TAPS + bank * per + k
                    done = 0
                    while done < chans:
                        index = tap * chans + done
                        owner, inside = index // rows, index % rows
                        part, at = inside // piece, inside % piece
                        length = min(chans - done, rows - inside, piece - at)
                        turn = (part - k) * cols % lanes
                        value = tile[done:done + length]
                        if turn:
                            value = pltpu.roll(value, turn, 1)
                        dest = blocks.at[owner // near, owner % near, at:at + length, part * cols:(part + 1) * cols]
                        value = value[:, part * cols:(part + 1) * cols]
                        dest[...] = dest[...] + value if add else value
                        done += length

        put(result, False)
        if step < TAPS - 1:
            @pl.when(device == 0)
            def _(step=step, put=put):
                right = jnp.concatenate([windows(video, 0) for video in range(videos)], axis=0)
                extra = dot(firsts, right, ROWS_COLS)
                for frame in range(1, TAPS - 1 - step):
                    right = jnp.concatenate([windows(video, frame) for video in range(videos)], axis=0)
                    extra = extra + dot(firsts, right, ROWS_COLS)
                put(extra, True)

    me = device % near
    own[...] = blocks[:, me]
    top, rest = halves(small_out[...])
    count = top.shape[0]
    lat_top, lat_rest = halves(lat_far[...])
    cells, depth = lat_top.shape
    for turn, send in enumerate(sends, 1):
        for k in range(far):
            send[k * piece:(k + 1) * piece] = blocks[k, paired(me, turn, near)].astype(bf16)
        at = far * piece
        send[at:at + count] = top
        send[at + count:at + 2 * count] = rest
        send[at + 2 * count:at + 2 * count + cells, :depth] = lat_top
        send[at + 2 * count + cells:at + 2 * count + 2 * cells, :depth] = lat_rest


def plane_sum_body(near, far, *refs):
    own, got, small, lat_own = refs[0], refs[1:near], refs[near], refs[near + 1]
    kept, sends, small_out, latent_grad, total = (
        refs[near + 2], refs[near + 3:near + far + 2], *refs[near + far + 2:])
    piece = own.shape[1]
    count = small.shape[0]
    cells, depth = lat_own.shape
    for k in range(far):
        total[k] = functools.reduce(lambda a, b: a + b[k * piece:(k + 1) * piece].astype(f32), got, own[k])
    at = far * piece

    def joined(ref, start, length):
        return ref[start:start + length].astype(f32) + ref[start + length:start + 2 * length].astype(f32)

    summed = functools.reduce(lambda a, b: a + joined(b, at, count), got, small[...])
    small_out[...] = summed
    latent_grad[...] = lat_own[...] + joined(got[0], at + 2 * count, cells)[:, :depth]
    me = lax.axis_index("ctx") // near
    kept[...] = total[me]
    top, rest = halves(summed)
    for turn, send in enumerate(sends, 1):
        send[0:piece] = total[paired(me, turn, far)].astype(bf16)
        send[piece:piece + count] = top
        send[piece + count:piece + 2 * count] = rest


def line_sum_body(far, *refs):
    kept, got, small, filter_grad, mod_grads, vector_grads = refs[0], refs[1:far], *refs[far:]
    piece, lanes = kept.shape
    count = small.shape[0]
    total = functools.reduce(lambda a, b: a + b[0:piece].astype(f32), got, kept[...])
    cols, rows = filter_grad.shape
    turned = total.T
    for part in range(lanes // cols):
        first, last = part * piece, min(rows, (part + 1) * piece)
        if first < last:
            filter_grad[:, first:last] = turned[part * cols:(part + 1) * cols, :last - first]
    summed = functools.reduce(
        lambda a, b: a + b[piece:piece + count].astype(f32) + b[piece + count:piece + 2 * count].astype(f32),
        got, small[...])
    split, length = mod_grads.shape[0], mod_grads.shape[0] + vector_grads.shape[0]
    for k in range(mod_grads.shape[1] // lanes):
        mod_grads[:, k * lanes:(k + 1) * lanes] = summed[k * length:k * length + split]
        vector_grads[:, k * lanes:(k + 1) * lanes] = summed[k * length + split:(k + 1) * length]


def local(features, grad_out, mean, rstd, latent, gamma, beta, ws, bs, wt, bt, kernel):
    _, frames, height, width, chans = features.shape
    outs = grad_out.shape[-1]
    depth, length = latent.shape[2:]
    count, videos = lax.axis_size("ctx"), lax.axis_size("vid")
    near = math.gcd(count, NEAR)
    far = count // near
    pixels = height * width
    size = frames * pixels
    rows, cols = TAPS**3 * chans // count, outs // videos
    piece = -(-rows // (TILE * videos)) * TILE
    gamma, beta, bs, bt = (value.reshape(1, chans) for value in (gamma, beta, bs, bt))
    feats = features.reshape(size, chans)
    grads = grad_out.reshape(size, outs)

    def along_ctx(value, target):
        return lax.ppermute(value, "ctx", [(s, target(s)) for s in range(count)])

    def others(value):
        return [value] + [
            lax.ppermute(value, "vid", [(s, (s + turn) % videos) for s in range(videos)])
            for turn in range(1, videos)]

    def near_got(values):
        return [along_ctx(value, lambda s: s - s % near + paired(s % near, turn, near))
                for turn, value in enumerate(values, 1)]

    def far_got(values):
        return [along_ctx(value, lambda s: paired(s // near, turn, far) * near + s % near)
                for turn, value in enumerate(values, 1)]

    beyond = lax.ppermute(grads, "ctx", [(s, s - 1) for s in range(1, count)])
    act_t, slope, normed, gain, tab = call(
        functools.partial(modulate_body, frames, height, width),
        (shaped((chans, size), bf16), shaped((size, chans)), shaped((size, chans)), shaped((pixels, chans)),
         shaped((length, chans))),
        name="modulate",
        far_args=tuple(range(10)),
    )(feats, mean, rstd, latent, gamma, beta, ws, bs, wt, bt)
    grads_all, acts_all, beyond_all = others(grads), others(act_t), others(beyond)
    small_rows = 2 * depth + 4
    cells = length // 2
    feats_grad, small, lat_own, lat_far = call(
        functools.partial(input_grad_body, frames, height, width),
        (shaped((size, chans), bf16), shaped((small_rows, chans)), shaped((cells, depth)), shaped((cells, depth))),
        (pltpu.VMEM((TAPS, 2 * frames, (height + 2) * width, outs), bf16), pltpu.VMEM((size, chans), f32)),
        name="input_grad",
        far_args=(0, 2, 7, 8, 9, 10, 11),
    )(grads, beyond, kernel, slope, normed, gain, tab, latent, ws, wt, gamma, beta)
    banks = -(-TAPS // min(videos, TAPS))
    count_small = -(-small_rows * (chans // outs) // TILE) * TILE
    extra = 2 * count_small + -(-2 * cells // TILE) * TILE
    own, *sends, small = call(
        functools.partial(filter_grad_body, frames, height, width, videos, near, piece),
        [shaped((far, piece, outs))] + [shaped((far * piece + extra, outs), bf16)] * (near - 1)
        + [shaped((count_small, outs))],
        (pltpu.VMEM((videos, banks, 2 * frames, (height + 2) * width, outs), bf16),
         pltpu.VMEM((far, near, piece, outs), f32)),
        name="filter_grad",
        far_args=(videos,),
    )(*acts_all, *grads_all, *beyond_all, *others(small), lat_far)
    kept, *sends, small, latent_grad = call(
        functools.partial(plane_sum_body, near, far),
        [shaped((piece, outs))] + [shaped((piece + 2 * count_small, outs), bf16)] * (far - 1)
        + [shaped((count_small, outs)), shaped((cells, depth))],
        (pltpu.VMEM((far, piece, outs), f32),),
        name="plane_sum",
    )(own, *near_got(sends), small, lat_own)
    filter_grad, mod_grads, vector_grads = call(
        functools.partial(line_sum_body, far),
        (shaped((cols, rows)), shaped((2 * depth, chans)), shaped((4, chans))),
        name="line_sum",
    )(kept, *far_got(sends), small)
    return (
        feats_grad.reshape(features.shape),
        filter_grad.T,
        mod_grads.reshape(2, depth, chans),
        vector_grads,
        latent_grad.T[None, None],
    )


def solution(mesh):
    split = P("vid", "ctx", None, None, None)
    return jax.shard_map(
        local,
        mesh=mesh,
        in_specs=(split, split, P("vid", None), P("vid", None), P("vid", None, None, None)) + (P(),) * 7,
        out_specs=(split, P("ctx", "vid"), P(), P(), P("vid", "ctx", None, None)),
        check_vma=False,
    )
```

```python
import functools
import math

import jax
import jax.numpy as jnp
from jax import lax
from jax.experimental import pallas as pl
from jax.experimental.pallas import tpu as pltpu
from jax.sharding import PartitionSpec as P

NEAR = 4
CELL = 4
TAPS = 3
TILE = 16

f32 = jnp.float32
bf16 = jnp.bfloat16
dot = functools.partial(lax.dot_general, preferred_element_type=f32)
exact = functools.partial(dot, precision=lax.Precision.HIGHEST)
ROWS_COLS = (((1,), (0,)), ((), ()))
ROWS_ROWS = (((1,), (1,)), ((), ()))
COLS_COLS = (((0,), (0,)), ((), ()))


def call(body, outs, scratch=(), name=None, far_args=()):
    def run(*args):
        args = [pltpu.with_memory_space_constraint(arg, pltpu.HBM) if k in far_args else arg
                for k, arg in enumerate(args)]

        def full(*refs):
            refs = list(refs)
            sems = refs.pop()
            buffers = [refs.pop() for _ in far_args][::-1]
            moves = [pltpu.make_async_copy(refs[at], buffer, sems.at[k])
                     for k, (at, buffer) in enumerate(zip(far_args, buffers))]
            for move in moves:
                move.start()
            for at, buffer in zip(far_args, buffers):
                refs[at] = buffer
            for move in moves:
                move.wait()
            body(*refs)

        return pl.pallas_call(
            full if far_args else body,
            out_shape=outs,
            in_specs=[pl.BlockSpec(memory_space=pltpu.HBM if k in far_args else pltpu.VMEM) for k in range(len(args))],
            scratch_shapes=list(scratch) + [pltpu.VMEM(args[k].shape, args[k].dtype) for k in far_args]
            + ([pltpu.SemaphoreType.DMA((len(far_args),))] if far_args else []),
            name=name,
            compiler_params=pltpu.CompilerParams(vmem_limit_bytes=50 * 2**20),
        )(*args)

    return run


def halves(value):
    top = value.astype(bf16)
    return top, (value - top.astype(f32)).astype(bf16)


def shaped(shape, kind=f32):
    return jax.ShapeDtypeStruct(shape, kind)


def paired(place, turn, size):
    return place ^ turn if size & (size - 1) == 0 else (place + turn) % size


def cell_matrix(height, width, cells):
    pixel = lax.broadcasted_iota(jnp.int32, (height * width, cells), 0)
    cell = lax.broadcasted_iota(jnp.int32, (height * width, cells), 1)
    place = (pixel // width) // CELL * (width // CELL) + pixel % width // CELL
    return jnp.where(place == cell, 1.0, 0.0).astype(f32)


def modulate_body(frames, height, width, feats, mean, rstd, latent, gamma, beta, ws, bs, wt, bt,
                  act_t, slope, normed_out, gain_out, tab_out):
    chans = feats.shape[1]
    groups = mean.shape[1]
    pixels = height * width
    lat = latent[0, lax.axis_index("ctx") * frames // CELL]
    group = lax.broadcasted_iota(jnp.int32, (groups, chans), 0)
    chan = lax.broadcasted_iota(jnp.int32, (groups, chans), 1)
    member = jnp.where(chan // (chans // groups) == group, 1.0, 0.0).astype(f32)
    mean_chan = exact(mean[...], member, ROWS_COLS)
    rstd_chan = exact(rstd[...], member, ROWS_COLS)
    scale_tab = exact(lat, ws[...], COLS_COLS) + bs[...]
    shift_tab = exact(lat, wt[...], COLS_COLS) + bt[...]
    tab_out[...] = scale_tab
    cells = cell_matrix(height, width, lat.shape[1])
    scale_map = exact(cells, scale_tab, ROWS_COLS)
    shift_map = exact(cells, shift_tab, ROWS_COLS)
    gain_out[...] = scale_map * (gamma[...] * rstd_chan)
    for frame in range(frames):
        at = pl.ds(frame * pixels, pixels)
        normed = (feats[at, :].astype(f32) - mean_chan) * rstd_chan
        modulated = (normed * gamma[...] + beta[...]) * scale_map + shift_map
        squashed = jax.nn.sigmoid(modulated)
        normed_out[at, :] = normed
        slope[at, :] = squashed * (1.0 + modulated * (1.0 - squashed))
        act_t[:, at] = (modulated * squashed).T.astype(bf16)


def column_shifts(value, width):
    column = lax.broadcasted_iota(jnp.int32, value.shape, 0) % width
    rows = value.shape[0]
    return (
        jnp.where(column == width - 1, 0.0, pltpu.roll(value, rows - 1, 0)),
        value,
        jnp.where(column == 0, 0.0, pltpu.roll(value, 1, 0)),
    )


def clear_borders(padded, width):
    lead = padded.shape[:-2]
    length, lanes = padded.shape[-2:]
    edge = jnp.zeros(lead + (width, lanes), padded.dtype)
    every = (slice(None),) * len(lead)
    padded[every + (slice(0, width),)] = edge
    padded[every + (slice(length - width, length),)] = edge


def input_grad_body(frames, height, width, grads, beyond, weights, slope, normed, gain, tab, latent,
                    ws, wt, gamma, beta, feats_grad, small, lat_own, lat_far, shifted, total):
    pixels = height * width
    chans = gain.shape[1]
    device = lax.axis_index("ctx")
    clear_borders(shifted, width)
    for half, source in enumerate((grads, beyond)):
        for col, value in enumerate(column_shifts(source[...].astype(f32), width)):
            for frame in range(frames):
                shifted[col, half * frames + frame, width:width + pixels] = (
                    value[frame * pixels:(frame + 1) * pixels].astype(bf16))

    def window(frame, row, col):
        start = (TAPS - 1 - row) * width
        return shifted[col, frame, start:start + pixels]

    def filters(step):
        return jnp.concatenate(
            [weights[(step * TAPS * TAPS + k) * chans:(step * TAPS * TAPS + k + 1) * chans, :]
             for k in range(TAPS * TAPS)], axis=1)

    def windows(frame_list):
        return jnp.concatenate(
            [jnp.concatenate([window(frame, k // TAPS, k % TAPS) for k in range(TAPS * TAPS)], axis=1)
             for frame in frame_list], axis=0)

    for step in range(TAPS):
        term = dot(windows([t + TAPS - 1 - step for t in range(frames)]), filters(step), ROWS_ROWS)
        total[...] = term if step == 0 else total[...] + term

    @pl.when(device == 0)
    def _():
        for step in range(TAPS - 1):
            for frame in range(TAPS - 1 - step):
                total[0:pixels] += dot(windows([frame]), filters(step), ROWS_ROWS)

    pooled_shift = jnp.zeros((pixels, chans), f32)
    pooled_norm = jnp.zeros((pixels, chans), f32)
    for frame in range(frames):
        at = pl.ds(frame * pixels, pixels)
        pre = total[at, :] * slope[at, :]
        feats_grad[at, :] = (pre * gain[...]).astype(bf16)
        pooled_shift += pre
        pooled_norm += pre * normed[at, :]
    lat = latent[0, device * frames // CELL]
    depth, length = lat.shape
    cells = cell_matrix(height, width, length)
    shift_pool = exact(cells, pooled_shift, COLS_COLS)
    norm_pool = exact(cells, pooled_norm, COLS_COLS)
    scale_pool = norm_pool * gamma[...] + shift_pool * beta[...]
    small[0:depth] = exact(lat, scale_pool, ROWS_COLS)
    small[depth:2 * depth] = exact(lat, shift_pool, ROWS_COLS)
    for row, field in enumerate((norm_pool * tab[...], shift_pool * tab[...], scale_pool, shift_pool)):
        small[2 * depth + row:2 * depth + row + 1] = jnp.sum(field, axis=0, keepdims=True)
    latent_sum = exact(scale_pool, ws[...], ROWS_ROWS) + exact(shift_pool, wt[...], ROWS_ROWS)
    first, second = latent_sum[:length // 2], latent_sum[length // 2:]
    even = device % 2 == 0
    lat_own[...] = jnp.where(even, first, second)
    lat_far[...] = jnp.where(even, second, first)


def filter_grad_body(frames, height, width, videos, near, piece, *refs):
    acts, refs = refs[:videos], refs[videos:]
    grads, refs = refs[:videos], refs[videos:]
    beyond, refs = refs[:videos], refs[videos:]
    smalls, refs = refs[:videos], refs[videos:]
    lat_far, own, refs = refs[0], refs[1], refs[2:]
    sends, small_out, packs, blocks = refs
    pixels = height * width
    chans = acts[0].shape[0]
    lanes = grads[0].shape[1]
    cols = lanes // videos
    device = lax.axis_index("ctx")
    here = lax.axis_index("vid")
    per = min(videos, TAPS)
    banks = -(-TAPS // per)
    lane = lax.broadcasted_iota(jnp.int32, (1, lanes), 1)
    small = functools.reduce(lambda a, b: a + b, [ref[...] for ref in smalls])
    small_out[...] = jnp.zeros_like(small_out)
    for k in range(chans // lanes):
        small_out[k * small.shape[0]:(k + 1) * small.shape[0]] = small[:, k * lanes:(k + 1) * lanes]

    clear_borders(packs, width)
    for video in range(videos):
        for half, source in enumerate((grads[video], beyond[video])):
            value = pltpu.roll(source[...].astype(f32), lax.rem(lanes - here * cols, lanes), 1)
            moved = column_shifts(value, width)
            for bank in range(banks):
                packed = moved[bank * per]
                for k in range(1, min(per, TAPS - bank * per)):
                    packed = jnp.where(lane >= k * cols, pltpu.roll(moved[bank * per + k], k * cols, 1), packed)
                packed = packed.astype(bf16)
                for frame in range(frames):
                    packs[video, bank, half * frames + frame, width:width + pixels] = (
                        packed[frame * pixels:(frame + 1) * pixels])

    def window(video, frame, row, bank):
        start = (TAPS - 1 - row) * width
        return packs[video, bank, frame, start:start + pixels]

    slots = [(row, bank) for row in range(TAPS) for bank in range(banks)]

    def windows(video, frame):
        return jnp.concatenate([window(video, frame, row, bank) for row, bank in slots], axis=1)

    far, rows = blocks.shape[0], TAPS**3 * chans // (blocks.shape[0] * near)
    every = jnp.concatenate([ref[...] for ref in acts], axis=1)
    firsts = jnp.concatenate([ref[:, 0:pixels] for ref in acts], axis=1)
    if piece * videos > rows:
        blocks[:, :, piece - TILE:] = jnp.zeros((far, near, TILE, lanes), f32)

    for step in range(TAPS):
        right = jnp.concatenate(
            [windows(video, t + TAPS - 1 - step) for video in range(videos) for t in range(frames)], axis=0)
        result = dot(every, right, ROWS_COLS)

        def put(result, add, step=step):
            for place, (row, bank) in enumerate(slots):
                tile = result[:, place * lanes:(place + 1) * lanes]
                for k in range(min(per, TAPS - bank * per)):
                    tap = (step * TAPS + row) * TAPS + bank * per + k
                    done = 0
                    while done < chans:
                        index = tap * chans + done
                        owner, inside = index // rows, index % rows
                        part, at = inside // piece, inside % piece
                        length = min(chans - done, rows - inside, piece - at)
                        turn = (part - k) * cols % lanes
                        value = tile[done:done + length]
                        if turn:
                            value = pltpu.roll(value, turn, 1)
                        dest = blocks.at[owner // near, owner % near, at:at + length, part * cols:(part + 1) * cols]
                        value = value[:, part * cols:(part + 1) * cols]
                        dest[...] = dest[...] + value if add else value
                        done += length

        put(result, False)
        if step < TAPS - 1:
            @pl.when(device == 0)
            def _(step=step, put=put):
                right = jnp.concatenate([windows(video, 0) for video in range(videos)], axis=0)
                extra = dot(firsts, right, ROWS_COLS)
                for frame in range(1, TAPS - 1 - step):
                    right = jnp.concatenate([windows(video, frame) for video in range(videos)], axis=0)
                    extra = extra + dot(firsts, right, ROWS_COLS)
                put(extra, True)

    me = device % near
    own[...] = blocks[:, me]
    top, rest = halves(small_out[...])
    count = top.shape[0]
    lat_top, lat_rest = halves(lat_far[...])
    cells, depth = lat_top.shape
    for turn in range(1, near):
        send = sends.at[paired(me, turn, near)]
        for k in range(far):
            send[k * piece:(k + 1) * piece] = blocks[k, paired(me, turn, near)].astype(bf16)
        at = far * piece
        send[at:at + count] = top
        send[at + count:at + 2 * count] = rest
        send[at + 2 * count:at + 2 * count + cells, :depth] = lat_top
        send[at + 2 * count + cells:at + 2 * count + 2 * cells, :depth] = lat_rest


def plane_sum_body(near, far, *refs):
    own, got_all, small, lat_own, kept, sends, small_out, latent_grad, total = refs
    place = lax.axis_index("ctx") % near
    got = [got_all.at[paired(place, turn, near)] for turn in range(1, near)]
    piece = own.shape[1]
    count = small.shape[0]
    cells, depth = lat_own.shape
    for k in range(far):
        total[k] = functools.reduce(lambda a, b: a + b[k * piece:(k + 1) * piece].astype(f32), got, own[k])
    at = far * piece

    def joined(ref, start, length):
        return ref[start:start + length].astype(f32) + ref[start + length:start + 2 * length].astype(f32)

    summed = functools.reduce(lambda a, b: a + joined(b, at, count), got, small[...])
    small_out[...] = summed
    latent_grad[...] = lat_own[...] + joined(got[0], at + 2 * count, cells)[:, :depth]
    me = lax.axis_index("ctx") // near
    kept[...] = total[me]
    top, rest = halves(summed)
    for turn in range(1, far):
        send = sends.at[paired(me, turn, far)]
        send[0:piece] = total[paired(me, turn, far)].astype(bf16)
        send[piece:piece + count] = top
        send[piece + count:piece + 2 * count] = rest


def line_sum_body(far, *refs):
    kept, got_all, small, filter_grad, mod_grads, vector_grads = refs
    place = lax.axis_index("ctx") // (lax.axis_size("ctx") // far)
    got = [got_all.at[paired(place, turn, far)] for turn in range(1, far)]
    piece, lanes = kept.shape
    count = small.shape[0]
    total = functools.reduce(lambda a, b: a + b[0:piece].astype(f32), got, kept[...])
    cols, rows = filter_grad.shape
    turned = total.T
    for part in range(lanes // cols):
        first, last = part * piece, min(rows, (part + 1) * piece)
        if first < last:
            filter_grad[:, first:last] = turned[part * cols:(part + 1) * cols, :last - first]
    summed = functools.reduce(
        lambda a, b: a + b[piece:piece + count].astype(f32) + b[piece + count:piece + 2 * count].astype(f32),
        got, small[...])
    split, length = mod_grads.shape[0], mod_grads.shape[0] + vector_grads.shape[0]
    for k in range(mod_grads.shape[1] // lanes):
        mod_grads[:, k * lanes:(k + 1) * lanes] = summed[k * length:k * length + split]
        vector_grads[:, k * lanes:(k + 1) * lanes] = summed[k * length + split:(k + 1) * length]


def local(features, grad_out, mean, rstd, latent, gamma, beta, ws, bs, wt, bt, kernel):
    _, frames, height, width, chans = features.shape
    outs = grad_out.shape[-1]
    depth, length = latent.shape[2:]
    count, videos = lax.axis_size("ctx"), lax.axis_size("vid")
    near = math.gcd(count, NEAR)
    far = count // near
    pixels = height * width
    size = frames * pixels
    rows, cols = TAPS**3 * chans // count, outs // videos
    piece = -(-rows // (TILE * videos)) * TILE
    gamma, beta, bs, bt = (value.reshape(1, chans) for value in (gamma, beta, bs, bt))
    feats = features.reshape(size, chans)
    grads = grad_out.reshape(size, outs)

    def others(value):
        return [value] + [
            lax.ppermute(value, "vid", [(s, (s + turn) % videos) for s in range(videos)])
            for turn in range(1, videos)]

    def near_got(values):
        groups = [[line * near + k for k in range(near)] for line in range(far)]
        return lax.all_to_all(values, "ctx", 0, 0, axis_index_groups=groups)

    def far_got(values):
        groups = [[k * near + place for k in range(far)] for place in range(near)]
        return lax.all_to_all(values, "ctx", 0, 0, axis_index_groups=groups)

    beyond = lax.ppermute(grads, "ctx", [(s, s - 1) for s in range(1, count)])
    act_t, slope, normed, gain, tab = call(
        functools.partial(modulate_body, frames, height, width),
        (shaped((chans, size), bf16), shaped((size, chans)), shaped((size, chans)), shaped((pixels, chans)),
         shaped((length, chans))),
        name="modulate",
        far_args=tuple(range(10)),
    )(feats, mean, rstd, latent, gamma, beta, ws, bs, wt, bt)
    grads_all, acts_all, beyond_all = others(grads), others(act_t), others(beyond)
    small_rows = 2 * depth + 4
    cells = length // 2
    feats_grad, small, lat_own, lat_far = call(
        functools.partial(input_grad_body, frames, height, width),
        (shaped((size, chans), bf16), shaped((small_rows, chans)), shaped((cells, depth)), shaped((cells, depth))),
        (pltpu.VMEM((TAPS, 2 * frames, (height + 2) * width, outs), bf16), pltpu.VMEM((size, chans), f32)),
        name="input_grad",
        far_args=(0, 2, 7, 8, 9, 10, 11),
    )(grads, beyond, kernel, slope, normed, gain, tab, latent, ws, wt, gamma, beta)
    banks = -(-TAPS // min(videos, TAPS))
    count_small = -(-small_rows * (chans // outs) // TILE) * TILE
    extra = 2 * count_small + -(-2 * cells // TILE) * TILE
    own, sends, small = call(
        functools.partial(filter_grad_body, frames, height, width, videos, near, piece),
        [shaped((far, piece, outs))] + [shaped((near, far * piece + extra, outs), bf16)]
        + [shaped((count_small, outs))],
        (pltpu.VMEM((videos, banks, 2 * frames, (height + 2) * width, outs), bf16),
         pltpu.VMEM((far, near, piece, outs), f32)),
        name="filter_grad",
        far_args=(videos,),
    )(*acts_all, *grads_all, *beyond_all, *others(small), lat_far)
    kept, sends, small, latent_grad = call(
        functools.partial(plane_sum_body, near, far),
        [shaped((piece, outs))] + [shaped((far, piece + 2 * count_small, outs), bf16)]
        + [shaped((count_small, outs)), shaped((cells, depth))],
        (pltpu.VMEM((far, piece, outs), f32),),
        name="plane_sum",
    )(own, near_got(sends), small, lat_own)
    filter_grad, mod_grads, vector_grads = call(
        functools.partial(line_sum_body, far),
        (shaped((cols, rows)), shaped((2 * depth, chans)), shaped((4, chans))),
        name="line_sum",
    )(kept, far_got(sends), small)
    return (
        feats_grad.reshape(features.shape),
        filter_grad.T,
        mod_grads.reshape(2, depth, chans),
        vector_grads,
        latent_grad.T[None, None],
    )


def solution(mesh):
    split = P("vid", "ctx", None, None, None)
    return jax.shard_map(
        local,
        mesh=mesh,
        in_specs=(split, split, P("vid", None), P("vid", None), P("vid", None, None, None)) + (P(),) * 7,
        out_specs=(split, P("ctx", "vid"), P(), P(), P("vid", "ctx", None, None)),
        check_vma=False,
    )
```

```python
import functools
import math

import jax
import jax.numpy as jnp
from jax import lax
from jax.experimental import pallas as pl
from jax.experimental.pallas import tpu as pltpu
from jax.sharding import PartitionSpec as P

NEAR = 4
CELL = 4
TAPS = 3
TILE = 16

f32 = jnp.float32
bf16 = jnp.bfloat16
dot = functools.partial(lax.dot_general, preferred_element_type=f32)
exact = functools.partial(dot, precision=lax.Precision.HIGHEST)
ROWS_COLS = (((1,), (0,)), ((), ()))
ROWS_ROWS = (((1,), (1,)), ((), ()))
COLS_COLS = (((0,), (0,)), ((), ()))


def call(body, outs, scratch=(), name=None, far_args=()):
    def run(*args):
        args = [pltpu.with_memory_space_constraint(arg, pltpu.HBM) if k in far_args else arg
                for k, arg in enumerate(args)]

        def full(*refs):
            refs = list(refs)
            sems = refs.pop()
            buffers = [refs.pop() for _ in far_args][::-1]
            moves = [pltpu.make_async_copy(refs[at], buffer, sems.at[k])
                     for k, (at, buffer) in enumerate(zip(far_args, buffers))]
            for move in moves:
                move.start()
            for at, buffer in zip(far_args, buffers):
                refs[at] = buffer
            for move in moves:
                move.wait()
            body(*refs)

        return pl.pallas_call(
            full if far_args else body,
            out_shape=outs,
            in_specs=[pl.BlockSpec(memory_space=pltpu.HBM if k in far_args else pltpu.VMEM) for k in range(len(args))],
            scratch_shapes=list(scratch) + [pltpu.VMEM(args[k].shape, args[k].dtype) for k in far_args]
            + ([pltpu.SemaphoreType.DMA((len(far_args),))] if far_args else []),
            name=name,
            compiler_params=pltpu.CompilerParams(vmem_limit_bytes=50 * 2**20),
        )(*args)

    return run


def halves(value):
    top = value.astype(bf16)
    return top, (value - top.astype(f32)).astype(bf16)


def shaped(shape, kind=f32):
    return jax.ShapeDtypeStruct(shape, kind)


def cell_matrix(height, width, cells):
    pixel = lax.broadcasted_iota(jnp.int32, (height * width, cells), 0)
    cell = lax.broadcasted_iota(jnp.int32, (height * width, cells), 1)
    place = (pixel // width) // CELL * (width // CELL) + pixel % width // CELL
    return jnp.where(place == cell, 1.0, 0.0).astype(f32)


def modulate_body(frames, height, width, feats, mean, rstd, latent, gamma, beta, ws, bs, wt, bt,
                  act_t, slope, normed_out, gain_out, tab_out):
    chans = feats.shape[1]
    groups = mean.shape[1]
    pixels = height * width
    lat = latent[0, lax.axis_index("ctx") * frames // CELL]
    group = lax.broadcasted_iota(jnp.int32, (groups, chans), 0)
    chan = lax.broadcasted_iota(jnp.int32, (groups, chans), 1)
    member = jnp.where(chan // (chans // groups) == group, 1.0, 0.0).astype(f32)
    mean_chan = exact(mean[...], member, ROWS_COLS)
    rstd_chan = exact(rstd[...], member, ROWS_COLS)
    scale_tab = exact(lat, ws[...], COLS_COLS) + bs[...]
    shift_tab = exact(lat, wt[...], COLS_COLS) + bt[...]
    tab_out[...] = scale_tab
    cells = cell_matrix(height, width, lat.shape[1])
    scale_map = exact(cells, scale_tab, ROWS_COLS)
    shift_map = exact(cells, shift_tab, ROWS_COLS)
    gain_out[...] = scale_map * (gamma[...] * rstd_chan)
    for frame in range(frames):
        at = pl.ds(frame * pixels, pixels)
        normed = (feats[at, :].astype(f32) - mean_chan) * rstd_chan
        modulated = (normed * gamma[...] + beta[...]) * scale_map + shift_map
        squashed = jax.nn.sigmoid(modulated)
        normed_out[at, :] = normed
        slope[at, :] = squashed * (1.0 + modulated * (1.0 - squashed))
        act_t[:, at] = (modulated * squashed).T.astype(bf16)


def column_shifts(value, width):
    column = lax.broadcasted_iota(jnp.int32, value.shape, 0) % width
    rows = value.shape[0]
    return (
        jnp.where(column == width - 1, 0.0, pltpu.roll(value, rows - 1, 0)),
        value,
        jnp.where(column == 0, 0.0, pltpu.roll(value, 1, 0)),
    )


def clear_borders(padded, width):
    lead = padded.shape[:-2]
    length, lanes = padded.shape[-2:]
    edge = jnp.zeros(lead + (width, lanes), padded.dtype)
    every = (slice(None),) * len(lead)
    padded[every + (slice(0, width),)] = edge
    padded[every + (slice(length - width, length),)] = edge


def input_grad_body(frames, height, width, grads, beyond, weights, slope, normed, gain, tab, latent,
                    ws, wt, gamma, beta, feats_grad, small, lat_own, lat_far, shifted, total):
    pixels = height * width
    chans = gain.shape[1]
    device = lax.axis_index("ctx")
    clear_borders(shifted, width)
    for half, source in enumerate((grads, beyond)):
        for col, value in enumerate(column_shifts(source[...].astype(f32), width)):
            for frame in range(frames):
                shifted[col, half * frames + frame, width:width + pixels] = (
                    value[frame * pixels:(frame + 1) * pixels].astype(bf16))

    def window(frame, row, col):
        start = (TAPS - 1 - row) * width
        return shifted[col, frame, start:start + pixels]

    def filters(step):
        return jnp.concatenate(
            [weights[(step * TAPS * TAPS + k) * chans:(step * TAPS * TAPS + k + 1) * chans, :]
             for k in range(TAPS * TAPS)], axis=1)

    def windows(frame_list):
        return jnp.concatenate(
            [jnp.concatenate([window(frame, k // TAPS, k % TAPS) for k in range(TAPS * TAPS)], axis=1)
             for frame in frame_list], axis=0)

    for step in range(TAPS):
        term = dot(windows([t + TAPS - 1 - step for t in range(frames)]), filters(step), ROWS_ROWS)
        total[...] = term if step == 0 else total[...] + term

    @pl.when(device == 0)
    def _():
        for step in range(TAPS - 1):
            for frame in range(TAPS - 1 - step):
                total[0:pixels] += dot(windows([frame]), filters(step), ROWS_ROWS)

    pooled_shift = jnp.zeros((pixels, chans), f32)
    pooled_norm = jnp.zeros((pixels, chans), f32)
    for frame in range(frames):
        at = pl.ds(frame * pixels, pixels)
        pre = total[at, :] * slope[at, :]
        feats_grad[at, :] = (pre * gain[...]).astype(bf16)
        pooled_shift += pre
        pooled_norm += pre * normed[at, :]
    lat = latent[0, device * frames // CELL]
    depth, length = lat.shape
    cells = cell_matrix(height, width, length)
    shift_pool = exact(cells, pooled_shift, COLS_COLS)
    norm_pool = exact(cells, pooled_norm, COLS_COLS)
    scale_pool = norm_pool * gamma[...] + shift_pool * beta[...]
    parts = [exact(lat, scale_pool, ROWS_COLS), exact(lat, shift_pool, ROWS_COLS)]
    for field in (norm_pool * tab[...], shift_pool * tab[...], scale_pool, shift_pool):
        parts.append(jnp.sum(field, axis=0, keepdims=True))
    lanes = small.shape[1]
    small[small.shape[0] - TILE:] = jnp.zeros((TILE, lanes), f32)
    at = 0
    for k in range(chans // lanes):
        for part in parts:
            small[at:at + part.shape[0]] = part[:, k * lanes:(k + 1) * lanes]
            at += part.shape[0]
    latent_sum = exact(scale_pool, ws[...], ROWS_ROWS) + exact(shift_pool, wt[...], ROWS_ROWS)
    first, second = latent_sum[:length // 2], latent_sum[length // 2:]
    even = device % 2 == 0
    lat_own[...] = jnp.where(even, first, second)
    lat_far[...] = jnp.where(even, second, first)


def filter_grad_body(frames, height, width, videos, near, piece, *refs):
    acts, refs = refs[:videos], refs[videos:]
    grads, refs = refs[:videos], refs[videos:]
    beyond, refs = refs[:videos], refs[videos:]
    own_far, own_line, line_send, *sends, packs, blocks = refs
    pixels = height * width
    chans = acts[0].shape[0]
    lanes = grads[0].shape[1]
    cols = lanes // videos
    device = lax.axis_index("ctx")
    here = lax.axis_index("vid")
    per = min(videos, TAPS)
    banks = -(-TAPS // per)
    lane = lax.broadcasted_iota(jnp.int32, (1, lanes), 1)
    clear_borders(packs, width)
    for video in range(videos):
        for half, source in enumerate((grads[video], beyond[video])):
            value = pltpu.roll(source[...].astype(f32), lax.rem(lanes - here * cols, lanes), 1)
            moved = column_shifts(value, width)
            for bank in range(banks):
                packed = moved[bank * per]
                for k in range(1, min(per, TAPS - bank * per)):
                    packed = jnp.where(lane >= k * cols, pltpu.roll(moved[bank * per + k], k * cols, 1), packed)
                packed = packed.astype(bf16)
                for frame in range(frames):
                    packs[video, bank, half * frames + frame, width:width + pixels] = (
                        packed[frame * pixels:(frame + 1) * pixels])

    def window(video, frame, row, bank):
        start = (TAPS - 1 - row) * width
        return packs[video, bank, frame, start:start + pixels]

    slots = [(row, bank) for row in range(TAPS) for bank in range(banks)]

    def windows(video, frame):
        return jnp.concatenate([window(video, frame, row, bank) for row, bank in slots], axis=1)

    far, rows = blocks.shape[0], TAPS**3 * chans // (blocks.shape[0] * near)
    every = jnp.concatenate([ref[...] for ref in acts], axis=1)
    firsts = jnp.concatenate([ref[:, 0:pixels] for ref in acts], axis=1)
    if piece * videos > rows:
        blocks[:, :, piece - TILE:] = jnp.zeros((far, near, TILE, lanes), f32)

    for step in range(TAPS):
        right = jnp.concatenate(
            [windows(video, t + TAPS - 1 - step) for video in range(videos) for t in range(frames)], axis=0)
        result = dot(every, right, ROWS_COLS)

        def put(result, add, step=step):
            for place, (row, bank) in enumerate(slots):
                tile = result[:, place * lanes:(place + 1) * lanes]
                for k in range(min(per, TAPS - bank * per)):
                    tap = (step * TAPS + row) * TAPS + bank * per + k
                    done = 0
                    while done < chans:
                        index = tap * chans + done
                        owner, inside = index // rows, index % rows
                        part, at = inside // piece, inside % piece
                        length = min(chans - done, rows - inside, piece - at)
                        turn = (part - k) * cols % lanes
                        value = tile[done:done + length]
                        if turn:
                            value = pltpu.roll(value, turn, 1)
                        dest = blocks.at[owner // near, owner % near, at:at + length, part * cols:(part + 1) * cols]
                        value = value[:, part * cols:(part + 1) * cols]
                        dest[...] = dest[...] + value if add else value
                        done += length

        put(result, False)
        if step < TAPS - 1:
            @pl.when(device == 0)
            def _(step=step, put=put):
                right = jnp.concatenate([windows(video, 0) for video in range(videos)], axis=0)
                extra = dot(firsts, right, ROWS_COLS)
                for frame in range(1, TAPS - 1 - step):
                    right = jnp.concatenate([windows(video, frame) for video in range(videos)], axis=0)
                    extra = extra + dot(firsts, right, ROWS_COLS)
                put(extra, True)

    line, place = device // near, device % near
    own_line[...] = blocks[line]
    for k in range(near):
        line_send[k * piece:(k + 1) * piece] = blocks[line ^ 1, k].astype(bf16)
    for k in range(far - 2):
        own_far[k] = blocks[line ^ (k + 2), place]
        for turn, send in enumerate(sends, 1):
            send[k * piece:(k + 1) * piece] = blocks[line ^ (k + 2), place ^ turn].astype(bf16)


def first_sum_body(near, far, videos, *refs):
    own_far, own_line, line_got, refs = refs[0], refs[1], refs[2], refs[3:]
    plane_got, refs = refs[:near - 1], refs[near - 1:]
    smalls, lat_far, refs = refs[:videos], refs[videos], refs[videos + 1:]
    kept, small_out, refs = refs[0], refs[1], refs[2:]
    plane_sends, line_sends, total = refs[:near - 1], refs[near - 1:-1], refs[-1]
    piece = own_line.shape[1]
    count = smalls[0].shape[0]
    place = lax.axis_index("ctx") % near
    for k, send in enumerate(line_sends):
        send[...] = functools.reduce(
            lambda a, b: a + b[k * piece:(k + 1) * piece].astype(f32), plane_got, own_far[k]).astype(bf16)
    for k in range(near):
        total[k] = own_line[k] + line_got[k * piece:(k + 1) * piece].astype(f32)
    kept[...] = total[place]
    summed = functools.reduce(lambda a, b: a + b, [ref[...] for ref in smalls])
    small_out[...] = summed
    top, rest = halves(summed)
    lat_top, lat_rest = halves(lat_far[...])
    cells, depth = lat_top.shape
    at = piece + 2 * count
    for turn, send in enumerate(plane_sends, 1):
        send[0:piece] = total[place ^ turn].astype(bf16)
        send[piece:piece + count] = top
        send[piece + count:at] = rest
        send[at:at + cells, :depth] = lat_top
        send[at + cells:at + 2 * cells, :depth] = lat_rest


def last_sum_body(near, far, *refs):
    kept, small, lat_own, refs = refs[0], refs[1], refs[2], refs[3:]
    plane_got, line_got, refs = refs[:near - 1], refs[near - 1:near + far - 3], refs[near + far - 3:]
    filter_grad, mod_grads, vector_grads, latent_grad = refs
    piece, lanes = kept.shape
    count = small.shape[0]

    def joined(ref, start, length):
        return ref[start:start + length].astype(f32) + ref[start + length:start + 2 * length].astype(f32)

    total = functools.reduce(lambda a, b: a + b[0:piece].astype(f32), plane_got + line_got, kept[...])
    cols, rows = filter_grad.shape
    turned = total.T
    for part in range(lanes // cols):
        first, last = part * piece, min(rows, (part + 1) * piece)
        if first < last:
            filter_grad[:, first:last] = turned[part * cols:(part + 1) * cols, :last - first]
    summed = functools.reduce(lambda a, b: a + joined(b, piece, count), plane_got, small[...])
    split, length = mod_grads.shape[0], mod_grads.shape[0] + vector_grads.shape[0]
    for k in range(mod_grads.shape[1] // lanes):
        mod_grads[:, k * lanes:(k + 1) * lanes] = summed[k * length:k * length + split]
        vector_grads[:, k * lanes:(k + 1) * lanes] = summed[k * length + split:(k + 1) * length]
    cells, depth = lat_own.shape
    latent_grad[...] = lat_own[...] + joined(plane_got[0], piece + 2 * count, cells)[:, :depth]


def local(features, grad_out, mean, rstd, latent, gamma, beta, ws, bs, wt, bt, kernel):
    _, frames, height, width, chans = features.shape
    outs = grad_out.shape[-1]
    depth, length = latent.shape[2:]
    count, videos = lax.axis_size("ctx"), lax.axis_size("vid")
    near = math.gcd(count, NEAR)
    far = count // near
    pixels = height * width
    size = frames * pixels
    rows, cols = TAPS**3 * chans // count, outs // videos
    piece = -(-rows // (TILE * videos)) * TILE
    gamma, beta, bs, bt = (value.reshape(1, chans) for value in (gamma, beta, bs, bt))
    feats = features.reshape(size, chans)
    grads = grad_out.reshape(size, outs)

    def along_ctx(value, target):
        return lax.ppermute(value, "ctx", [(s, target(s)) for s in range(count)])

    def others(value):
        return [value] + [
            lax.ppermute(value, "vid", [(s, (s + turn) % videos) for s in range(videos)])
            for turn in range(1, videos)]

    def plane_got(values):
        return [along_ctx(value, lambda s: s ^ turn) for turn, value in enumerate(values, 1)]

    def line_got(values, first):
        return [along_ctx(value, lambda s: s ^ (turn * near)) for turn, value in enumerate(values, first)]

    beyond = lax.ppermute(grads, "ctx", [(s, s - 1) for s in range(1, count)])
    act_t, slope, normed, gain, tab = call(
        functools.partial(modulate_body, frames, height, width),
        (shaped((chans, size), bf16), shaped((size, chans)), shaped((size, chans)), shaped((pixels, chans)),
         shaped((length, chans))),
        name="modulate",
        far_args=tuple(range(10)),
    )(feats, mean, rstd, latent, gamma, beta, ws, bs, wt, bt)
    grads_all, acts_all, beyond_all = others(grads), others(act_t), others(beyond)
    cells = length // 2
    count_small = -(-(2 * depth + 4) * (chans // outs) // TILE) * TILE
    feats_grad, small, lat_own, lat_far = call(
        functools.partial(input_grad_body, frames, height, width),
        (shaped((size, chans), bf16), shaped((count_small, outs)), shaped((cells, depth)), shaped((cells, depth))),
        (pltpu.VMEM((TAPS, 2 * frames, (height + 2) * width, outs), bf16), pltpu.VMEM((size, chans), f32)),
        name="input_grad",
        far_args=(0, 2, 7, 8, 9, 10, 11),
    )(grads, beyond, kernel, slope, normed, gain, tab, latent, ws, wt, gamma, beta)
    small = functools.reduce(lambda a, b: a + b, line_got([small] * (far - 1), 1), small)
    banks = -(-TAPS // min(videos, TAPS))
    own_far, own_line, line_send, *plane_sends = call(
        functools.partial(filter_grad_body, frames, height, width, videos, near, piece),
        [shaped((far - 2, piece, outs)), shaped((near, piece, outs)), shaped((near * piece, outs), bf16)]
        + [shaped(((far - 2) * piece, outs), bf16)] * (near - 1),
        (pltpu.VMEM((videos, banks, 2 * frames, (height + 2) * width, outs), bf16),
         pltpu.VMEM((far, near, piece, outs), f32)),
        name="filter_grad",
        far_args=(videos,),
    )(*acts_all, *grads_all, *beyond_all)
    extra = 2 * count_small + -(-2 * cells // TILE) * TILE
    kept, small, *sends = call(
        functools.partial(first_sum_body, near, far, videos),
        [shaped((piece, outs)), shaped((count_small, outs))]
        + [shaped((piece + extra, outs), bf16)] * (near - 1) + [shaped((piece, outs), bf16)] * (far - 2),
        (pltpu.VMEM((near, piece, outs), f32),),
        name="first_sum",
    )(own_far, own_line, *line_got([line_send], 1), *plane_got(plane_sends), *others(small), lat_far)
    filter_grad, mod_grads, vector_grads, latent_grad = call(
        functools.partial(last_sum_body, near, far),
        (shaped((cols, rows)), shaped((2 * depth, chans)), shaped((4, chans)), shaped((cells, depth))),
        name="last_sum",
    )(kept, small, lat_own, *plane_got(sends[:near - 1]), *line_got(sends[near - 1:], 2))
    return (
        feats_grad.reshape(features.shape),
        filter_grad.T,
        mod_grads.reshape(2, depth, chans),
        vector_grads,
        latent_grad.T[None, None],
    )


def solution(mesh):
    split = P("vid", "ctx", None, None, None)
    return jax.shard_map(
        local,
        mesh=mesh,
        in_specs=(split, split, P("vid", None), P("vid", None), P("vid", None, None, None)) + (P(),) * 7,
        out_specs=(split, P("ctx", "vid"), P(), P(), P("vid", "ctx", None, None)),
        check_vma=False,
    )
```

```python
import functools
import math

import jax
import jax.numpy as jnp
from jax import lax
from jax.experimental import pallas as pl
from jax.experimental.pallas import tpu as pltpu
from jax.sharding import PartitionSpec as P

NEAR = 4
CELL = 4
TAPS = 3
TILE = 16

f32 = jnp.float32
bf16 = jnp.bfloat16
dot = functools.partial(lax.dot_general, preferred_element_type=f32)
exact = functools.partial(dot, precision=lax.Precision.HIGHEST)
ROWS_COLS = (((1,), (0,)), ((), ()))
ROWS_ROWS = (((1,), (1,)), ((), ()))
COLS_COLS = (((0,), (0,)), ((), ()))


def call(body, outs, scratch=(), name=None, far_args=(), keep=(), aliases=None):
    outs = list(outs)
    lost = [k for k in far_args if k not in keep]

    def run(*args):
        args = [pltpu.with_memory_space_constraint(arg, pltpu.HBM) if k in far_args else arg
                for k, arg in enumerate(args)]

        def full(*refs):
            refs = list(refs)
            sems = refs.pop()
            buffers = {k: refs.pop() for k in lost[::-1]}
            first = len(args) + len(outs)
            buffers.update({k: refs.pop(first) for k in keep})
            moves = [pltpu.make_async_copy(refs[k], buffers[k], sems.at[at]) for at, k in enumerate(far_args)]
            for move in moves:
                move.start()
            for k in far_args:
                refs[k] = buffers[k]
            for move in moves:
                move.wait()
            body(*refs)

        return pl.pallas_call(
            full if far_args else body,
            out_shape=outs + [shaped(args[k].shape, args[k].dtype) for k in keep],
            in_specs=[pl.BlockSpec(memory_space=pltpu.HBM if k in far_args else pltpu.VMEM) for k in range(len(args))],
            scratch_shapes=list(scratch) + [pltpu.VMEM(args[k].shape, args[k].dtype) for k in lost]
            + ([pltpu.SemaphoreType.DMA((len(far_args),))] if far_args else []),
            input_output_aliases=aliases or {},
            name=name,
            cost_estimate=pl.CostEstimate(flops=1000, bytes_accessed=1000, transcendentals=0),
            compiler_params=pltpu.CompilerParams(vmem_limit_bytes=50 * 2**20),
        )(*args)

    return run


def halves(value):
    top = value.astype(bf16)
    return top, (value - top.astype(f32)).astype(bf16)


def shaped(shape, kind=f32):
    return jax.ShapeDtypeStruct(shape, kind)


def cell_matrix(height, width, cells):
    pixel = lax.broadcasted_iota(jnp.int32, (height * width, cells), 0)
    cell = lax.broadcasted_iota(jnp.int32, (height * width, cells), 1)
    place = (pixel // width) // CELL * (width // CELL) + pixel % width // CELL
    return jnp.where(place == cell, 1.0, 0.0).astype(f32)


def modulate_body(frames, height, width, feats, mean, rstd, latent, gamma, beta, ws, bs, wt, bt, grads, weights,
                  act_t, slope, normed_out, gain_out, tab_out):
    chans = feats.shape[1]
    groups = mean.shape[1]
    pixels = height * width
    lat = latent[0, lax.axis_index("ctx") * frames // CELL]
    group = lax.broadcasted_iota(jnp.int32, (groups, chans), 0)
    chan = lax.broadcasted_iota(jnp.int32, (groups, chans), 1)
    member = jnp.where(chan // (chans // groups) == group, 1.0, 0.0).astype(f32)
    mean_chan = exact(mean[...], member, ROWS_COLS)
    rstd_chan = exact(rstd[...], member, ROWS_COLS)
    scale_tab = exact(lat, ws[...], COLS_COLS) + bs[...]
    shift_tab = exact(lat, wt[...], COLS_COLS) + bt[...]
    tab_out[...] = scale_tab
    cells = cell_matrix(height, width, lat.shape[1])
    scale_map = exact(cells, scale_tab, ROWS_COLS)
    shift_map = exact(cells, shift_tab, ROWS_COLS)
    gain_out[...] = scale_map * (gamma[...] * rstd_chan)
    for frame in range(frames):
        at = pl.ds(frame * pixels, pixels)
        normed = (feats[at, :].astype(f32) - mean_chan) * rstd_chan
        modulated = (normed * gamma[...] + beta[...]) * scale_map + shift_map
        squashed = jax.nn.sigmoid(modulated)
        normed_out[at, :] = normed
        slope[at, :] = squashed * (1.0 + modulated * (1.0 - squashed))
        act_t[:, at] = (modulated * squashed).T.astype(bf16)


def column_shifts(value, width):
    column = lax.broadcasted_iota(jnp.int32, value.shape, 0) % width
    rows = value.shape[0]
    return (
        jnp.where(column == width - 1, 0.0, pltpu.roll(value, rows - 1, 0)),
        value,
        jnp.where(column == 0, 0.0, pltpu.roll(value, 1, 0)),
    )


def clear_borders(padded, width):
    lead = padded.shape[:-2]
    length, lanes = padded.shape[-2:]
    edge = jnp.zeros(lead + (width, lanes), padded.dtype)
    every = (slice(None),) * len(lead)
    padded[every + (slice(0, width),)] = edge
    padded[every + (slice(length - width, length),)] = edge


def put_shifts(shifted, source, frames, pixels, width):
    clear_borders(shifted, width)
    for col, value in enumerate(column_shifts(source[...].astype(f32), width)):
        for frame in range(frames):
            shifted[col, frame, width:width + pixels] = value[frame * pixels:(frame + 1) * pixels].astype(bf16)


def taps_of(weights, step, chans):
    return jnp.concatenate(
        [weights[(step * TAPS * TAPS + k) * chans:(step * TAPS * TAPS + k + 1) * chans, :]
         for k in range(TAPS * TAPS)], axis=1)


def shifted_rows(shifted, frame_list, pixels, width):
    def window(frame, row, col):
        start = (TAPS - 1 - row) * width
        return shifted[col, frame, start:start + pixels]

    return jnp.concatenate(
        [jnp.concatenate([window(frame, k // TAPS, k % TAPS) for k in range(TAPS * TAPS)], axis=1)
         for frame in frame_list], axis=0)


def add_rows(total, term, first):
    if first == 0 and term.shape[0] == total.shape[0]:
        total[...] += term
    else:
        total[first:first + term.shape[0]] += term


def conv_own_body(frames, height, width, grads, weights, total, shifted):
    pixels = height * width
    chans = total.shape[1]
    put_shifts(shifted, grads, frames, pixels, width)
    total[...] = jnp.zeros_like(total)
    for step in range(TAPS):
        pairs = [(t, t + TAPS - 1 - step) for t in range(frames) if t + TAPS - 1 - step < frames]
        if pairs:
            rows = shifted_rows(shifted, [frame for _, frame in pairs], pixels, width)
            add_rows(total, dot(rows, taps_of(weights, step, chans), ROWS_ROWS), pairs[0][0] * pixels)

    @pl.when(lax.axis_index("ctx") == 0)
    def _():
        for step in range(TAPS - 1):
            for frame in range(TAPS - 1 - step):
                rows = shifted_rows(shifted, [frame], pixels, width)
                add_rows(total, dot(rows, taps_of(weights, step, chans), ROWS_ROWS), 0)


def input_grad_body(frames, height, width, beyond, weights, partial, slope, normed, gain, tab, latent,
                    ws, wt, gamma, beta, feats_grad, small, lat_own, lat_far, shifted, total):
    pixels = height * width
    chans = gain.shape[1]
    device = lax.axis_index("ctx")
    put_shifts(shifted, beyond, frames, pixels, width)
    total[...] = partial[...]
    for step in range(TAPS):
        pairs = [(t, t + TAPS - 1 - step - frames) for t in range(frames) if t + TAPS - 1 - step >= frames]
        if pairs:
            rows = shifted_rows(shifted, [frame for _, frame in pairs], pixels, width)
            add_rows(total, dot(rows, taps_of(weights, step, chans), ROWS_ROWS), pairs[0][0] * pixels)

    pooled_shift = jnp.zeros((pixels, chans), f32)
    pooled_norm = jnp.zeros((pixels, chans), f32)
    for frame in range(frames):
        at = pl.ds(frame * pixels, pixels)
        pre = total[at, :] * slope[at, :]
        feats_grad[at, :] = (pre * gain[...]).astype(bf16)
        pooled_shift += pre
        pooled_norm += pre * normed[at, :]
    lat = latent[0, device * frames // CELL]
    depth, length = lat.shape
    cells = cell_matrix(height, width, length)
    shift_pool = exact(cells, pooled_shift, COLS_COLS)
    norm_pool = exact(cells, pooled_norm, COLS_COLS)
    scale_pool = norm_pool * gamma[...] + shift_pool * beta[...]
    parts = [exact(lat, scale_pool, ROWS_COLS), exact(lat, shift_pool, ROWS_COLS)]
    for field in (norm_pool * tab[...], shift_pool * tab[...], scale_pool, shift_pool):
        parts.append(jnp.sum(field, axis=0, keepdims=True))
    lanes = small.shape[1]
    small[small.shape[0] - TILE:] = jnp.zeros((TILE, lanes), f32)
    at = 0
    for k in range(chans // lanes):
        for part in parts:
            small[at:at + part.shape[0]] = part[:, k * lanes:(k + 1) * lanes]
            at += part.shape[0]
    latent_sum = exact(scale_pool, ws[...], ROWS_ROWS) + exact(shift_pool, wt[...], ROWS_ROWS)
    first, second = latent_sum[:length // 2], latent_sum[length // 2:]
    even = device % 2 == 0
    lat_own[...] = jnp.where(even, first, second)
    lat_far[...] = jnp.where(even, second, first)


class FilterParts:
    def __init__(self, frames, height, width, videos, near, piece, packs, blocks, lanes, chans):
        self.frames, self.pixels, self.width, self.videos, self.near = frames, height * width, width, videos, near
        self.piece, self.packs, self.blocks, self.lanes, self.chans = piece, packs, blocks, lanes, chans
        self.cols = lanes // videos
        self.per = min(videos, TAPS)
        self.banks = -(-TAPS // self.per)
        self.slots = [(row, bank) for row in range(TAPS) for bank in range(self.banks)]
        self.rows = TAPS**3 * chans // (blocks.shape[0] * near)

    def pack(self, sources):
        clear_borders(self.packs, self.width)
        lane = lax.broadcasted_iota(jnp.int32, (1, self.lanes), 1)
        turn = lax.rem(self.lanes - lax.axis_index("vid") * self.cols, self.lanes)
        for video, source in enumerate(sources):
            moved = column_shifts(pltpu.roll(source[...].astype(f32), turn, 1), self.width)
            for bank in range(self.banks):
                packed = moved[bank * self.per]
                for k in range(1, min(self.per, TAPS - bank * self.per)):
                    other = pltpu.roll(moved[bank * self.per + k], k * self.cols, 1)
                    packed = jnp.where(lane >= k * self.cols, other, packed)
                packed = packed.astype(bf16)
                for frame in range(self.frames):
                    self.packs[video, bank, frame, self.width:self.width + self.pixels] = (
                        packed[frame * self.pixels:(frame + 1) * self.pixels])

    def product(self, acts, pairs):
        def window(video, frame, row, bank):
            start = (TAPS - 1 - row) * self.width
            return self.packs[video, bank, frame, start:start + self.pixels]

        left = jnp.concatenate(
            [act[:, t * self.pixels:(t + 1) * self.pixels] for act in acts for t, _ in pairs], axis=1)
        right = jnp.concatenate(
            [jnp.concatenate([window(video, frame, row, bank) for row, bank in self.slots], axis=1)
             for video in range(self.videos) for _, frame in pairs], axis=0)
        return dot(left, right, ROWS_COLS)

    def put(self, step, result, add):
        for place, (row, bank) in enumerate(self.slots):
            tile = None if result is None else result[:, place * self.lanes:(place + 1) * self.lanes]
            for k in range(min(self.per, TAPS - bank * self.per)):
                tap = (step * TAPS + row) * TAPS + bank * self.per + k
                done = 0
                while done < self.chans:
                    index = tap * self.chans + done
                    owner, inside = index // self.rows, index % self.rows
                    part, at = inside // self.piece, inside % self.piece
                    length = min(self.chans - done, self.rows - inside, self.piece - at)
                    low, high = part * self.cols, (part + 1) * self.cols
                    dest = self.blocks.at[owner // self.near, owner % self.near, at:at + length, low:high]
                    if tile is None:
                        dest[...] = jnp.zeros((length, self.cols), f32)
                    else:
                        value = tile[done:done + length]
                        turn = (part - k) * self.cols % self.lanes
                        if turn:
                            value = pltpu.roll(value, turn, 1)
                        value = value[:, low:high]
                        dest[...] = dest[...] + value if add else value
                    done += length


def filter_own_body(frames, height, width, videos, near, piece, *refs):
    acts, grads, (_, blocks, packs) = refs[:videos], refs[videos:2 * videos], refs[2 * videos:]
    parts = FilterParts(frames, height, width, videos, near, piece, packs, blocks, grads[0].shape[1], acts[0].shape[0])
    parts.pack(grads)
    far, lanes = blocks.shape[0], blocks.shape[3]
    first = lax.axis_index("ctx") == 0
    if piece * videos > parts.rows:
        blocks[:, :, piece - TILE:] = jnp.zeros((far, near, TILE, lanes), f32)
    for step in range(TAPS):
        pairs = [(t, t + TAPS - 1 - step) for t in range(frames) if t + TAPS - 1 - step < frames]
        parts.put(step, parts.product(acts, pairs) if pairs else None, False)
        if step < TAPS - 1:
            @pl.when(first)
            def _(step=step):
                extra = [parts.product(acts, [(0, frame)]) for frame in range(TAPS - 1 - step)]
                parts.put(step, functools.reduce(lambda a, b: a + b, extra), True)


def filter_grad_body(frames, height, width, videos, near, piece, *refs):
    acts, beyond, refs = refs[:videos], refs[videos:2 * videos], refs[2 * videos + 2:]
    blocks, own_far, own_line, line_send, *sends, packs = refs
    parts = FilterParts(frames, height, width, videos, near, piece, packs, blocks, beyond[0].shape[1], acts[0].shape[0])
    parts.pack(beyond)
    far = blocks.shape[0]
    for step in range(TAPS):
        pairs = [(t, t + TAPS - 1 - step - frames) for t in range(frames) if t + TAPS - 1 - step >= frames]
        if pairs:
            parts.put(step, parts.product(acts, pairs), True)
    device = lax.axis_index("ctx")
    line, place = device // near, device % near
    own_line[...] = blocks[line]
    for k in range(near):
        line_send[k * piece:(k + 1) * piece] = blocks[line ^ 1, k].astype(bf16)
    for k in range(far - 2):
        own_far[k] = blocks[line ^ (k + 2), place]
        for turn, send in enumerate(sends, 1):
            send[k * piece:(k + 1) * piece] = blocks[line ^ (k + 2), place ^ turn].astype(bf16)


def first_sum_body(near, far, videos, *refs):
    own_far, own_line, line_got, refs = refs[0], refs[1], refs[2], refs[3:]
    plane_got, refs = refs[:near - 1][::-1], refs[near - 1:]
    smalls, lat_far, refs = refs[:videos], refs[videos], refs[videos + 1:]
    kept, small_out, refs = refs[0], refs[1], refs[2:]
    plane_sends, line_sends, total = refs[:near - 1], refs[near - 1:-1], refs[-1]
    piece = own_line.shape[1]
    count = smalls[0].shape[0]
    place = lax.axis_index("ctx") % near
    for k, send in enumerate(line_sends):
        send[...] = functools.reduce(
            lambda a, b: a + b[k * piece:(k + 1) * piece].astype(f32), plane_got, own_far[k]).astype(bf16)
    for k in range(near):
        total[k] = own_line[k] + line_got[k * piece:(k + 1) * piece].astype(f32)
    kept[...] = total[place]
    summed = functools.reduce(lambda a, b: a + b, [ref[...] for ref in smalls])
    small_out[...] = summed
    top, rest = halves(summed)
    lat_top, lat_rest = halves(lat_far[...])
    cells, depth = lat_top.shape
    at = piece + 2 * count
    for turn, send in enumerate(plane_sends, 1):
        send[0:piece] = total[place ^ turn].astype(bf16)
        send[piece:piece + count] = top
        send[piece + count:at] = rest
        send[at:at + cells, :depth] = lat_top
        send[at + cells:at + 2 * cells, :depth] = lat_rest


def last_sum_body(near, far, *refs):
    kept, small, lat_own, refs = refs[0], refs[1], refs[2], refs[3:]
    line_got, plane_got, refs = refs[:far - 2], refs[far - 2:near + far - 3][::-1], refs[near + far - 3:]
    filter_grad, mod_grads, vector_grads, latent_grad = refs
    piece, lanes = kept.shape
    count = small.shape[0]

    def joined(ref, start, length):
        return ref[start:start + length].astype(f32) + ref[start + length:start + 2 * length].astype(f32)

    total = functools.reduce(lambda a, b: a + b[0:piece].astype(f32), plane_got + line_got, kept[...])
    cols, rows = filter_grad.shape
    turned = total.T
    for part in range(lanes // cols):
        first, last = part * piece, min(rows, (part + 1) * piece)
        if first < last:
            filter_grad[:, first:last] = turned[part * cols:(part + 1) * cols, :last - first]
    summed = functools.reduce(lambda a, b: a + joined(b, piece, count), plane_got, small[...])
    split, length = mod_grads.shape[0], mod_grads.shape[0] + vector_grads.shape[0]
    for k in range(mod_grads.shape[1] // lanes):
        mod_grads[:, k * lanes:(k + 1) * lanes] = summed[k * length:k * length + split]
        vector_grads[:, k * lanes:(k + 1) * lanes] = summed[k * length + split:(k + 1) * length]
    cells, depth = lat_own.shape
    latent_grad[...] = lat_own[...] + joined(plane_got[0], piece + 2 * count, cells)[:, :depth]


def local(features, grad_out, mean, rstd, latent, gamma, beta, ws, bs, wt, bt, kernel):
    _, frames, height, width, chans = features.shape
    outs = grad_out.shape[-1]
    depth, length = latent.shape[2:]
    count, videos = lax.axis_size("ctx"), lax.axis_size("vid")
    near = math.gcd(count, NEAR)
    far = count // near
    pixels = height * width
    size = frames * pixels
    rows, cols = TAPS**3 * chans // count, outs // videos
    piece = -(-rows // (TILE * videos)) * TILE
    gamma, beta, bs, bt = (value.reshape(1, chans) for value in (gamma, beta, bs, bt))
    feats = features.reshape(size, chans)
    grads = grad_out.reshape(size, outs)

    def along_ctx(value, target):
        return lax.ppermute(value, "ctx", [(s, target(s)) for s in range(count)])

    def others(value):
        return [value] + [
            lax.ppermute(value, "vid", [(s, (s + turn) % videos) for s in range(videos)])
            for turn in range(1, videos)]

    def plane_got(values):
        got = {turn: along_ctx(values[turn - 1], lambda s: s ^ turn) for turn in range(near - 1, 0, -1)}
        return [got[turn] for turn in range(1, near)]

    def line_got(values, first):
        turns = range(first, first + len(values))
        got = {turn: along_ctx(values[turn - first], lambda s: s ^ (turn * near)) for turn in reversed(turns)}
        return [got[turn] for turn in turns]

    beyond = lax.ppermute(grads, "ctx", [(s, s - 1) for s in range(1, count)])
    act_t, slope, normed, gain, tab, latent, gamma, beta, ws, wt, grads_near, kernel = call(
        functools.partial(modulate_body, frames, height, width),
        (shaped((chans, size), bf16), shaped((size, chans)), shaped((size, chans)), shaped((pixels, chans)),
         shaped((length, chans))),
        name="modulate",
        far_args=tuple(range(12)),
        keep=(3, 4, 5, 6, 8, 10, 11),
    )(feats, mean, rstd, latent, gamma, beta, ws, bs, wt, bt, grads, kernel)
    acts_all = others(act_t)
    grads_all = others(grads_near)
    shifts = pltpu.VMEM((TAPS, frames, (height + 2) * width, outs), bf16)
    partial, = call(
        functools.partial(conv_own_body, frames, height, width),
        (shaped((size, chans)),),
        (shifts,),
        name="conv_own",
    )(grads_near, kernel)
    banks = -(-TAPS // min(videos, TAPS))
    packs = pltpu.VMEM((videos, banks, frames, (height + 2) * width, outs), bf16)
    blocks, = call(
        functools.partial(filter_own_body, frames, height, width, videos, near, piece),
        (shaped((far, near, piece, outs)),),
        (packs,),
        name="filter_own",
    )(*acts_all, *grads_all, partial)
    beyond, blocks = lax.optimization_barrier((beyond, blocks))
    beyond_all = others(beyond)
    cells = length // 2
    count_small = -(-(2 * depth + 4) * (chans // outs) // TILE) * TILE
    feats_grad, small, lat_own, lat_far = call(
        functools.partial(input_grad_body, frames, height, width),
        (shaped((size, chans), bf16), shaped((count_small, outs)), shaped((cells, depth)), shaped((cells, depth))),
        (shifts, pltpu.VMEM((size, chans), f32)),
        name="input_grad",
    )(beyond, kernel, partial, slope, normed, gain, tab, latent, ws, wt, gamma, beta)
    step = 1
    while step < far:
        small = small + along_ctx(small, lambda s: s ^ (step * near))
        step *= 2
    blocks, own_far, own_line, line_send, *plane_sends = call(
        functools.partial(filter_grad_body, frames, height, width, videos, near, piece),
        [shaped(blocks.shape), shaped((far - 2, piece, outs)), shaped((near, piece, outs)),
         shaped((near * piece, outs), bf16)]
        + [shaped(((far - 2) * piece, outs), bf16)] * (near - 1),
        (packs,),
        name="filter_grad",
        aliases={2 * videos: 0},
    )(*acts_all, *beyond_all, blocks, lat_far)
    extra = 2 * count_small + -(-2 * cells // TILE) * TILE
    line_in = line_got([line_send], 1)
    plane_in = plane_got(plane_sends)
    kept, small, *sends = call(
        functools.partial(first_sum_body, near, far, videos),
        [shaped((piece, outs)), shaped((count_small, outs))]
        + [shaped((piece + extra, outs), bf16)] * (near - 1) + [shaped((piece, outs), bf16)] * (far - 2),
        (pltpu.VMEM((near, piece, outs), f32),),
        name="first_sum",
    )(own_far, own_line, *line_in, *plane_in[::-1], *others(small), lat_far)
    line_in = line_got(sends[near - 1:], 2)
    plane_in = plane_got(sends[:near - 1])
    filter_grad, mod_grads, vector_grads, latent_grad = call(
        functools.partial(last_sum_body, near, far),
        (shaped((cols, rows)), shaped((2 * depth, chans)), shaped((4, chans)), shaped((cells, depth))),
        name="last_sum",
    )(kept, small, lat_own, *line_in[::-1], *plane_in[::-1])
    return (
        feats_grad.reshape(features.shape),
        filter_grad.T,
        mod_grads.reshape(2, depth, chans),
        vector_grads,
        latent_grad.T[None, None],
    )


def solution(mesh):
    split = P("vid", "ctx", None, None, None)
    return jax.shard_map(
        local,
        mesh=mesh,
        in_specs=(split, split, P("vid", None), P("vid", None), P("vid", None, None, None)) + (P(),) * 7,
        out_specs=(split, P("ctx", "vid"), P(), P(), P("vid", "ctx", None, None)),
        check_vma=False,
    )
```

```python
import functools
import math

import jax
import jax.numpy as jnp
from jax import lax
from jax.experimental import pallas as pl
from jax.experimental.pallas import tpu as pltpu
from jax.sharding import PartitionSpec as P

NEAR = 4
CELL = 4
TAPS = 3
TILE = 16

f32 = jnp.float32
bf16 = jnp.bfloat16
dot = functools.partial(lax.dot_general, preferred_element_type=f32)
exact = functools.partial(dot, precision=lax.Precision.HIGHEST)
ROWS_COLS = (((1,), (0,)), ((), ()))
ROWS_ROWS = (((1,), (1,)), ((), ()))
COLS_COLS = (((0,), (0,)), ((), ()))


def call(body, outs, scratch=(), name=None, far_args=(), keep=(), aliases=None, work=1000):
    outs = list(outs)
    lost = [k for k in far_args if k not in keep]

    def run(*args):
        args = [pltpu.with_memory_space_constraint(arg, pltpu.HBM) if k in far_args else arg
                for k, arg in enumerate(args)]

        def full(*refs):
            refs = list(refs)
            sems = refs.pop()
            buffers = {k: refs.pop() for k in lost[::-1]}
            first = len(args) + len(outs)
            buffers.update({k: refs.pop(first) for k in keep})
            moves = [pltpu.make_async_copy(refs[k], buffers[k], sems.at[at]) for at, k in enumerate(far_args)]
            for move in moves:
                move.start()
            for k in far_args:
                refs[k] = buffers[k]
            for move in moves:
                move.wait()
            body(*refs)

        return pl.pallas_call(
            full if far_args else body,
            out_shape=outs + [shaped(args[k].shape, args[k].dtype) for k in keep],
            in_specs=[pl.BlockSpec(memory_space=pltpu.HBM if k in far_args else pltpu.VMEM) for k in range(len(args))],
            scratch_shapes=list(scratch) + [pltpu.VMEM(args[k].shape, args[k].dtype) for k in lost]
            + ([pltpu.SemaphoreType.DMA((len(far_args),))] if far_args else []),
            input_output_aliases=aliases or {},
            name=name,
            cost_estimate=pl.CostEstimate(flops=work, bytes_accessed=work, transcendentals=0),
            compiler_params=pltpu.CompilerParams(vmem_limit_bytes=50 * 2**20),
        )(*args)

    return run


def halves(value):
    top = value.astype(bf16)
    return top, (value - top.astype(f32)).astype(bf16)


def shaped(shape, kind=f32):
    return jax.ShapeDtypeStruct(shape, kind)


def cell_matrix(height, width, cells):
    pixel = lax.broadcasted_iota(jnp.int32, (height * width, cells), 0)
    cell = lax.broadcasted_iota(jnp.int32, (height * width, cells), 1)
    place = (pixel // width) // CELL * (width // CELL) + pixel % width // CELL
    return jnp.where(place == cell, 1.0, 0.0).astype(f32)


def modulate_body(frames, height, width, feats, mean, rstd, latent, gamma, beta, ws, bs, wt, bt, grads, weights, *refs):
    acts, (slope, normed_out, gain_out, tab_out, partial, shifted) = refs[:frames], refs[frames:]
    chans = feats.shape[1]
    groups = mean.shape[1]
    pixels = height * width
    lat = latent[0, lax.axis_index("ctx") * frames // CELL]
    group = lax.broadcasted_iota(jnp.int32, (groups, chans), 0)
    chan = lax.broadcasted_iota(jnp.int32, (groups, chans), 1)
    member = jnp.where(chan // (chans // groups) == group, 1.0, 0.0).astype(f32)
    mean_chan = exact(mean[...], member, ROWS_COLS)
    rstd_chan = exact(rstd[...], member, ROWS_COLS)
    scale_tab = exact(lat, ws[...], COLS_COLS) + bs[...]
    shift_tab = exact(lat, wt[...], COLS_COLS) + bt[...]
    tab_out[...] = scale_tab
    cells = cell_matrix(height, width, lat.shape[1])
    scale_map = exact(cells, scale_tab, ROWS_COLS)
    shift_map = exact(cells, shift_tab, ROWS_COLS)
    gain_out[...] = scale_map * (gamma[...] * rstd_chan)
    for frame in range(frames):
        at = pl.ds(frame * pixels, pixels)
        normed = (feats[at, :].astype(f32) - mean_chan) * rstd_chan
        modulated = (normed * gamma[...] + beta[...]) * scale_map + shift_map
        squashed = jax.nn.sigmoid(modulated)
        normed_out[at, :] = normed
        slope[at, :] = squashed * (1.0 + modulated * (1.0 - squashed))
        acts[frame][...] = (modulated * squashed).T.astype(bf16)
    conv_own_body(frames, height, width, grads, weights, partial, shifted)


def column_shifts(value, width):
    column = lax.broadcasted_iota(jnp.int32, value.shape, 0) % width
    rows = value.shape[0]
    return (
        jnp.where(column == width - 1, 0.0, pltpu.roll(value, rows - 1, 0)),
        value,
        jnp.where(column == 0, 0.0, pltpu.roll(value, 1, 0)),
    )


def clear_borders(padded, width):
    lead = padded.shape[:-2]
    length, lanes = padded.shape[-2:]
    edge = jnp.zeros(lead + (width, lanes), padded.dtype)
    every = (slice(None),) * len(lead)
    padded[every + (slice(0, width),)] = edge
    padded[every + (slice(length - width, length),)] = edge


def put_shifts(shifted, source, frames, pixels, width):
    clear_borders(shifted, width)
    for col, value in enumerate(column_shifts(source[...].astype(f32), width)):
        for frame in range(frames):
            shifted[col, frame, width:width + pixels] = value[frame * pixels:(frame + 1) * pixels].astype(bf16)


def taps_of(weights, step, chans):
    return jnp.concatenate(
        [weights[(step * TAPS * TAPS + k) * chans:(step * TAPS * TAPS + k + 1) * chans, :]
         for k in range(TAPS * TAPS)], axis=1)


def shifted_rows(shifted, frame_list, pixels, width):
    def window(frame, row, col):
        start = (TAPS - 1 - row) * width
        return shifted[col, frame, start:start + pixels]

    return jnp.concatenate(
        [jnp.concatenate([window(frame, k // TAPS, k % TAPS) for k in range(TAPS * TAPS)], axis=1)
         for frame in frame_list], axis=0)


def add_rows(total, term, first):
    if first == 0 and term.shape[0] == total.shape[0]:
        total[...] += term
    else:
        total[first:first + term.shape[0]] += term


def conv_own_body(frames, height, width, grads, weights, total, shifted):
    pixels = height * width
    chans = total.shape[1]
    put_shifts(shifted, grads, frames, pixels, width)
    total[...] = jnp.zeros_like(total)
    for step in range(TAPS):
        pairs = [(t, t + TAPS - 1 - step) for t in range(frames) if t + TAPS - 1 - step < frames]
        if pairs:
            rows = shifted_rows(shifted, [frame for _, frame in pairs], pixels, width)
            add_rows(total, dot(rows, taps_of(weights, step, chans), ROWS_ROWS), pairs[0][0] * pixels)

    @pl.when(lax.axis_index("ctx") == 0)
    def _():
        for step in range(TAPS - 1):
            for frame in range(TAPS - 1 - step):
                rows = shifted_rows(shifted, [frame], pixels, width)
                add_rows(total, dot(rows, taps_of(weights, step, chans), ROWS_ROWS), 0)


def input_grad_body(frames, height, width, beyond, weights, partial, slope, normed, gain, tab, latent,
                    ws, wt, gamma, beta, feats_grad, small, lat_own, lat_far, shifted, total):
    pixels = height * width
    chans = gain.shape[1]
    device = lax.axis_index("ctx")
    put_shifts(shifted, beyond, frames, pixels, width)
    total[...] = partial[...]
    for step in range(TAPS):
        pairs = [(t, t + TAPS - 1 - step - frames) for t in range(frames) if t + TAPS - 1 - step >= frames]
        if pairs:
            rows = shifted_rows(shifted, [frame for _, frame in pairs], pixels, width)
            add_rows(total, dot(rows, taps_of(weights, step, chans), ROWS_ROWS), pairs[0][0] * pixels)

    pooled_shift = jnp.zeros((pixels, chans), f32)
    pooled_norm = jnp.zeros((pixels, chans), f32)
    for frame in range(frames):
        at = pl.ds(frame * pixels, pixels)
        pre = total[at, :] * slope[at, :]
        feats_grad[at, :] = (pre * gain[...]).astype(bf16)
        pooled_shift += pre
        pooled_norm += pre * normed[at, :]
    lat = latent[0, device * frames // CELL]
    depth, length = lat.shape
    cells = cell_matrix(height, width, length)
    shift_pool = exact(cells, pooled_shift, COLS_COLS)
    norm_pool = exact(cells, pooled_norm, COLS_COLS)
    scale_pool = norm_pool * gamma[...] + shift_pool * beta[...]
    parts = [exact(lat, scale_pool, ROWS_COLS), exact(lat, shift_pool, ROWS_COLS)]
    for field in (norm_pool * tab[...], shift_pool * tab[...], scale_pool, shift_pool):
        parts.append(jnp.sum(field, axis=0, keepdims=True))
    lanes = small.shape[1]
    small[small.shape[0] - TILE:] = jnp.zeros((TILE, lanes), f32)
    at = 0
    for k in range(chans // lanes):
        for part in parts:
            small[at:at + part.shape[0]] = part[:, k * lanes:(k + 1) * lanes]
            at += part.shape[0]
    latent_sum = exact(scale_pool, ws[...], ROWS_ROWS) + exact(shift_pool, wt[...], ROWS_ROWS)
    first, second = latent_sum[:length // 2], latent_sum[length // 2:]
    even = device % 2 == 0
    lat_own[...] = jnp.where(even, first, second)
    lat_far[...] = jnp.where(even, second, first)


class FilterParts:
    def __init__(self, frames, height, width, videos, near, piece, packs, blocks, lanes, chans):
        self.frames, self.pixels, self.width, self.videos, self.near = frames, height * width, width, videos, near
        self.piece, self.packs, self.blocks, self.lanes, self.chans = piece, packs, blocks, lanes, chans
        self.cols = lanes // videos
        self.per = min(videos, TAPS)
        self.banks = -(-TAPS // self.per)
        self.slots = [(row, bank) for row in range(TAPS) for bank in range(self.banks)]
        self.rows = TAPS**3 * chans // (blocks.shape[0] * near)

    def pack(self, sources):
        clear_borders(self.packs, self.width)
        lane = lax.broadcasted_iota(jnp.int32, (1, self.lanes), 1)
        turn = lax.rem(self.lanes - lax.axis_index("vid") * self.cols, self.lanes)
        for video, source in enumerate(sources):
            moved = column_shifts(pltpu.roll(source[...].astype(f32), turn, 1), self.width)
            for bank in range(self.banks):
                packed = moved[bank * self.per]
                for k in range(1, min(self.per, TAPS - bank * self.per)):
                    other = pltpu.roll(moved[bank * self.per + k], k * self.cols, 1)
                    packed = jnp.where(lane >= k * self.cols, other, packed)
                packed = packed.astype(bf16)
                for frame in range(self.frames):
                    self.packs[video, bank, frame, self.width:self.width + self.pixels] = (
                        packed[frame * self.pixels:(frame + 1) * self.pixels])

    def product(self, acts, pairs):
        def window(video, frame, row, bank):
            start = (TAPS - 1 - row) * self.width
            return self.packs[video, bank, frame, start:start + self.pixels]

        left = jnp.concatenate(
            [acts[t * self.videos + video][...] for video in range(self.videos) for t, _ in pairs], axis=1)
        right = jnp.concatenate(
            [jnp.concatenate([window(video, frame, row, bank) for row, bank in self.slots], axis=1)
             for video in range(self.videos) for _, frame in pairs], axis=0)
        return dot(left, right, ROWS_COLS)

    def put(self, step, result, add):
        for place, (row, bank) in enumerate(self.slots):
            tile = None if result is None else result[:, place * self.lanes:(place + 1) * self.lanes]
            for k in range(min(self.per, TAPS - bank * self.per)):
                tap = (step * TAPS + row) * TAPS + bank * self.per + k
                done = 0
                while done < self.chans:
                    index = tap * self.chans + done
                    owner, inside = index // self.rows, index % self.rows
                    part, at = inside // self.piece, inside % self.piece
                    length = min(self.chans - done, self.rows - inside, self.piece - at)
                    low, high = part * self.cols, (part + 1) * self.cols
                    dest = self.blocks.at[owner // self.near, owner % self.near, at:at + length, low:high]
                    if tile is None:
                        dest[...] = jnp.zeros((length, self.cols), f32)
                    else:
                        value = tile[done:done + length]
                        turn = (part - k) * self.cols % self.lanes
                        if turn:
                            value = pltpu.roll(value, turn, 1)
                        value = value[:, low:high]
                        dest[...] = dest[...] + value if add else value
                    done += length


def filter_own_body(frames, height, width, videos, near, piece, *refs):
    acts, refs = refs[:frames * videos], refs[frames * videos:]
    grads, (_, blocks, packs) = refs[:videos], refs[videos:]
    parts = FilterParts(frames, height, width, videos, near, piece, packs, blocks, grads[0].shape[1], acts[0].shape[0])
    parts.pack(grads)
    far, lanes = blocks.shape[0], blocks.shape[3]
    first = lax.axis_index("ctx") == 0
    if piece * videos > parts.rows:
        blocks[:, :, piece - TILE:] = jnp.zeros((far, near, TILE, lanes), f32)
    for step in range(TAPS):
        pairs = [(t, t + TAPS - 1 - step) for t in range(frames) if t + TAPS - 1 - step < frames]
        parts.put(step, parts.product(acts, pairs) if pairs else None, False)
        if step < TAPS - 1:
            @pl.when(first)
            def _(step=step):
                extra = [parts.product(acts, [(0, frame)]) for frame in range(TAPS - 1 - step)]
                parts.put(step, functools.reduce(lambda a, b: a + b, extra), True)


def filter_grad_body(frames, height, width, videos, near, piece, *refs):
    acts, refs = refs[:frames * videos], refs[frames * videos:]
    beyond, refs = refs[:videos], refs[videos + 2:]
    blocks, own_far, own_line, line_send, *sends, packs = refs
    parts = FilterParts(frames, height, width, videos, near, piece, packs, blocks, beyond[0].shape[1], acts[0].shape[0])
    parts.pack(beyond)
    far = blocks.shape[0]
    for step in range(TAPS):
        pairs = [(t, t + TAPS - 1 - step - frames) for t in range(frames) if t + TAPS - 1 - step >= frames]
        if pairs:
            parts.put(step, parts.product(acts, pairs), True)
    device = lax.axis_index("ctx")
    line, place = device // near, device % near
    own_line[...] = blocks[line]
    for k in range(near):
        line_send[k * piece:(k + 1) * piece] = blocks[line ^ 1, k].astype(bf16)
    for k in range(far - 2):
        own_far[k] = blocks[line ^ (k + 2), place]
        for turn, send in enumerate(sends, 1):
            send[k * piece:(k + 1) * piece] = blocks[line ^ (k + 2), place ^ turn].astype(bf16)


def first_sum_body(near, far, videos, *refs):
    own_far, own_line, line_got, refs = refs[0], refs[1], refs[2], refs[3:]
    plane_got, refs = refs[:near - 1][::-1], refs[near - 1:]
    smalls, lat_far, refs = refs[:videos], refs[videos], refs[videos + 1:]
    kept, small_out, refs = refs[0], refs[1], refs[2:]
    plane_sends, line_sends, total = refs[:near - 1], refs[near - 1:-1], refs[-1]
    piece = own_line.shape[1]
    count = smalls[0].shape[0]
    place = lax.axis_index("ctx") % near
    for k, send in enumerate(line_sends):
        send[...] = functools.reduce(
            lambda a, b: a + b[k * piece:(k + 1) * piece].astype(f32), plane_got, own_far[k]).astype(bf16)
    for k in range(near):
        total[k] = own_line[k] + line_got[k * piece:(k + 1) * piece].astype(f32)
    kept[...] = total[place]
    summed = functools.reduce(lambda a, b: a + b, [ref[...] for ref in smalls])
    small_out[...] = summed
    top, rest = halves(summed)
    lat_top, lat_rest = halves(lat_far[...])
    cells, depth = lat_top.shape
    at = piece + 2 * count
    for turn, send in enumerate(plane_sends, 1):
        send[0:piece] = total[place ^ turn].astype(bf16)
        send[piece:piece + count] = top
        send[piece + count:at] = rest
        send[at:at + cells, :depth] = lat_top
        send[at + cells:at + 2 * cells, :depth] = lat_rest


def last_sum_body(near, far, *refs):
    kept, small, lat_own, refs = refs[0], refs[1], refs[2], refs[3:]
    line_got, plane_got, refs = refs[:far - 2], refs[far - 2:near + far - 3][::-1], refs[near + far - 3:]
    filter_grad, mod_grads, vector_grads, latent_grad = refs
    piece, lanes = kept.shape
    count = small.shape[0]

    def joined(ref, start, length):
        return ref[start:start + length].astype(f32) + ref[start + length:start + 2 * length].astype(f32)

    total = functools.reduce(lambda a, b: a + b[0:piece].astype(f32), plane_got + line_got, kept[...])
    cols, rows = filter_grad.shape
    turned = total.T
    for part in range(lanes // cols):
        first, last = part * piece, min(rows, (part + 1) * piece)
        if first < last:
            filter_grad[:, first:last] = turned[part * cols:(part + 1) * cols, :last - first]
    summed = functools.reduce(lambda a, b: a + joined(b, piece, count), plane_got, small[...])
    split, length = mod_grads.shape[0], mod_grads.shape[0] + vector_grads.shape[0]
    for k in range(mod_grads.shape[1] // lanes):
        mod_grads[:, k * lanes:(k + 1) * lanes] = summed[k * length:k * length + split]
        vector_grads[:, k * lanes:(k + 1) * lanes] = summed[k * length + split:(k + 1) * length]
    cells, depth = lat_own.shape
    latent_grad[...] = lat_own[...] + joined(plane_got[0], piece + 2 * count, cells)[:, :depth]


def local(features, grad_out, mean, rstd, latent, gamma, beta, ws, bs, wt, bt, kernel):
    _, frames, height, width, chans = features.shape
    outs = grad_out.shape[-1]
    depth, length = latent.shape[2:]
    count, videos = lax.axis_size("ctx"), lax.axis_size("vid")
    near = math.gcd(count, NEAR)
    far = count // near
    pixels = height * width
    size = frames * pixels
    rows, cols = TAPS**3 * chans // count, outs // videos
    piece = -(-rows // (TILE * videos)) * TILE
    gamma, beta, bs, bt = (value.reshape(1, chans) for value in (gamma, beta, bs, bt))
    feats = features.reshape(size, chans)
    grads = grad_out.reshape(size, outs)

    def along_ctx(value, target):
        return lax.ppermute(value, "ctx", [(s, target(s)) for s in range(count)])

    def others(value):
        return [value] + [
            lax.ppermute(value, "vid", [(s, (s + turn) % videos) for s in range(videos)])
            for turn in range(1, videos)]

    def plane_got(values):
        got = {turn: along_ctx(values[turn - 1], lambda s: s ^ turn) for turn in range(near - 1, 0, -1)}
        return [got[turn] for turn in range(1, near)]

    def line_got(values, first):
        turns = range(first, first + len(values))
        got = {turn: along_ctx(values[turn - first], lambda s: s ^ (turn * near)) for turn in reversed(turns)}
        return [got[turn] for turn in turns]

    beyond = lax.ppermute(grads, "ctx", [(s, s - 1) for s in range(1, count)])
    shifts = pltpu.VMEM((TAPS, frames, (height + 2) * width, outs), bf16)
    *acts, slope, normed, gain, tab, partial, latent, gamma, beta, ws, wt, grads_near, kernel = call(
        functools.partial(modulate_body, frames, height, width),
        [shaped((chans, pixels), bf16)] * frames
        + [shaped((size, chans)), shaped((size, chans)), shaped((pixels, chans)),
         shaped((length, chans)), shaped((size, chans))],
        (shifts,),
        name="modulate",
        far_args=tuple(range(12)),
        keep=(3, 4, 5, 6, 8, 10, 11),
    )(feats, mean, rstd, latent, gamma, beta, ws, bs, wt, bt, grads, kernel)
    acts_all = [value for act in acts for value in others(act)]
    grads_all = others(grads_near)
    beyond_all = others(beyond)
    cells = length // 2
    count_small = -(-(2 * depth + 4) * (chans // outs) // TILE) * TILE
    feats_grad, small, lat_own, lat_far = call(
        functools.partial(input_grad_body, frames, height, width),
        (shaped((size, chans), bf16), shaped((count_small, outs)), shaped((cells, depth)), shaped((cells, depth))),
        (shifts, pltpu.VMEM((size, chans), f32)),
        name="input_grad",
        work=2 * size * TAPS**3 * chans * outs,
    )(beyond, kernel, partial, slope, normed, gain, tab, latent, ws, wt, gamma, beta)
    banks = -(-TAPS // min(videos, TAPS))
    packs = pltpu.VMEM((videos, banks, frames, (height + 2) * width, outs), bf16)
    blocks, = call(
        functools.partial(filter_own_body, frames, height, width, videos, near, piece),
        (shaped((far, near, piece, outs)),),
        (packs,),
        name="filter_own",
    )(*acts_all, *grads_all, lat_far)
    got, blocks = lax.optimization_barrier((along_ctx(small, lambda s: s ^ near), blocks))
    small = small + got
    blocks, own_far, own_line, line_send, *plane_sends = call(
        functools.partial(filter_grad_body, frames, height, width, videos, near, piece),
        [shaped(blocks.shape), shaped((far - 2, piece, outs)), shaped((near, piece, outs)),
         shaped((near * piece, outs), bf16)]
        + [shaped(((far - 2) * piece, outs), bf16)] * (near - 1),
        (packs,),
        name="filter_grad",
        aliases={(frames + 1) * videos: 0},
    )(*acts_all, *beyond_all, blocks, small)
    step = 2
    while step < far:
        got = along_ctx(small, lambda s: s ^ (step * near))
        got, line_send, *plane_sends = lax.optimization_barrier((got, line_send, *plane_sends))
        small = small + got
        step *= 2
    extra = 2 * count_small + -(-2 * cells // TILE) * TILE
    line_in = line_got([line_send], 1)
    plane_in = plane_got(plane_sends)
    kept, small, *sends = call(
        functools.partial(first_sum_body, near, far, videos),
        [shaped((piece, outs)), shaped((count_small, outs))]
        + [shaped((piece + extra, outs), bf16)] * (near - 1) + [shaped((piece, outs), bf16)] * (far - 2),
        (pltpu.VMEM((near, piece, outs), f32),),
        name="first_sum",
    )(own_far, own_line, *line_in, *plane_in[::-1], *others(small), lat_far)
    line_in = line_got(sends[near - 1:], 2)
    plane_in = plane_got(sends[:near - 1])
    filter_grad, mod_grads, vector_grads, latent_grad = call(
        functools.partial(last_sum_body, near, far),
        (shaped((cols, rows)), shaped((2 * depth, chans)), shaped((4, chans)), shaped((cells, depth))),
        name="last_sum",
    )(kept, small, lat_own, *line_in[::-1], *plane_in[::-1])
    return (
        feats_grad.reshape(features.shape),
        filter_grad.T,
        mod_grads.reshape(2, depth, chans),
        vector_grads,
        latent_grad.T[None, None],
    )


def solution(mesh):
    split = P("vid", "ctx", None, None, None)
    return jax.shard_map(
        local,
        mesh=mesh,
        in_specs=(split, split, P("vid", None), P("vid", None), P("vid", None, None, None)) + (P(),) * 7,
        out_specs=(split, P("ctx", "vid"), P(), P(), P("vid", "ctx", None, None)),
        check_vma=False,
    )
```

```python
import functools
import math

import jax
import jax.numpy as jnp
from jax import lax
from jax.experimental import pallas as pl
from jax.experimental.pallas import tpu as pltpu
from jax.sharding import PartitionSpec as P

NEAR = 4
CELL = 4
TAPS = 3
TILE = 16

f32 = jnp.float32
bf16 = jnp.bfloat16
dot = functools.partial(lax.dot_general, preferred_element_type=f32)
exact = functools.partial(dot, precision=lax.Precision.HIGHEST)
ROWS_COLS = (((1,), (0,)), ((), ()))
ROWS_ROWS = (((1,), (1,)), ((), ()))
COLS_COLS = (((0,), (0,)), ((), ()))


def call(body, outs, scratch=(), name=None, far_args=(), keep=(), work=1000):
    outs = list(outs)
    lost = [k for k in far_args if k not in keep]

    def run(*args):
        args = [pltpu.with_memory_space_constraint(arg, pltpu.HBM) if k in far_args else arg
                for k, arg in enumerate(args)]

        def full(*refs):
            refs = list(refs)
            sems = refs.pop()
            buffers = {k: refs.pop() for k in lost[::-1]}
            first = len(args) + len(outs)
            buffers.update({k: refs.pop(first) for k in keep})
            moves = [pltpu.make_async_copy(refs[k], buffers[k], sems.at[at]) for at, k in enumerate(far_args)]
            for move in moves:
                move.start()
            for k in far_args:
                refs[k] = buffers[k]
            for move in moves:
                move.wait()
            body(*refs)

        return pl.pallas_call(
            full if far_args else body,
            out_shape=outs + [shaped(args[k].shape, args[k].dtype) for k in keep],
            in_specs=[pl.BlockSpec(memory_space=pltpu.HBM if k in far_args else pltpu.VMEM) for k in range(len(args))],
            scratch_shapes=list(scratch) + [pltpu.VMEM(args[k].shape, args[k].dtype) for k in lost]
            + ([pltpu.SemaphoreType.DMA((len(far_args),))] if far_args else []),
            name=name,
            cost_estimate=pl.CostEstimate(flops=work, bytes_accessed=work, transcendentals=0),
            compiler_params=pltpu.CompilerParams(vmem_limit_bytes=28 * 2**20),
        )(*args)

    return run


def halves(value):
    top = value.astype(bf16)
    return top, (value - top.astype(f32)).astype(bf16)


def shaped(shape, kind=f32):
    return jax.ShapeDtypeStruct(shape, kind)


def cell_matrix(height, width, cells):
    pixel = lax.broadcasted_iota(jnp.int32, (height * width, cells), 0)
    cell = lax.broadcasted_iota(jnp.int32, (height * width, cells), 1)
    place = (pixel // width) // CELL * (width // CELL) + pixel % width // CELL
    return jnp.where(place == cell, 1.0, 0.0).astype(f32)


def modulate_body(frames, height, width, feats, mean, rstd, latent, gamma, beta, ws, bs, wt, bt, grads, weights, *refs):
    acts, (slope, normed_out, gain_out, tab_out, partial, shifted) = refs[:frames], refs[frames:]
    chans = feats.shape[1]
    groups = mean.shape[1]
    pixels = height * width
    lat = latent[0, lax.axis_index("ctx") * frames // CELL]
    group = lax.broadcasted_iota(jnp.int32, (groups, chans), 0)
    chan = lax.broadcasted_iota(jnp.int32, (groups, chans), 1)
    member = jnp.where(chan // (chans // groups) == group, 1.0, 0.0).astype(f32)
    mean_chan = exact(mean[...], member, ROWS_COLS)
    rstd_chan = exact(rstd[...], member, ROWS_COLS)
    scale_tab = exact(lat, ws[...], COLS_COLS) + bs[...]
    shift_tab = exact(lat, wt[...], COLS_COLS) + bt[...]
    tab_out[...] = scale_tab
    cells = cell_matrix(height, width, lat.shape[1])
    scale_map = exact(cells, scale_tab, ROWS_COLS)
    shift_map = exact(cells, shift_tab, ROWS_COLS)
    gain_out[...] = scale_map * (gamma[...] * rstd_chan)
    for frame in range(frames):
        at = pl.ds(frame * pixels, pixels)
        normed = (feats[at, :].astype(f32) - mean_chan) * rstd_chan
        modulated = (normed * gamma[...] + beta[...]) * scale_map + shift_map
        squashed = jax.nn.sigmoid(modulated)
        normed_out[at, :] = normed
        slope[at, :] = squashed * (1.0 + modulated * (1.0 - squashed))
        acts[frame][...] = (modulated * squashed).T.astype(bf16)
    conv_own_body(frames, height, width, grads, weights, partial, shifted)


def column_shifts(value, width):
    column = lax.broadcasted_iota(jnp.int32, value.shape, 0) % width
    rows = value.shape[0]
    return (
        jnp.where(column == width - 1, 0.0, pltpu.roll(value, rows - 1, 0)),
        value,
        jnp.where(column == 0, 0.0, pltpu.roll(value, 1, 0)),
    )


def clear_borders(padded, width):
    lead = padded.shape[:-2]
    length, lanes = padded.shape[-2:]
    edge = jnp.zeros(lead + (width, lanes), padded.dtype)
    every = (slice(None),) * len(lead)
    padded[every + (slice(0, width),)] = edge
    padded[every + (slice(length - width, length),)] = edge


def put_shifts(shifted, source, frames, pixels, width):
    clear_borders(shifted, width)
    for col, value in enumerate(column_shifts(source[...].astype(f32), width)):
        for frame in range(frames):
            shifted[col, frame, width:width + pixels] = value[frame * pixels:(frame + 1) * pixels].astype(bf16)


def taps_of(weights, step, chans):
    return jnp.concatenate(
        [weights[(step * TAPS * TAPS + k) * chans:(step * TAPS * TAPS + k + 1) * chans, :]
         for k in range(TAPS * TAPS)], axis=1)


def shifted_rows(shifted, frame_list, pixels, width):
    def window(frame, row, col):
        start = (TAPS - 1 - row) * width
        return shifted[col, frame, start:start + pixels]

    return jnp.concatenate(
        [jnp.concatenate([window(frame, k // TAPS, k % TAPS) for k in range(TAPS * TAPS)], axis=1)
         for frame in frame_list], axis=0)


def add_rows(total, term, first):
    if first == 0 and term.shape[0] == total.shape[0]:
        total[...] += term
    else:
        total[first:first + term.shape[0]] += term


def conv_own_body(frames, height, width, grads, weights, total, shifted):
    pixels = height * width
    chans = total.shape[1]
    put_shifts(shifted, grads, frames, pixels, width)
    total[...] = jnp.zeros_like(total)
    for step in range(TAPS):
        pairs = [(t, t + TAPS - 1 - step) for t in range(frames) if t + TAPS - 1 - step < frames]
        if pairs:
            rows = shifted_rows(shifted, [frame for _, frame in pairs], pixels, width)
            add_rows(total, dot(rows, taps_of(weights, step, chans), ROWS_ROWS), pairs[0][0] * pixels)

    @pl.when(lax.axis_index("ctx") == 0)
    def _():
        for step in range(TAPS - 1):
            for frame in range(TAPS - 1 - step):
                rows = shifted_rows(shifted, [frame], pixels, width)
                add_rows(total, dot(rows, taps_of(weights, step, chans), ROWS_ROWS), 0)


def input_grad_body(frames, height, width, beyond, weights, partial, slope, normed, gain, tab, latent,
                    ws, wt, gamma, beta, feats_grad, small, lat_own, shifted, total):
    pixels = height * width
    chans = gain.shape[1]
    device = lax.axis_index("ctx")
    put_shifts(shifted, beyond, frames, pixels, width)
    total[...] = partial[...]
    for step in range(TAPS):
        pairs = [(t, t + TAPS - 1 - step - frames) for t in range(frames) if t + TAPS - 1 - step >= frames]
        if pairs:
            rows = shifted_rows(shifted, [frame for _, frame in pairs], pixels, width)
            add_rows(total, dot(rows, taps_of(weights, step, chans), ROWS_ROWS), pairs[0][0] * pixels)

    pooled_shift = jnp.zeros((pixels, chans), f32)
    pooled_norm = jnp.zeros((pixels, chans), f32)
    for frame in range(frames):
        at = pl.ds(frame * pixels, pixels)
        pre = total[at, :] * slope[at, :]
        feats_grad[at, :] = (pre * gain[...]).astype(bf16)
        pooled_shift += pre
        pooled_norm += pre * normed[at, :]
    lat = latent[0, device * frames // CELL]
    depth, length = lat.shape
    cells = cell_matrix(height, width, length)
    shift_pool = exact(cells, pooled_shift, COLS_COLS)
    norm_pool = exact(cells, pooled_norm, COLS_COLS)
    scale_pool = norm_pool * gamma[...] + shift_pool * beta[...]
    parts = [exact(lat, scale_pool, ROWS_COLS), exact(lat, shift_pool, ROWS_COLS)]
    for field in (norm_pool * tab[...], shift_pool * tab[...], scale_pool, shift_pool):
        parts.append(jnp.sum(field, axis=0, keepdims=True))
    lanes = small.shape[1]
    small[small.shape[0] - TILE:] = jnp.zeros((TILE, lanes), f32)
    at = 0
    for k in range(chans // lanes):
        for part in parts:
            small[at:at + part.shape[0]] = part[:, k * lanes:(k + 1) * lanes]
            at += part.shape[0]
    latent_sum = exact(scale_pool, ws[...], ROWS_ROWS) + exact(shift_pool, wt[...], ROWS_ROWS)
    first, second = latent_sum[:length // 2], latent_sum[length // 2:]
    even = device % 2 == 0
    lat_own[...] = jnp.where(even, first, second)
    lat_far = jnp.where(even, second, first)
    here = lax.axis_index("vid")
    for video in range(lanes // depth):
        @pl.when(here == video)
        def _(video=video):
            small[at:at + length // 2, video * depth:(video + 1) * depth] = lat_far


class FilterParts:
    def __init__(self, frames, height, width, videos, near, shifted, blocks, chans):
        self.frames, self.pixels, self.width, self.videos, self.near = frames, height * width, width, videos, near
        self.shifted, self.blocks, self.lanes, self.chans = shifted, blocks, blocks.shape[3], chans
        owners = blocks.shape[0] * near
        self.rows = TAPS**3 * chans // owners
        pair = lax.axis_index("ctx") // near // 2
        self.start, self.stop = pair * 2 * near * self.rows, (pair + 1) * 2 * near * self.rows
        self.even = lax.axis_index("vid") % 2 == 0

    def needed(self, step, row):
        low = (step * TAPS + row) * TAPS * self.chans
        high = low + TAPS * self.chans
        inside = (low < self.stop) & (high > self.start)
        outside = (low < self.start) | (high > self.stop)
        return jnp.where(self.even, inside.astype(jnp.int32), outside.astype(jnp.int32)) == 1

    def shift(self, sources):
        for video, source in enumerate(sources):
            put_shifts(self.shifted.at[video], source, self.frames, self.pixels, self.width)

    def product(self, acts, row, pairs):
        start = (TAPS - 1 - row) * self.width
        left = jnp.concatenate(
            [acts[t * self.videos + video][...] for video in range(self.videos) for t, _ in pairs], axis=1)
        right = jnp.concatenate(
            [jnp.concatenate([self.shifted[video, col, frame, start:start + self.pixels] for col in range(TAPS)], axis=1)
             for video in range(self.videos) for _, frame in pairs], axis=0)
        return dot(left, right, ROWS_COLS)

    def put(self, step, row, result, base=None):
        for col in range(TAPS):
            tap = (step * TAPS + row) * TAPS + col
            done = 0
            while done < self.chans:
                index = tap * self.chans + done
                owner, at = index // self.rows, index % self.rows
                length = min(self.chans - done, self.rows - at)
                part = (owner // self.near, owner % self.near, slice(at, at + length))
                terms = [] if base is None else [base[part]]
                if result is not None:
                    terms.append(result[done:done + length, col * self.lanes:(col + 1) * self.lanes])
                self.blocks[part] = sum(terms[1:], terms[0]) if terms else jnp.zeros((length, self.lanes), f32)
                done += length


def filter_own_body(frames, height, width, videos, near, *refs):
    acts, refs = refs[:frames * videos], refs[frames * videos:]
    grads, (_, blocks, shifted) = refs[:videos], refs[videos:]
    parts = FilterParts(frames, height, width, videos, near, shifted, blocks, acts[0].shape[0])
    parts.shift(grads)
    first = lax.axis_index("ctx") == 0
    for step in range(TAPS):
        pairs = [(t, t + TAPS - 1 - step) for t in range(frames) if t + TAPS - 1 - step < frames]
        for row in range(TAPS):
            @pl.when(parts.needed(step, row))
            def _(step=step, row=row, pairs=pairs):
                parts.put(step, row, parts.product(acts, row, pairs) if pairs else None)
                if step < TAPS - 1:
                    @pl.when(first)
                    def _():
                        extra = [parts.product(acts, row, [(0, frame)]) for frame in range(TAPS - 1 - step)]
                        parts.put(step, row, functools.reduce(lambda a, b: a + b, extra), blocks)


def put_pair(ref, at, value):
    top, rest = halves(value)
    ref[at:at + value.shape[0]] = top
    ref[at + value.shape[0]:at + 2 * value.shape[0]] = rest


def take_pair(ref, at, length):
    return ref[at:at + length].astype(f32) + ref[at + length:at + 2 * length].astype(f32)


def filter_grad_body(frames, height, width, videos, near, *refs):
    acts, refs = refs[:frames * videos], refs[frames * videos:]
    beyond, refs = refs[:videos], refs[videos:]
    smalls, base, refs = refs[:videos], refs[videos], refs[videos + 1:]
    own_far, own_line, small_out, line_send, *sends, shifted, blocks = refs
    parts = FilterParts(frames, height, width, videos, near, shifted, blocks, acts[0].shape[0])
    parts.shift(beyond)
    far, _, piece, _ = blocks.shape
    for step in range(TAPS):
        pairs = [(t, t + TAPS - 1 - step - frames) for t in range(frames) if t + TAPS - 1 - step >= frames]
        for row in range(TAPS):
            @pl.when(parts.needed(step, row))
            def _(step=step, row=row, pairs=pairs):
                parts.put(step, row, parts.product(acts, row, pairs) if pairs else None, base)
    device = lax.axis_index("ctx")
    line, place = device // near, device % near
    small = functools.reduce(lambda a, b: a + b, [ref[...] for ref in smalls])
    small_out[...] = small

    @pl.when(parts.even)
    def _():
        own_line[...] = blocks[line]
        for k in range(near):
            line_send[k * piece:(k + 1) * piece] = blocks[line ^ 1, k].astype(bf16)

    @pl.when(jnp.logical_not(parts.even))
    def _():
        for k in range(far - 2):
            own_far[k] = blocks[line ^ (k + 2), place]
        for turn, send in enumerate(sends, 1):
            for k in range(far - 2):
                send[k * piece:(k + 1) * piece] = blocks[line ^ (k + 2), place ^ turn].astype(bf16)
            put_pair(send, (far - 2) * piece, small)


def first_sum_body(near, far, entries, *refs):
    own_far, own_line, small, line_got, refs = *refs[:4], refs[4:]
    plane_got, refs = refs[:near - 1][::-1], refs[near - 1:]
    kept, small_out, small_send, refs = *refs[:3], refs[3:]
    plane_sends, line_sends, total = refs[:near - 1], refs[near - 1:-1], refs[-1]
    piece = own_line.shape[1]
    count = small.shape[0]
    place = lax.axis_index("ctx") % near
    even = lax.axis_index("vid") % 2 == 0

    @pl.when(even)
    def _():
        for k in range(near):
            total[k] = own_line[k] + line_got[k * piece:(k + 1) * piece].astype(f32)
        kept[...] = total[place]
        for turn, send in enumerate(plane_sends, 1):
            send[...] = total[place ^ turn].astype(bf16)

    @pl.when(jnp.logical_not(even))
    def _():
        got = [take_pair(ref, (far - 2) * piece, count) for ref in plane_got]
        row = lax.broadcasted_iota(jnp.int32, small.shape, 0)
        summed = jnp.where(row < entries, functools.reduce(lambda a, b: a + b, got, small[...]), got[0])
        small_out[...] = summed
        put_pair(small_send, 0, summed)
        for k, send in enumerate(line_sends):
            send[0:piece] = functools.reduce(
                lambda a, b: a + b[k * piece:(k + 1) * piece].astype(f32), plane_got, own_far[k]).astype(bf16)
            put_pair(send, piece, summed)


def last_sum_body(near, far, entries, *refs):
    kept, small, small_got, refs = *refs[:3], refs[3:]
    line_got, plane_got, refs = refs[:far - 2], refs[far - 2:near + far - 3], refs[near + far - 3:]
    mine, theirs, small_out, turned = refs
    piece = kept.shape[0]
    count = small.shape[0]
    cols, rows = mine.shape
    here = lax.axis_index("vid")
    even = here % 2 == 0

    @pl.when(even)
    def _():
        turned[...] = functools.reduce(lambda a, b: a + b[...].astype(f32), plane_got, kept[...]).T

    @pl.when(jnp.logical_not(even))
    def _():
        total = functools.reduce(lambda a, b: a + b, [ref[0:piece].astype(f32) for ref in line_got])
        turned[...] = total.T
        got = [take_pair(ref, piece, count) for ref in line_got] + [take_pair(small_got, 0, count)]
        row = lax.broadcasted_iota(jnp.int32, small.shape, 0)
        small_out[...] = jnp.where(row < entries, functools.reduce(lambda a, b: a + b, got, small[...]), small[...])

    mine[...] = turned[pl.ds(pl.multiple_of(here * cols, cols), cols)][:, :rows]
    theirs[...] = turned[pl.ds(pl.multiple_of((here ^ 1) * cols, cols), cols)][:, :rows]


def finish_body(entries, mine, theirs, small, small_got, lat_own, filter_grad, mod_grads, vector_grads, latent_grad):
    filter_grad[...] = mine[...] + theirs[...]
    here = lax.axis_index("vid")
    summed = jnp.where(here % 2 == 0, small_got[...], small[...])
    lanes = small.shape[1]
    split, length = mod_grads.shape[0], mod_grads.shape[0] + vector_grads.shape[0]
    for k in range(mod_grads.shape[1] // lanes):
        mod_grads[:, k * lanes:(k + 1) * lanes] = summed[k * length:k * length + split]
        vector_grads[:, k * lanes:(k + 1) * lanes] = summed[k * length + split:(k + 1) * length]
    cells, depth = lat_own.shape
    for video in range(lanes // depth):
        @pl.when(here == video)
        def _(video=video):
            latent_grad[...] = lat_own[...] + summed[entries:entries + cells, video * depth:(video + 1) * depth]


def local(features, grad_out, mean, rstd, latent, gamma, beta, ws, bs, wt, bt, kernel):
    _, frames, height, width, chans = features.shape
    outs = grad_out.shape[-1]
    depth, length = latent.shape[2:]
    count, videos = lax.axis_size("ctx"), lax.axis_size("vid")
    near = math.gcd(count, NEAR)
    far = count // near
    pixels = height * width
    size = frames * pixels
    rows, cols = TAPS**3 * chans // count, outs // videos
    piece = -(-rows // TILE) * TILE
    gamma, beta, bs, bt = (value.reshape(1, chans) for value in (gamma, beta, bs, bt))
    feats = features.reshape(size, chans)
    grads = grad_out.reshape(size, outs)

    def along_ctx(value, target, odd):
        pairs = [(s * videos + v, target(s) * videos + v) for s in range(count) for v in range(odd, videos, 2)]
        return lax.ppermute(value, ("ctx", "vid"), pairs)

    def other_core(value):
        return lax.ppermute(value, "vid", [(v, v ^ 1) for v in range(videos)])

    def others(value):
        return [value] + [
            lax.ppermute(value, "vid", [(s, (s + turn) % videos) for s in range(videos)])
            for turn in range(1, videos)]

    def plane_got(values, odd):
        return [along_ctx(value, lambda s: s ^ turn, odd) for turn, value in enumerate(values, 1)]

    def line_got(values, first, odd):
        return [along_ctx(value, lambda s: s ^ (turn * near), odd) for turn, value in enumerate(values, first)]

    beyond = lax.ppermute(grads, "ctx", [(s, s - 1) for s in range(1, count)])
    shifts = pltpu.VMEM((TAPS, frames, (height + 2) * width, outs), bf16)
    *acts, slope, normed, gain, tab, partial, latent, gamma, beta, ws, wt, grads_near, kernel = call(
        functools.partial(modulate_body, frames, height, width),
        [shaped((chans, pixels), bf16)] * frames
        + [shaped((size, chans)), shaped((size, chans)), shaped((pixels, chans)),
         shaped((length, chans)), shaped((size, chans))],
        (shifts,),
        name="modulate",
        far_args=tuple(range(12)),
        keep=(3, 4, 5, 6, 8, 10, 11),
    )(feats, mean, rstd, latent, gamma, beta, ws, bs, wt, bt, grads, kernel)
    acts_all = [value for act in acts for value in others(act)]
    grads_all = others(grads_near)
    beyond_all = others(beyond)
    cells = length // 2
    entries = (2 * depth + 4) * (chans // outs)
    count_small = -(-(entries + cells) // TILE) * TILE
    feats_grad, small, lat_own = call(
        functools.partial(input_grad_body, frames, height, width),
        (shaped((size, chans), bf16), shaped((count_small, outs)), shaped((cells, depth))),
        (shifts, pltpu.VMEM((size, chans), f32)),
        name="input_grad",
    )(beyond, kernel, partial, slope, normed, gain, tab, latent, ws, wt, gamma, beta)
    smalls = others(small)
    shifts = pltpu.VMEM((videos, TAPS, frames, (height + 2) * width, outs), bf16)
    blocks, = call(
        functools.partial(filter_own_body, frames, height, width, videos, near),
        (shaped((far, near, piece, outs)),),
        (shifts,),
        name="filter_own",
    )(*acts_all, *grads_all, lat_own)
    own_far, own_line, small, line_send, *plane_sends = call(
        functools.partial(filter_grad_body, frames, height, width, videos, near),
        [shaped((far - 2, piece, outs)), shaped((near, piece, outs)),
         shaped((count_small, outs)), shaped((near * piece, outs), bf16)]
        + [shaped(((far - 2) * piece + 2 * count_small, outs), bf16)] * (near - 1),
        (shifts, pltpu.VMEM(blocks.shape, f32)),
        name="filter_grad",
    )(*acts_all, *beyond_all, *smalls, blocks)
    line_in = line_got([line_send], 1, 0)
    plane_in = plane_got(plane_sends, 1)
    kept, small, small_send, *sends = call(
        functools.partial(first_sum_body, near, far, entries),
        [shaped((piece, outs)), shaped((count_small, outs)), shaped((2 * count_small, outs), bf16)]
        + [shaped((piece, outs), bf16)] * (near - 1) + [shaped((piece + 2 * count_small, outs), bf16)] * (far - 2),
        (pltpu.VMEM((near, piece, outs), f32),),
        name="first_sum",
    )(own_far, own_line, small, *line_in, *plane_in[::-1])
    line_in = line_got(sends[near - 1:], 2, 1)
    plane_in = plane_got(sends[:near - 1], 0)
    mine, theirs, small = call(
        functools.partial(last_sum_body, near, far, entries),
        (shaped((cols, rows)), shaped((cols, rows)), shaped((count_small, outs))),
        (pltpu.VMEM((outs, piece), f32),),
        name="last_sum",
    )(kept, small, *line_got([small_send], 1, 1), *line_in[::-1], *plane_in[::-1])
    filter_grad, mod_grads, vector_grads, latent_grad = call(
        functools.partial(finish_body, entries),
        (shaped((cols, rows)), shaped((2 * depth, chans)), shaped((4, chans)), shaped((cells, depth))),
        name="finish",
    )(mine, other_core(theirs), small, other_core(small), lat_own)
    return (
        feats_grad.reshape(features.shape),
        filter_grad.T,
        mod_grads.reshape(2, depth, chans),
        vector_grads,
        latent_grad.T[None, None],
    )


def solution(mesh):
    split = P("vid", "ctx", None, None, None)
    return jax.shard_map(
        local,
        mesh=mesh,
        in_specs=(split, split, P("vid", None), P("vid", None), P("vid", None, None, None)) + (P(),) * 7,
        out_specs=(split, P("ctx", "vid"), P(), P(), P("vid", "ctx", None, None)),
        check_vma=False,
    )
```

```python
import functools
import math

import jax
import jax.numpy as jnp
from jax import lax
from jax.experimental import pallas as pl
from jax.experimental.pallas import tpu as pltpu
from jax.sharding import PartitionSpec as P

NEAR = 4
CELL = 4
TAPS = 3
TILE = 16

f32 = jnp.float32
bf16 = jnp.bfloat16
dot = functools.partial(lax.dot_general, preferred_element_type=f32)
exact = functools.partial(dot, precision=lax.Precision.HIGHEST)
ROWS_COLS = (((1,), (0,)), ((), ()))
ROWS_ROWS = (((1,), (1,)), ((), ()))
COLS_COLS = (((0,), (0,)), ((), ()))


def call(body, outs, scratch=(), name=None, far_args=(), keep=(), work=1000):
    outs = list(outs)
    lost = [k for k in far_args if k not in keep]

    def run(*args):
        args = [pltpu.with_memory_space_constraint(arg, pltpu.HBM) if k in far_args else arg
                for k, arg in enumerate(args)]

        def full(*refs):
            refs = list(refs)
            sems = refs.pop()
            buffers = {k: refs.pop() for k in lost[::-1]}
            first = len(args) + len(outs)
            buffers.update({k: refs.pop(first) for k in keep})
            moves = [pltpu.make_async_copy(refs[k], buffers[k], sems.at[at]) for at, k in enumerate(far_args)]
            for move in moves:
                move.start()
            for k in far_args:
                refs[k] = buffers[k]
            for move in moves:
                move.wait()
            body(*refs)

        return pl.pallas_call(
            full if far_args else body,
            out_shape=outs + [shaped(args[k].shape, args[k].dtype) for k in keep],
            in_specs=[pl.BlockSpec(memory_space=pltpu.HBM if k in far_args else pltpu.VMEM) for k in range(len(args))],
            scratch_shapes=list(scratch) + [pltpu.VMEM(args[k].shape, args[k].dtype) for k in lost]
            + ([pltpu.SemaphoreType.DMA((len(far_args),))] if far_args else []),
            name=name,
            cost_estimate=pl.CostEstimate(flops=work, bytes_accessed=work, transcendentals=0),
            compiler_params=pltpu.CompilerParams(vmem_limit_bytes=28 * 2**20),
        )(*args)

    return run


def halves(value):
    top = value.astype(bf16)
    return top, (value - top.astype(f32)).astype(bf16)


def shaped(shape, kind=f32):
    return jax.ShapeDtypeStruct(shape, kind)


def cell_matrix(height, width, cells):
    pixel = lax.broadcasted_iota(jnp.int32, (height * width, cells), 0)
    cell = lax.broadcasted_iota(jnp.int32, (height * width, cells), 1)
    place = (pixel // width) // CELL * (width // CELL) + pixel % width // CELL
    return jnp.where(place == cell, 1.0, 0.0).astype(f32)


def modulate_body(frames, height, width, feats, mean, rstd, latent, gamma, beta, ws, bs, wt, bt, grads, weights, *refs):
    acts, (slope, normed_out, gain_out, tab_out, partial, shifted) = refs[:frames], refs[frames:]
    chans = feats.shape[1]
    groups = mean.shape[1]
    pixels = height * width
    lat = latent[0, lax.axis_index("ctx") * frames // CELL]
    group = lax.broadcasted_iota(jnp.int32, (groups, chans), 0)
    chan = lax.broadcasted_iota(jnp.int32, (groups, chans), 1)
    member = jnp.where(chan // (chans // groups) == group, 1.0, 0.0).astype(f32)
    mean_chan = exact(mean[...], member, ROWS_COLS)
    rstd_chan = exact(rstd[...], member, ROWS_COLS)
    scale_tab = exact(lat, ws[...], COLS_COLS) + bs[...]
    shift_tab = exact(lat, wt[...], COLS_COLS) + bt[...]
    tab_out[...] = scale_tab
    cells = cell_matrix(height, width, lat.shape[1])
    scale_map = exact(cells, scale_tab, ROWS_COLS)
    shift_map = exact(cells, shift_tab, ROWS_COLS)
    gain_out[...] = scale_map * (gamma[...] * rstd_chan)
    for frame in range(frames):
        at = pl.ds(frame * pixels, pixels)
        normed = (feats[at, :].astype(f32) - mean_chan) * rstd_chan
        modulated = (normed * gamma[...] + beta[...]) * scale_map + shift_map
        squashed = jax.nn.sigmoid(modulated)
        normed_out[at, :] = normed
        slope[at, :] = squashed * (1.0 + modulated * (1.0 - squashed))
        acts[frame][...] = (modulated * squashed).T.astype(bf16)
    conv_own_body(frames, height, width, grads, weights, partial, shifted)


def column_shifts(value, width):
    column = lax.broadcasted_iota(jnp.int32, value.shape, 0) % width
    rows = value.shape[0]
    return (
        jnp.where(column == width - 1, 0.0, pltpu.roll(value, rows - 1, 0)),
        value,
        jnp.where(column == 0, 0.0, pltpu.roll(value, 1, 0)),
    )


def clear_borders(padded, width):
    lead = padded.shape[:-2]
    length, lanes = padded.shape[-2:]
    edge = jnp.zeros(lead + (width, lanes), padded.dtype)
    every = (slice(None),) * len(lead)
    padded[every + (slice(0, width),)] = edge
    padded[every + (slice(length - width, length),)] = edge


def put_shifts(shifted, source, frames, pixels, width):
    clear_borders(shifted, width)
    for col, value in enumerate(column_shifts(source[...].astype(f32), width)):
        for frame in range(frames):
            shifted[col, frame, width:width + pixels] = value[frame * pixels:(frame + 1) * pixels].astype(bf16)


def taps_of(weights, step, chans):
    return jnp.concatenate(
        [weights[(step * TAPS * TAPS + k) * chans:(step * TAPS * TAPS + k + 1) * chans, :]
         for k in range(TAPS * TAPS)], axis=1)


def shifted_rows(shifted, frame_list, pixels, width):
    def window(frame, row, col):
        start = (TAPS - 1 - row) * width
        return shifted[col, frame, start:start + pixels]

    return jnp.concatenate(
        [jnp.concatenate([window(frame, k // TAPS, k % TAPS) for k in range(TAPS * TAPS)], axis=1)
         for frame in frame_list], axis=0)


def add_rows(total, term, first):
    if first == 0 and term.shape[0] == total.shape[0]:
        total[...] += term
    else:
        total[first:first + term.shape[0]] += term


def conv_own_body(frames, height, width, grads, weights, total, shifted):
    pixels = height * width
    chans = total.shape[1]
    put_shifts(shifted, grads, frames, pixels, width)
    total[...] = jnp.zeros_like(total)
    for step in range(TAPS):
        pairs = [(t, t + TAPS - 1 - step) for t in range(frames) if t + TAPS - 1 - step < frames]
        if pairs:
            rows = shifted_rows(shifted, [frame for _, frame in pairs], pixels, width)
            add_rows(total, dot(rows, taps_of(weights, step, chans), ROWS_ROWS), pairs[0][0] * pixels)

    @pl.when(lax.axis_index("ctx") == 0)
    def _():
        for step in range(TAPS - 1):
            for frame in range(TAPS - 1 - step):
                rows = shifted_rows(shifted, [frame], pixels, width)
                add_rows(total, dot(rows, taps_of(weights, step, chans), ROWS_ROWS), 0)


def input_grad_body(frames, height, width, beyond, weights, partial, slope, normed, gain, tab, latent,
                    ws, wt, gamma, beta, feats_grad, small, lat_own, shifted, total):
    pixels = height * width
    chans = gain.shape[1]
    device = lax.axis_index("ctx")
    put_shifts(shifted, beyond, frames, pixels, width)
    total[...] = partial[...]
    for step in range(TAPS):
        pairs = [(t, t + TAPS - 1 - step - frames) for t in range(frames) if t + TAPS - 1 - step >= frames]
        if pairs:
            rows = shifted_rows(shifted, [frame for _, frame in pairs], pixels, width)
            add_rows(total, dot(rows, taps_of(weights, step, chans), ROWS_ROWS), pairs[0][0] * pixels)

    pooled_shift = jnp.zeros((pixels, chans), f32)
    pooled_norm = jnp.zeros((pixels, chans), f32)
    for frame in range(frames):
        at = pl.ds(frame * pixels, pixels)
        pre = total[at, :] * slope[at, :]
        feats_grad[at, :] = (pre * gain[...]).astype(bf16)
        pooled_shift += pre
        pooled_norm += pre * normed[at, :]
    lat = latent[0, device * frames // CELL]
    depth, length = lat.shape
    cells = cell_matrix(height, width, length)
    shift_pool = exact(cells, pooled_shift, COLS_COLS)
    norm_pool = exact(cells, pooled_norm, COLS_COLS)
    scale_pool = norm_pool * gamma[...] + shift_pool * beta[...]
    parts = [exact(lat, scale_pool, ROWS_COLS), exact(lat, shift_pool, ROWS_COLS)]
    for field in (norm_pool * tab[...], shift_pool * tab[...], scale_pool, shift_pool):
        parts.append(jnp.sum(field, axis=0, keepdims=True))
    lanes = small.shape[1]
    small[small.shape[0] - TILE:] = jnp.zeros((TILE, lanes), f32)
    at = 0
    for k in range(chans // lanes):
        for part in parts:
            small[at:at + part.shape[0]] = part[:, k * lanes:(k + 1) * lanes]
            at += part.shape[0]
    latent_sum = exact(scale_pool, ws[...], ROWS_ROWS) + exact(shift_pool, wt[...], ROWS_ROWS)
    first, second = latent_sum[:length // 2], latent_sum[length // 2:]
    even = device % 2 == 0
    lat_own[...] = jnp.where(even, first, second)
    lat_far = jnp.where(even, second, first)
    here = lax.axis_index("vid")
    for video in range(lanes // depth):
        @pl.when(here == video)
        def _(video=video):
            small[at:at + length // 2, video * depth:(video + 1) * depth] = lat_far


class FilterParts:
    def __init__(self, frames, height, width, videos, near, piece, packs, blocks, lanes, chans):
        self.frames, self.pixels, self.width, self.videos, self.near = frames, height * width, width, videos, near
        self.piece, self.packs, self.blocks, self.lanes, self.chans = piece, packs, blocks, lanes, chans
        self.cols = lanes // videos
        self.per = min(videos, TAPS)
        self.banks = -(-TAPS // self.per)
        self.slots = [(row, bank) for row in range(TAPS) for bank in range(self.banks)]
        self.rows = TAPS**3 * chans // (blocks.shape[0] * near)

    def pack(self, sources):
        clear_borders(self.packs, self.width)
        lane = lax.broadcasted_iota(jnp.int32, (1, self.lanes), 1)
        turn = lax.rem(self.lanes - lax.axis_index("vid") * self.cols, self.lanes)
        for video, source in enumerate(sources):
            moved = column_shifts(pltpu.roll(source[...].astype(f32), turn, 1), self.width)
            for bank in range(self.banks):
                packed = moved[bank * self.per]
                for k in range(1, min(self.per, TAPS - bank * self.per)):
                    other = pltpu.roll(moved[bank * self.per + k], k * self.cols, 1)
                    packed = jnp.where(lane >= k * self.cols, other, packed)
                packed = packed.astype(bf16)
                for frame in range(self.frames):
                    self.packs[video, bank, frame, self.width:self.width + self.pixels] = (
                        packed[frame * self.pixels:(frame + 1) * self.pixels])

    def product(self, acts, pairs):
        def window(video, frame, row, bank):
            start = (TAPS - 1 - row) * self.width
            return self.packs[video, bank, frame, start:start + self.pixels]

        left = jnp.concatenate(
            [acts[t * self.videos + video][...] for video in range(self.videos) for t, _ in pairs], axis=1)
        right = jnp.concatenate(
            [jnp.concatenate([window(video, frame, row, bank) for row, bank in self.slots], axis=1)
             for video in range(self.videos) for _, frame in pairs], axis=0)
        return dot(left, right, ROWS_COLS)

    def put(self, step, result, base=None):
        for place, (row, bank) in enumerate(self.slots):
            tile = None if result is None else result[:, place * self.lanes:(place + 1) * self.lanes]
            for k in range(min(self.per, TAPS - bank * self.per)):
                tap = (step * TAPS + row) * TAPS + bank * self.per + k
                done = 0
                while done < self.chans:
                    index = tap * self.chans + done
                    owner, inside = index // self.rows, index % self.rows
                    part, at = inside // self.piece, inside % self.piece
                    length = min(self.chans - done, self.rows - inside, self.piece - at)
                    low, high = part * self.cols, (part + 1) * self.cols
                    dest = (owner // self.near, owner % self.near, slice(at, at + length), slice(low, high))
                    terms = [] if base is None else [base[dest]]
                    if tile is not None:
                        value = tile[done:done + length]
                        turn = (part - k) * self.cols % self.lanes
                        if turn:
                            value = pltpu.roll(value, turn, 1)
                        terms.append(value[:, low:high])
                    self.blocks[dest] = sum(terms[1:], terms[0]) if terms else jnp.zeros((length, self.cols), f32)
                    done += length


def filter_own_body(frames, height, width, videos, near, piece, *refs):
    acts, refs = refs[:frames * videos], refs[frames * videos:]
    grads, (_, blocks, packs) = refs[:videos], refs[videos:]
    parts = FilterParts(frames, height, width, videos, near, piece, packs, blocks, grads[0].shape[1], acts[0].shape[0])
    parts.pack(grads)
    far, lanes = blocks.shape[0], blocks.shape[3]
    first = lax.axis_index("ctx") == 0
    if piece * videos > parts.rows:
        blocks[:, :, piece - TILE:] = jnp.zeros((far, near, TILE, lanes), f32)
    for step in range(TAPS):
        pairs = [(t, t + TAPS - 1 - step) for t in range(frames) if t + TAPS - 1 - step < frames]
        parts.put(step, parts.product(acts, pairs) if pairs else None)
        if step < TAPS - 1:
            @pl.when(first)
            def _(step=step):
                extra = [parts.product(acts, [(0, frame)]) for frame in range(TAPS - 1 - step)]
                parts.put(step, functools.reduce(lambda a, b: a + b, extra), blocks)


def put_pair(ref, at, value):
    top, rest = halves(value)
    ref[at:at + value.shape[0]] = top
    ref[at + value.shape[0]:at + 2 * value.shape[0]] = rest


def take_pair(ref, at, length):
    return ref[at:at + length].astype(f32) + ref[at + length:at + 2 * length].astype(f32)


def filter_grad_body(frames, height, width, videos, near, piece, *refs):
    acts, refs = refs[:frames * videos], refs[frames * videos:]
    beyond, refs = refs[:videos], refs[videos:]
    smalls, base, refs = refs[:videos], refs[videos], refs[videos + 1:]
    own_far, own_line, small_out, line_send, *sends, packs, blocks = refs
    parts = FilterParts(frames, height, width, videos, near, piece, packs, blocks, beyond[0].shape[1], acts[0].shape[0])
    parts.pack(beyond)
    far, lanes = blocks.shape[0], blocks.shape[3]
    if piece * videos > parts.rows:
        blocks[:, :, piece - TILE:] = jnp.zeros((far, near, TILE, lanes), f32)
    for step in range(TAPS):
        pairs = [(t, t + TAPS - 1 - step - frames) for t in range(frames) if t + TAPS - 1 - step >= frames]
        parts.put(step, parts.product(acts, pairs) if pairs else None, base)
    device = lax.axis_index("ctx")
    line, place = device // near, device % near
    small = functools.reduce(lambda a, b: a + b, [ref[...] for ref in smalls])
    small_out[...] = small
    own_line[...] = blocks[line]
    for k in range(near):
        line_send[k * piece:(k + 1) * piece] = blocks[line ^ 1, k].astype(bf16)
    for k in range(far - 2):
        own_far[k] = blocks[line ^ (k + 2), place]
    for turn, send in enumerate(sends, 1):
        for k in range(far - 2):
            send[k * piece:(k + 1) * piece] = blocks[line ^ (k + 2), place ^ turn].astype(bf16)
        put_pair(send, (far - 2) * piece, small)


def first_sum_body(near, far, entries, *refs):
    own_far, own_line, small, line_got, refs = *refs[:4], refs[4:]
    plane_got, refs = refs[:near - 1][::-1], refs[near - 1:]
    kept, small_out, small_send, refs = *refs[:3], refs[3:]
    plane_sends, line_sends, total = refs[:near - 1], refs[near - 1:-1], refs[-1]
    piece = own_line.shape[1]
    count = small.shape[0]
    place = lax.axis_index("ctx") % near
    got = [take_pair(ref, (far - 2) * piece, count) for ref in plane_got]
    row = lax.broadcasted_iota(jnp.int32, small.shape, 0)
    summed = jnp.where(row < entries, functools.reduce(lambda a, b: a + b, got, small[...]), got[0])
    small_out[...] = summed
    put_pair(small_send, 0, summed)
    for k, send in enumerate(line_sends):
        send[0:piece] = functools.reduce(
            lambda a, b: a + b[k * piece:(k + 1) * piece].astype(f32), plane_got, own_far[k]).astype(bf16)
        put_pair(send, piece, summed)
    for k in range(near):
        total[k] = own_line[k] + line_got[k * piece:(k + 1) * piece].astype(f32)
    kept[...] = total[place]
    for turn, send in enumerate(plane_sends, 1):
        send[...] = total[place ^ turn].astype(bf16)


def last_sum_body(near, far, entries, *refs):
    kept, small, small_got, lat_own, refs = *refs[:4], refs[4:]
    line_got, plane_got, refs = refs[:far - 2], refs[far - 2:near + far - 3], refs[near + far - 3:]
    filter_grad, mod_grads, vector_grads, latent_grad = refs
    piece, lanes = kept.shape
    count = small.shape[0]
    total = functools.reduce(lambda a, b: a + b[0:piece].astype(f32), line_got + plane_got, kept[...])
    cols, rows = filter_grad.shape
    turned = total.T
    for part in range(lanes // cols):
        first, last = part * piece, min(rows, (part + 1) * piece)
        if first < last:
            filter_grad[:, first:last] = turned[part * cols:(part + 1) * cols, :last - first]
    got = [take_pair(ref, piece, count) for ref in line_got] + [take_pair(small_got, 0, count)]
    summed = functools.reduce(lambda a, b: a + b, got, small[...])
    split, length = mod_grads.shape[0], mod_grads.shape[0] + vector_grads.shape[0]
    for k in range(mod_grads.shape[1] // lanes):
        mod_grads[:, k * lanes:(k + 1) * lanes] = summed[k * length:k * length + split]
        vector_grads[:, k * lanes:(k + 1) * lanes] = summed[k * length + split:(k + 1) * length]
    cells, depth = lat_own.shape
    here = lax.axis_index("vid")
    for video in range(lanes // depth):
        @pl.when(here == video)
        def _(video=video):
            latent_grad[...] = lat_own[...] + small[entries:entries + cells, video * depth:(video + 1) * depth]


def local(features, grad_out, mean, rstd, latent, gamma, beta, ws, bs, wt, bt, kernel):
    _, frames, height, width, chans = features.shape
    outs = grad_out.shape[-1]
    depth, length = latent.shape[2:]
    count, videos = lax.axis_size("ctx"), lax.axis_size("vid")
    near = math.gcd(count, NEAR)
    far = count // near
    pixels = height * width
    size = frames * pixels
    rows, cols = TAPS**3 * chans // count, outs // videos
    piece = -(-rows // (TILE * videos)) * TILE
    gamma, beta, bs, bt = (value.reshape(1, chans) for value in (gamma, beta, bs, bt))
    feats = features.reshape(size, chans)
    grads = grad_out.reshape(size, outs)

    def along_ctx(value, target):
        return lax.ppermute(value, "ctx", [(s, target(s)) for s in range(count)])

    def others(value):
        return [value] + [
            lax.ppermute(value, "vid", [(s, (s + turn) % videos) for s in range(videos)])
            for turn in range(1, videos)]

    def plane_got(values):
        got = {turn: along_ctx(values[turn - 1], lambda s: s ^ turn) for turn in range(near - 1, 0, -1)}
        return [got[turn] for turn in range(1, near)]

    def line_got(values, first):
        turns = range(first, first + len(values))
        got = {turn: along_ctx(values[turn - first], lambda s: s ^ (turn * near)) for turn in reversed(turns)}
        return [got[turn] for turn in turns]

    beyond = lax.ppermute(grads, "ctx", [(s, s - 1) for s in range(1, count)])
    shifts = pltpu.VMEM((TAPS, frames, (height + 2) * width, outs), bf16)
    *acts, slope, normed, gain, tab, partial, latent, gamma, beta, ws, wt, grads_near, kernel = call(
        functools.partial(modulate_body, frames, height, width),
        [shaped((chans, pixels), bf16)] * frames
        + [shaped((size, chans)), shaped((size, chans)), shaped((pixels, chans)),
         shaped((length, chans)), shaped((size, chans))],
        (shifts,),
        name="modulate",
        far_args=tuple(range(12)),
        keep=(3, 4, 5, 6, 8, 10, 11),
    )(feats, mean, rstd, latent, gamma, beta, ws, bs, wt, bt, grads, kernel)
    acts_all = [value for act in acts for value in others(act)]
    grads_all = others(grads_near)
    beyond_all = others(beyond)
    cells = length // 2
    entries = (2 * depth + 4) * (chans // outs)
    count_small = -(-(entries + cells) // TILE) * TILE
    feats_grad, small, lat_own = call(
        functools.partial(input_grad_body, frames, height, width),
        (shaped((size, chans), bf16), shaped((count_small, outs)), shaped((cells, depth))),
        (shifts, pltpu.VMEM((size, chans), f32)),
        name="input_grad",
    )(beyond, kernel, partial, slope, normed, gain, tab, latent, ws, wt, gamma, beta)
    smalls = others(small)
    banks = -(-TAPS // min(videos, TAPS))
    packs = pltpu.VMEM((videos, banks, frames, (height + 2) * width, outs), bf16)
    blocks, = call(
        functools.partial(filter_own_body, frames, height, width, videos, near, piece),
        (shaped((far, near, piece, outs)),),
        (packs,),
        name="filter_own",
    )(*acts_all, *grads_all, lat_own)
    own_far, own_line, small, line_send, *plane_sends = call(
        functools.partial(filter_grad_body, frames, height, width, videos, near, piece),
        [shaped((far - 2, piece, outs)), shaped((near, piece, outs)),
         shaped((count_small, outs)), shaped((near * piece, outs), bf16)]
        + [shaped(((far - 2) * piece + 2 * count_small, outs), bf16)] * (near - 1),
        (packs, pltpu.VMEM(blocks.shape, f32)),
        name="filter_grad",
    )(*acts_all, *beyond_all, *smalls, blocks)
    line_in = line_got([line_send], 1)
    plane_in = plane_got(plane_sends)
    kept, small, small_send, *sends = call(
        functools.partial(first_sum_body, near, far, entries),
        [shaped((piece, outs)), shaped((count_small, outs)), shaped((2 * count_small, outs), bf16)]
        + [shaped((piece, outs), bf16)] * (near - 1) + [shaped((piece + 2 * count_small, outs), bf16)] * (far - 2),
        (pltpu.VMEM((near, piece, outs), f32),),
        name="first_sum",
    )(own_far, own_line, small, *line_in, *plane_in[::-1])
    line_in = line_got(sends[near - 1:], 2)
    plane_in = plane_got(sends[:near - 1])
    filter_grad, mod_grads, vector_grads, latent_grad = call(
        functools.partial(last_sum_body, near, far, entries),
        (shaped((cols, rows)), shaped((2 * depth, chans)), shaped((4, chans)), shaped((cells, depth))),
        name="last_sum",
    )(kept, small, *line_got([small_send], 1), lat_own, *line_in[::-1], *plane_in[::-1])
    return (
        feats_grad.reshape(features.shape),
        filter_grad.T,
        mod_grads.reshape(2, depth, chans),
        vector_grads,
        latent_grad.T[None, None],
    )


def solution(mesh):
    split = P("vid", "ctx", None, None, None)
    return jax.shard_map(
        local,
        mesh=mesh,
        in_specs=(split, split, P("vid", None), P("vid", None), P("vid", None, None, None)) + (P(),) * 7,
        out_specs=(split, P("ctx", "vid"), P(), P(), P("vid", "ctx", None, None)),
        check_vma=False,
    )
```

```python
import functools
import math

import jax
import jax.numpy as jnp
from jax import lax
from jax.experimental import pallas as pl
from jax.experimental.pallas import tpu as pltpu
from jax.sharding import PartitionSpec as P

NEAR = 4
CELL = 4
TAPS = 3
TILE = 16

f32 = jnp.float32
bf16 = jnp.bfloat16
dot = functools.partial(lax.dot_general, preferred_element_type=f32)
exact = functools.partial(dot, precision=lax.Precision.HIGHEST)
ROWS_COLS = (((1,), (0,)), ((), ()))
ROWS_ROWS = (((1,), (1,)), ((), ()))
COLS_COLS = (((0,), (0,)), ((), ()))


def call(body, outs, scratch=(), name=None, far_args=(), keep=(), work=1000):
    outs = list(outs)
    lost = [k for k in far_args if k not in keep]

    def run(*args):
        args = [pltpu.with_memory_space_constraint(arg, pltpu.HBM) if k in far_args else arg
                for k, arg in enumerate(args)]

        def full(*refs):
            refs = list(refs)
            sems = refs.pop()
            buffers = {k: refs.pop() for k in lost[::-1]}
            first = len(args) + len(outs)
            buffers.update({k: refs.pop(first) for k in keep})
            moves = [pltpu.make_async_copy(refs[k], buffers[k], sems.at[at]) for at, k in enumerate(far_args)]
            for move in moves:
                move.start()
            for k in far_args:
                refs[k] = buffers[k]
            for move in moves:
                move.wait()
            body(*refs)

        return pl.pallas_call(
            full if far_args else body,
            out_shape=outs + [shaped(args[k].shape, args[k].dtype) for k in keep],
            in_specs=[pl.BlockSpec(memory_space=pltpu.HBM if k in far_args else pltpu.VMEM) for k in range(len(args))],
            scratch_shapes=list(scratch) + [pltpu.VMEM(args[k].shape, args[k].dtype) for k in lost]
            + ([pltpu.SemaphoreType.DMA((len(far_args),))] if far_args else []),
            name=name,
            cost_estimate=pl.CostEstimate(flops=work, bytes_accessed=work, transcendentals=0),
            compiler_params=pltpu.CompilerParams(vmem_limit_bytes=28 * 2**20),
        )(*args)

    return run


def shaped(shape, kind=f32):
    return jax.ShapeDtypeStruct(shape, kind)


def cell_matrix(height, width, cells):
    pixel = lax.broadcasted_iota(jnp.int32, (height * width, cells), 0)
    cell = lax.broadcasted_iota(jnp.int32, (height * width, cells), 1)
    place = (pixel // width) // CELL * (width // CELL) + pixel % width // CELL
    return jnp.where(place == cell, 1.0, 0.0).astype(f32)


def modulate_body(frames, height, width, feats, mean, rstd, latent, gamma, beta, ws, bs, wt, bt, grads, weights, *refs):
    acts, (slope, normed_out, gain_out, tab_out, partial, shifted) = refs[:frames], refs[frames:]
    chans = feats.shape[1]
    groups = mean.shape[1]
    pixels = height * width
    lat = latent[0, lax.axis_index("ctx") * frames // CELL]
    group = lax.broadcasted_iota(jnp.int32, (groups, chans), 0)
    chan = lax.broadcasted_iota(jnp.int32, (groups, chans), 1)
    member = jnp.where(chan // (chans // groups) == group, 1.0, 0.0).astype(f32)
    mean_chan = exact(mean[...], member, ROWS_COLS)
    rstd_chan = exact(rstd[...], member, ROWS_COLS)
    scale_tab = exact(lat, ws[...], COLS_COLS) + bs[...]
    shift_tab = exact(lat, wt[...], COLS_COLS) + bt[...]
    tab_out[...] = scale_tab
    cells = cell_matrix(height, width, lat.shape[1])
    scale_map = exact(cells, scale_tab, ROWS_COLS)
    shift_map = exact(cells, shift_tab, ROWS_COLS)
    gain_out[...] = scale_map * (gamma[...] * rstd_chan)
    for frame in range(frames):
        at = pl.ds(frame * pixels, pixels)
        normed = (feats[at, :].astype(f32) - mean_chan) * rstd_chan
        modulated = (normed * gamma[...] + beta[...]) * scale_map + shift_map
        squashed = jax.nn.sigmoid(modulated)
        normed_out[at, :] = normed
        slope[at, :] = squashed * (1.0 + modulated * (1.0 - squashed))
        acts[frame][...] = (modulated * squashed).T.astype(bf16)
    conv_own_body(frames, height, width, grads, weights, partial, shifted)


def column_shifts(value, width):
    column = lax.broadcasted_iota(jnp.int32, value.shape, 0) % width
    rows = value.shape[0]
    return (
        jnp.where(column == width - 1, 0.0, pltpu.roll(value, rows - 1, 0)),
        value,
        jnp.where(column == 0, 0.0, pltpu.roll(value, 1, 0)),
    )


def clear_borders(padded, width):
    lead = padded.shape[:-2]
    length, lanes = padded.shape[-2:]
    edge = jnp.zeros(lead + (width, lanes), padded.dtype)
    every = (slice(None),) * len(lead)
    padded[every + (slice(0, width),)] = edge
    padded[every + (slice(length - width, length),)] = edge


def put_shifts(shifted, source, frames, pixels, width):
    clear_borders(shifted, width)
    for col, value in enumerate(column_shifts(source[...].astype(f32), width)):
        for frame in range(frames):
            shifted[col, frame, width:width + pixels] = value[frame * pixels:(frame + 1) * pixels].astype(bf16)


def taps_of(weights, step, chans):
    return jnp.concatenate(
        [weights[(step * TAPS * TAPS + k) * chans:(step * TAPS * TAPS + k + 1) * chans, :]
         for k in range(TAPS * TAPS)], axis=1)


def shifted_rows(shifted, frame_list, pixels, width):
    def window(frame, row, col):
        start = (TAPS - 1 - row) * width
        return shifted[col, frame, start:start + pixels]

    return jnp.concatenate(
        [jnp.concatenate([window(frame, k // TAPS, k % TAPS) for k in range(TAPS * TAPS)], axis=1)
         for frame in frame_list], axis=0)


def add_rows(total, term, first):
    if first == 0 and term.shape[0] == total.shape[0]:
        total[...] += term
    else:
        total[first:first + term.shape[0]] += term


def conv_own_body(frames, height, width, grads, weights, total, shifted):
    pixels = height * width
    chans = total.shape[1]
    put_shifts(shifted, grads, frames, pixels, width)
    total[...] = jnp.zeros_like(total)
    for step in range(TAPS):
        pairs = [(t, t + TAPS - 1 - step) for t in range(frames) if t + TAPS - 1 - step < frames]
        if pairs:
            rows = shifted_rows(shifted, [frame for _, frame in pairs], pixels, width)
            add_rows(total, dot(rows, taps_of(weights, step, chans), ROWS_ROWS), pairs[0][0] * pixels)

    @pl.when(lax.axis_index("ctx") == 0)
    def _():
        for step in range(TAPS - 1):
            for frame in range(TAPS - 1 - step):
                rows = shifted_rows(shifted, [frame], pixels, width)
                add_rows(total, dot(rows, taps_of(weights, step, chans), ROWS_ROWS), 0)


def input_grad_body(frames, height, width, beyond, weights, partial, slope, normed, gain, tab, latent,
                    ws, wt, gamma, beta, feats_grad, small, lat_own, shifted, total):
    pixels = height * width
    chans = gain.shape[1]
    device = lax.axis_index("ctx")
    put_shifts(shifted, beyond, frames, pixels, width)
    total[...] = partial[...]
    for step in range(TAPS):
        pairs = [(t, t + TAPS - 1 - step - frames) for t in range(frames) if t + TAPS - 1 - step >= frames]
        if pairs:
            rows = shifted_rows(shifted, [frame for _, frame in pairs], pixels, width)
            add_rows(total, dot(rows, taps_of(weights, step, chans), ROWS_ROWS), pairs[0][0] * pixels)

    pooled_shift = jnp.zeros((pixels, chans), f32)
    pooled_norm = jnp.zeros((pixels, chans), f32)
    for frame in range(frames):
        at = pl.ds(frame * pixels, pixels)
        pre = total[at, :] * slope[at, :]
        feats_grad[at, :] = (pre * gain[...]).astype(bf16)
        pooled_shift += pre
        pooled_norm += pre * normed[at, :]
    lat = latent[0, device * frames // CELL]
    depth, length = lat.shape
    cells = cell_matrix(height, width, length)
    shift_pool = exact(cells, pooled_shift, COLS_COLS)
    norm_pool = exact(cells, pooled_norm, COLS_COLS)
    scale_pool = norm_pool * gamma[...] + shift_pool * beta[...]
    parts = [exact(lat, scale_pool, ROWS_COLS), exact(lat, shift_pool, ROWS_COLS)]
    for field in (norm_pool * tab[...], shift_pool * tab[...], scale_pool, shift_pool):
        parts.append(jnp.sum(field, axis=0, keepdims=True))
    lanes = small.shape[1]
    small[small.shape[0] - TILE:] = jnp.zeros((TILE, lanes), f32)
    at = 0
    for k in range(chans // lanes):
        for part in parts:
            small[at:at + part.shape[0]] = part[:, k * lanes:(k + 1) * lanes]
            at += part.shape[0]
    latent_sum = exact(scale_pool, ws[...], ROWS_ROWS) + exact(shift_pool, wt[...], ROWS_ROWS)
    first, second = latent_sum[:length // 2], latent_sum[length // 2:]
    even = device % 2 == 0
    lat_own[...] = jnp.where(even, first, second)
    lat_far = jnp.where(even, second, first)
    here = lax.axis_index("vid")
    for video in range(lanes // depth):
        @pl.when(here == video)
        def _(video=video):
            small[at:at + length // 2, video * depth:(video + 1) * depth] = lat_far


class FilterParts:
    def __init__(self, frames, height, width, videos, near, piece, packs, blocks, lanes, chans):
        self.frames, self.pixels, self.width, self.videos, self.near = frames, height * width, width, videos, near
        self.piece, self.packs, self.blocks, self.lanes, self.chans = piece, packs, blocks, lanes, chans
        self.cols = lanes // videos
        self.per = min(videos, TAPS)
        self.banks = -(-TAPS // self.per)
        self.slots = [(row, bank) for row in range(TAPS) for bank in range(self.banks)]
        self.rows = TAPS**3 * chans // (blocks.shape[0] * near)

    def pack(self, sources):
        clear_borders(self.packs, self.width)
        lane = lax.broadcasted_iota(jnp.int32, (1, self.lanes), 1)
        turn = lax.rem(self.lanes - lax.axis_index("vid") * self.cols, self.lanes)
        for video, source in enumerate(sources):
            moved = column_shifts(pltpu.roll(source[...].astype(f32), turn, 1), self.width)
            for bank in range(self.banks):
                packed = moved[bank * self.per]
                for k in range(1, min(self.per, TAPS - bank * self.per)):
                    other = pltpu.roll(moved[bank * self.per + k], k * self.cols, 1)
                    packed = jnp.where(lane >= k * self.cols, other, packed)
                packed = packed.astype(bf16)
                for frame in range(self.frames):
                    self.packs[video, bank, frame, self.width:self.width + self.pixels] = (
                        packed[frame * self.pixels:(frame + 1) * self.pixels])

    def product(self, acts, pairs):
        def window(video, frame, row, bank):
            start = (TAPS - 1 - row) * self.width
            return self.packs[video, bank, frame, start:start + self.pixels]

        left = jnp.concatenate(
            [acts[t * self.videos + video][...] for video in range(self.videos) for t, _ in pairs], axis=1)
        right = jnp.concatenate(
            [jnp.concatenate([window(video, frame, row, bank) for row, bank in self.slots], axis=1)
             for video in range(self.videos) for _, frame in pairs], axis=0)
        return dot(left, right, ROWS_COLS)

    def put(self, step, result, base=None):
        for place, (row, bank) in enumerate(self.slots):
            tile = None if result is None else result[:, place * self.lanes:(place + 1) * self.lanes]
            for k in range(min(self.per, TAPS - bank * self.per)):
                tap = (step * TAPS + row) * TAPS + bank * self.per + k
                done = 0
                while done < self.chans:
                    index = tap * self.chans + done
                    owner, inside = index // self.rows, index % self.rows
                    part, at = inside // self.piece, inside % self.piece
                    length = min(self.chans - done, self.rows - inside, self.piece - at)
                    low, high = part * self.cols, (part + 1) * self.cols
                    dest = (owner // self.near, owner % self.near, slice(at, at + length), slice(low, high))
                    terms = [] if base is None else [base[dest]]
                    if tile is not None:
                        value = tile[done:done + length]
                        turn = (part - k) * self.cols % self.lanes
                        if turn:
                            value = pltpu.roll(value, turn, 1)
                        terms.append(value[:, low:high])
                    self.blocks[dest] = sum(terms[1:], terms[0]) if terms else jnp.zeros((length, self.cols), f32)
                    done += length


def filter_own_body(frames, height, width, videos, near, piece, *refs):
    acts, refs = refs[:frames * videos], refs[frames * videos:]
    grads, (_, blocks, packs) = refs[:videos], refs[videos:]
    parts = FilterParts(frames, height, width, videos, near, piece, packs, blocks, grads[0].shape[1], acts[0].shape[0])
    parts.pack(grads)
    far, lanes = blocks.shape[0], blocks.shape[3]
    first = lax.axis_index("ctx") == 0
    if piece * videos > parts.rows:
        blocks[:, :, piece - TILE:] = jnp.zeros((far, near, TILE, lanes), f32)
    for step in range(TAPS):
        pairs = [(t, t + TAPS - 1 - step) for t in range(frames) if t + TAPS - 1 - step < frames]
        parts.put(step, parts.product(acts, pairs) if pairs else None)
        if step < TAPS - 1:
            @pl.when(first)
            def _(step=step):
                extra = [parts.product(acts, [(0, frame)]) for frame in range(TAPS - 1 - step)]
                parts.put(step, functools.reduce(lambda a, b: a + b, extra), blocks)


def filter_grad_body(frames, height, width, videos, near, piece, *refs):
    acts, refs = refs[:frames * videos], refs[frames * videos:]
    beyond, refs = refs[:videos], refs[videos:]
    smalls, base, refs = refs[:videos], refs[videos], refs[videos + 1:]
    own_far, own_line, small_out, line_send, *sends, packs, blocks = refs
    parts = FilterParts(frames, height, width, videos, near, piece, packs, blocks, beyond[0].shape[1], acts[0].shape[0])
    parts.pack(beyond)
    far, lanes = blocks.shape[0], blocks.shape[3]
    if piece * videos > parts.rows:
        blocks[:, :, piece - TILE:] = jnp.zeros((far, near, TILE, lanes), f32)
    for step in range(TAPS):
        pairs = [(t, t + TAPS - 1 - step - frames) for t in range(frames) if t + TAPS - 1 - step >= frames]
        parts.put(step, parts.product(acts, pairs) if pairs else None, base)
    device = lax.axis_index("ctx")
    line, place = device // near, device % near
    small = functools.reduce(lambda a, b: a + b, [ref[...] for ref in smalls])
    small_out[...] = small
    own_line[...] = blocks[line]
    for k in range(near):
        line_send[k * piece:(k + 1) * piece] = blocks[line ^ 1, k].astype(bf16)
    line_send[near * piece:near * piece + small.shape[0]] = small.astype(bf16)
    for k in range(far - 2):
        own_far[k] = blocks[line ^ (k + 2), place]
    for turn, send in enumerate(sends, 1):
        for k in range(far - 2):
            send[k * piece:(k + 1) * piece] = blocks[line ^ (k + 2), place ^ turn].astype(bf16)
        send[(far - 2) * piece:(far - 2) * piece + small.shape[0]] = small.astype(bf16)


def first_sum_body(near, far, entries, *refs):
    own_far, own_line, small, line_got, refs = *refs[:4], refs[4:]
    plane_got, refs = refs[:near - 1][::-1], refs[near - 1:]
    kept, small_out, refs = *refs[:2], refs[2:]
    plane_sends, line_sends, total = refs[:near - 1], refs[near - 1:-1], refs[-1]
    piece = own_line.shape[1]
    count = small.shape[0]
    place = lax.axis_index("ctx") % near
    got = [ref[(far - 2) * piece:(far - 2) * piece + count].astype(f32) for ref in plane_got]
    row = lax.broadcasted_iota(jnp.int32, small.shape, 0)
    summed = jnp.where(row < entries, functools.reduce(lambda a, b: a + b, got, small[...]), got[0])
    next_line = line_got[near * piece:near * piece + count]
    small_out[...] = jnp.where(row < entries, summed + next_line.astype(f32), summed)
    for k, send in enumerate(line_sends):
        send[0:piece] = functools.reduce(
            lambda a, b: a + b[k * piece:(k + 1) * piece].astype(f32), plane_got, own_far[k]).astype(bf16)
        send[piece:piece + count] = summed.astype(bf16)
    for k in range(near):
        total[k] = own_line[k] + line_got[k * piece:(k + 1) * piece].astype(f32)
    kept[...] = total[place]
    for turn, send in enumerate(plane_sends, 1):
        send[0:piece] = total[place ^ turn].astype(bf16)
        send[piece:piece + count] = next_line


def last_sum_body(near, far, entries, *refs):
    kept, small, lat_own, refs = *refs[:3], refs[3:]
    line_got, plane_got, refs = refs[:far - 2], refs[far - 2:near + far - 3], refs[near + far - 3:]
    filter_grad, mod_grads, vector_grads, latent_grad = refs
    piece, lanes = kept.shape
    count = small.shape[0]
    total = functools.reduce(lambda a, b: a + b[0:piece].astype(f32), line_got + plane_got, kept[...])
    cols, rows = filter_grad.shape
    turned = total.T
    for part in range(lanes // cols):
        first, last = part * piece, min(rows, (part + 1) * piece)
        if first < last:
            filter_grad[:, first:last] = turned[part * cols:(part + 1) * cols, :last - first]
    got = [ref[piece:piece + count].astype(f32) for ref in line_got + plane_got]
    summed = functools.reduce(lambda a, b: a + b, got, small[...])
    split, length = mod_grads.shape[0], mod_grads.shape[0] + vector_grads.shape[0]
    for k in range(mod_grads.shape[1] // lanes):
        mod_grads[:, k * lanes:(k + 1) * lanes] = summed[k * length:k * length + split]
        vector_grads[:, k * lanes:(k + 1) * lanes] = summed[k * length + split:(k + 1) * length]
    cells, depth = lat_own.shape
    here = lax.axis_index("vid")
    for video in range(lanes // depth):
        @pl.when(here == video)
        def _(video=video):
            latent_grad[...] = lat_own[...] + small[entries:entries + cells, video * depth:(video + 1) * depth]


def local(features, grad_out, mean, rstd, latent, gamma, beta, ws, bs, wt, bt, kernel):
    _, frames, height, width, chans = features.shape
    outs = grad_out.shape[-1]
    depth, length = latent.shape[2:]
    count, videos = lax.axis_size("ctx"), lax.axis_size("vid")
    near = math.gcd(count, NEAR)
    far = count // near
    pixels = height * width
    size = frames * pixels
    rows, cols = TAPS**3 * chans // count, outs // videos
    piece = -(-rows // (TILE * videos)) * TILE
    gamma, beta, bs, bt = (value.reshape(1, chans) for value in (gamma, beta, bs, bt))
    feats = features.reshape(size, chans)
    grads = grad_out.reshape(size, outs)

    def along_ctx(value, target):
        return lax.ppermute(value, "ctx", [(s, target(s)) for s in range(count)])

    def others(value):
        return [value] + [
            lax.ppermute(value, "vid", [(s, (s + turn) % videos) for s in range(videos)])
            for turn in range(1, videos)]

    def plane_got(values):
        got = {turn: along_ctx(values[turn - 1], lambda s: s ^ turn) for turn in range(near - 1, 0, -1)}
        return [got[turn] for turn in range(1, near)]

    def line_got(values, first):
        turns = range(first, first + len(values))
        got = {turn: along_ctx(values[turn - first], lambda s: s ^ (turn * near)) for turn in reversed(turns)}
        return [got[turn] for turn in turns]

    beyond = lax.ppermute(grads, "ctx", [(s, s - 1) for s in range(1, count)])
    shifts = pltpu.VMEM((TAPS, frames, (height + 2) * width, outs), bf16)
    *acts, slope, normed, gain, tab, partial, latent, gamma, beta, ws, wt, grads_near, kernel = call(
        functools.partial(modulate_body, frames, height, width),
        [shaped((chans, pixels), bf16)] * frames
        + [shaped((size, chans)), shaped((size, chans)), shaped((pixels, chans)),
         shaped((length, chans)), shaped((size, chans))],
        (shifts,),
        name="modulate",
        far_args=tuple(range(12)),
        keep=(3, 4, 5, 6, 8, 10, 11),
    )(feats, mean, rstd, latent, gamma, beta, ws, bs, wt, bt, grads, kernel)
    acts_all = [value for act in acts for value in others(act)]
    grads_all = others(grads_near)
    beyond_all = others(beyond)
    cells = length // 2
    entries = (2 * depth + 4) * (chans // outs)
    count_small = -(-(entries + cells) // TILE) * TILE
    feats_grad, small, lat_own = call(
        functools.partial(input_grad_body, frames, height, width),
        (shaped((size, chans), bf16), shaped((count_small, outs)), shaped((cells, depth))),
        (shifts, pltpu.VMEM((size, chans), f32)),
        name="input_grad",
    )(beyond, kernel, partial, slope, normed, gain, tab, latent, ws, wt, gamma, beta)
    smalls = others(small)
    banks = -(-TAPS // min(videos, TAPS))
    packs = pltpu.VMEM((videos, banks, frames, (height + 2) * width, outs), bf16)
    blocks, = call(
        functools.partial(filter_own_body, frames, height, width, videos, near, piece),
        (shaped((far, near, piece, outs)),),
        (packs,),
        name="filter_own",
    )(*acts_all, *grads_all, lat_own)
    own_far, own_line, small, line_send, *plane_sends = call(
        functools.partial(filter_grad_body, frames, height, width, videos, near, piece),
        [shaped((far - 2, piece, outs)), shaped((near, piece, outs)),
         shaped((count_small, outs)), shaped((near * piece + count_small, outs), bf16)]
        + [shaped(((far - 2) * piece + count_small, outs), bf16)] * (near - 1),
        (packs, pltpu.VMEM(blocks.shape, f32)),
        name="filter_grad",
    )(*acts_all, *beyond_all, *smalls, blocks)
    line_in = line_got([line_send], 1)
    plane_in = plane_got(plane_sends)
    kept, small, *sends = call(
        functools.partial(first_sum_body, near, far, entries),
        [shaped((piece, outs)), shaped((count_small, outs))]
        + [shaped((piece + count_small, outs), bf16)] * (near + far - 3),
        (pltpu.VMEM((near, piece, outs), f32),),
        name="first_sum",
    )(own_far, own_line, small, *line_in, *plane_in[::-1])
    line_in = line_got(sends[near - 1:], 2)
    plane_in = plane_got(sends[:near - 1])
    filter_grad, mod_grads, vector_grads, latent_grad = call(
        functools.partial(last_sum_body, near, far, entries),
        (shaped((cols, rows)), shaped((2 * depth, chans)), shaped((4, chans)), shaped((cells, depth))),
        name="last_sum",
    )(kept, small, lat_own, *line_in[::-1], *plane_in[::-1])
    return (
        feats_grad.reshape(features.shape),
        filter_grad.T,
        mod_grads.reshape(2, depth, chans),
        vector_grads,
        latent_grad.T[None, None],
    )


def solution(mesh):
    split = P("vid", "ctx", None, None, None)
    return jax.shard_map(
        local,
        mesh=mesh,
        in_specs=(split, split, P("vid", None), P("vid", None), P("vid", None, None, None)) + (P(),) * 7,
        out_specs=(split, P("ctx", "vid"), P(), P(), P("vid", "ctx", None, None)),
        check_vma=False,
    )
```

```python
import functools
import math

import jax
import jax.numpy as jnp
from jax import lax
from jax.experimental import pallas as pl
from jax.experimental.pallas import tpu as pltpu
from jax.sharding import PartitionSpec as P

NEAR = 4
CELL = 4
TAPS = 3
TILE = 16

f32 = jnp.float32
bf16 = jnp.bfloat16
dot = functools.partial(lax.dot_general, preferred_element_type=f32)
exact = functools.partial(dot, precision=lax.Precision.HIGHEST)
ROWS_COLS = (((1,), (0,)), ((), ()))
ROWS_ROWS = (((1,), (1,)), ((), ()))
COLS_COLS = (((0,), (0,)), ((), ()))


def call(body, outs, scratch=(), name=None, far_args=(), keep=(), work=1000):
    outs = list(outs)
    lost = [k for k in far_args if k not in keep]

    def run(*args):
        args = [pltpu.with_memory_space_constraint(arg, pltpu.HBM) if k in far_args else arg
                for k, arg in enumerate(args)]

        def full(*refs):
            refs = list(refs)
            sems = refs.pop()
            buffers = {k: refs.pop() for k in lost[::-1]}
            first = len(args) + len(outs)
            buffers.update({k: refs.pop(first) for k in keep})
            moves = [pltpu.make_async_copy(refs[k], buffers[k], sems.at[at]) for at, k in enumerate(far_args)]
            for move in moves:
                move.start()
            for k in far_args:
                refs[k] = buffers[k]
            for move in moves:
                move.wait()
            body(*refs)

        return pl.pallas_call(
            full if far_args else body,
            out_shape=outs + [shaped(args[k].shape, args[k].dtype) for k in keep],
            in_specs=[pl.BlockSpec(memory_space=pltpu.HBM if k in far_args else pltpu.VMEM) for k in range(len(args))],
            scratch_shapes=list(scratch) + [pltpu.VMEM(args[k].shape, args[k].dtype) for k in lost]
            + ([pltpu.SemaphoreType.DMA((len(far_args),))] if far_args else []),
            name=name,
            cost_estimate=pl.CostEstimate(flops=work, bytes_accessed=work, transcendentals=0),
            compiler_params=pltpu.CompilerParams(vmem_limit_bytes=28 * 2**20),
        )(*args)

    return run


def shaped(shape, kind=f32):
    return jax.ShapeDtypeStruct(shape, kind)


def cell_matrix(height, width, cells):
    pixel = lax.broadcasted_iota(jnp.int32, (height * width, cells), 0)
    cell = lax.broadcasted_iota(jnp.int32, (height * width, cells), 1)
    place = (pixel // width) // CELL * (width // CELL) + pixel % width // CELL
    return jnp.where(place == cell, 1.0, 0.0).astype(f32)


def modulate_body(frames, height, width, feats, mean, rstd, latent, gamma, beta, ws, bs, wt, bt, grads, weights, *refs):
    acts, (slope, normed_out, gain_out, tab_out, partial, shifted) = refs[:frames], refs[frames:]
    chans = feats.shape[1]
    groups = mean.shape[1]
    pixels = height * width
    lat = latent[0, lax.axis_index("ctx") * frames // CELL]
    group = lax.broadcasted_iota(jnp.int32, (groups, chans), 0)
    chan = lax.broadcasted_iota(jnp.int32, (groups, chans), 1)
    member = jnp.where(chan // (chans // groups) == group, 1.0, 0.0).astype(f32)
    mean_chan = exact(mean[...], member, ROWS_COLS)
    rstd_chan = exact(rstd[...], member, ROWS_COLS)
    scale_tab = exact(lat, ws[...], COLS_COLS) + bs[...]
    shift_tab = exact(lat, wt[...], COLS_COLS) + bt[...]
    tab_out[...] = scale_tab
    cells = cell_matrix(height, width, lat.shape[1])
    scale_map = exact(cells, scale_tab, ROWS_COLS)
    shift_map = exact(cells, shift_tab, ROWS_COLS)
    gain_out[...] = scale_map * (gamma[...] * rstd_chan)
    for frame in range(frames):
        at = pl.ds(frame * pixels, pixels)
        normed = (feats[at, :].astype(f32) - mean_chan) * rstd_chan
        modulated = (normed * gamma[...] + beta[...]) * scale_map + shift_map
        squashed = jax.nn.sigmoid(modulated)
        normed_out[at, :] = normed
        slope[at, :] = squashed * (1.0 + modulated * (1.0 - squashed))
        acts[frame][...] = (modulated * squashed).T.astype(bf16)
    conv_own_body(frames, height, width, grads, weights, partial, shifted)


def column_shifts(value, width):
    column = lax.broadcasted_iota(jnp.int32, value.shape, 0) % width
    rows = value.shape[0]
    return (
        jnp.where(column == width - 1, 0.0, pltpu.roll(value, rows - 1, 0)),
        value,
        jnp.where(column == 0, 0.0, pltpu.roll(value, 1, 0)),
    )


def clear_borders(padded, width):
    lead = padded.shape[:-2]
    length, lanes = padded.shape[-2:]
    edge = jnp.zeros(lead + (width, lanes), padded.dtype)
    every = (slice(None),) * len(lead)
    padded[every + (slice(0, width),)] = edge
    padded[every + (slice(length - width, length),)] = edge


def put_shifts(shifted, source, frames, pixels, width):
    clear_borders(shifted, width)
    for col, value in enumerate(column_shifts(source[...].astype(f32), width)):
        for frame in range(frames):
            shifted[col, frame, width:width + pixels] = value[frame * pixels:(frame + 1) * pixels].astype(bf16)


def taps_of(weights, step, chans):
    return jnp.concatenate(
        [weights[(step * TAPS * TAPS + k) * chans:(step * TAPS * TAPS + k + 1) * chans, :]
         for k in range(TAPS * TAPS)], axis=1)


def shifted_rows(shifted, frame_list, pixels, width):
    def window(frame, row, col):
        start = (TAPS - 1 - row) * width
        return shifted[col, frame, start:start + pixels]

    return jnp.concatenate(
        [jnp.concatenate([window(frame, k // TAPS, k % TAPS) for k in range(TAPS * TAPS)], axis=1)
         for frame in frame_list], axis=0)


def add_rows(total, term, first):
    if first == 0 and term.shape[0] == total.shape[0]:
        total[...] += term
    else:
        total[first:first + term.shape[0]] += term


def conv_own_body(frames, height, width, grads, weights, total, shifted):
    pixels = height * width
    chans = total.shape[1]
    put_shifts(shifted, grads, frames, pixels, width)
    total[...] = jnp.zeros_like(total)
    for step in range(TAPS):
        pairs = [(t, t + TAPS - 1 - step) for t in range(frames) if t + TAPS - 1 - step < frames]
        if pairs:
            rows = shifted_rows(shifted, [frame for _, frame in pairs], pixels, width)
            add_rows(total, dot(rows, taps_of(weights, step, chans), ROWS_ROWS), pairs[0][0] * pixels)

    @pl.when(lax.axis_index("ctx") == 0)
    def _():
        for step in range(TAPS - 1):
            for frame in range(TAPS - 1 - step):
                rows = shifted_rows(shifted, [frame], pixels, width)
                add_rows(total, dot(rows, taps_of(weights, step, chans), ROWS_ROWS), 0)


def input_grad_body(frames, height, width, beyond, weights, partial, slope, normed, gain, tab, latent,
                    ws, wt, gamma, beta, feats_grad, small, lat_own, shifted, total):
    pixels = height * width
    chans = gain.shape[1]
    device = lax.axis_index("ctx")
    put_shifts(shifted, beyond, frames, pixels, width)
    total[...] = partial[...]
    for step in range(TAPS):
        pairs = [(t, t + TAPS - 1 - step - frames) for t in range(frames) if t + TAPS - 1 - step >= frames]
        if pairs:
            rows = shifted_rows(shifted, [frame for _, frame in pairs], pixels, width)
            add_rows(total, dot(rows, taps_of(weights, step, chans), ROWS_ROWS), pairs[0][0] * pixels)

    pooled_shift = jnp.zeros((pixels, chans), f32)
    pooled_norm = jnp.zeros((pixels, chans), f32)
    for frame in range(frames):
        at = pl.ds(frame * pixels, pixels)
        pre = total[at, :] * slope[at, :]
        feats_grad[at, :] = (pre * gain[...]).astype(bf16)
        pooled_shift += pre
        pooled_norm += pre * normed[at, :]
    lat = latent[0, device * frames // CELL]
    depth, length = lat.shape
    cells = cell_matrix(height, width, length)
    shift_pool = exact(cells, pooled_shift, COLS_COLS)
    norm_pool = exact(cells, pooled_norm, COLS_COLS)
    scale_pool = norm_pool * gamma[...] + shift_pool * beta[...]
    parts = [exact(lat, scale_pool, ROWS_COLS), exact(lat, shift_pool, ROWS_COLS)]
    for field in (norm_pool * tab[...], shift_pool * tab[...], scale_pool, shift_pool):
        parts.append(jnp.sum(field, axis=0, keepdims=True))
    lanes = small.shape[1]
    small[small.shape[0] - TILE:] = jnp.zeros((TILE, lanes), f32)
    at = 0
    for k in range(chans // lanes):
        for part in parts:
            small[at:at + part.shape[0]] = part[:, k * lanes:(k + 1) * lanes]
            at += part.shape[0]
    latent_sum = exact(scale_pool, ws[...], ROWS_ROWS) + exact(shift_pool, wt[...], ROWS_ROWS)
    first, second = latent_sum[:length // 2], latent_sum[length // 2:]
    even = device % 2 == 0
    lat_own[...] = jnp.where(even, first, second)
    lat_far = jnp.where(even, second, first)
    here = lax.axis_index("vid")
    for video in range(lax.axis_size("vid")):
        @pl.when(here == video)
        def _(video=video):
            small[at:at + length // 2, video * depth:(video + 1) * depth] = lat_far


class FilterParts:
    def __init__(self, frames, height, width, videos, near, piece, packs, blocks, lanes, chans):
        self.frames, self.pixels, self.width, self.videos, self.near = frames, height * width, width, videos, near
        self.piece, self.packs, self.blocks, self.lanes, self.chans = piece, packs, blocks, lanes, chans
        self.cols = lanes // videos
        self.per = min(videos, TAPS)
        self.banks = -(-TAPS // self.per)
        self.slots = [(row, bank) for row in range(TAPS) for bank in range(self.banks)]
        self.rows = TAPS**3 * chans // (blocks.shape[0] * near)

    def pack(self, sources):
        clear_borders(self.packs, self.width)
        lane = lax.broadcasted_iota(jnp.int32, (1, self.lanes), 1)
        turn = lax.rem(self.lanes - lax.axis_index("vid") * self.cols, self.lanes)
        for video, source in enumerate(sources):
            moved = column_shifts(pltpu.roll(source[...].astype(f32), turn, 1), self.width)
            for bank in range(self.banks):
                packed = moved[bank * self.per]
                for k in range(1, min(self.per, TAPS - bank * self.per)):
                    other = pltpu.roll(moved[bank * self.per + k], k * self.cols, 1)
                    packed = jnp.where(lane >= k * self.cols, other, packed)
                packed = packed.astype(bf16)
                for frame in range(self.frames):
                    self.packs[video, bank, frame, self.width:self.width + self.pixels] = (
                        packed[frame * self.pixels:(frame + 1) * self.pixels])

    def product(self, acts, pairs):
        def window(video, frame, row, bank):
            start = (TAPS - 1 - row) * self.width
            return self.packs[video, bank, frame, start:start + self.pixels]

        left = jnp.concatenate(
            [acts[t * self.videos + video][...] for video in range(self.videos) for t, _ in pairs], axis=1)
        right = jnp.concatenate(
            [jnp.concatenate([window(video, frame, row, bank) for row, bank in self.slots], axis=1)
             for video in range(self.videos) for _, frame in pairs], axis=0)
        return dot(left, right, ROWS_COLS)

    def put(self, step, result, base=None):
        for place, (row, bank) in enumerate(self.slots):
            tile = None if result is None else result[:, place * self.lanes:(place + 1) * self.lanes]
            for k in range(min(self.per, TAPS - bank * self.per)):
                tap = (step * TAPS + row) * TAPS + bank * self.per + k
                done = 0
                while done < self.chans:
                    index = tap * self.chans + done
                    owner, inside = index // self.rows, index % self.rows
                    part, at = inside // self.piece, inside % self.piece
                    length = min(self.chans - done, self.rows - inside, self.piece - at)
                    low, high = part * self.cols, (part + 1) * self.cols
                    dest = (owner // self.near, owner % self.near, slice(at, at + length), slice(low, high))
                    terms = [] if base is None else [base[dest]]
                    if tile is not None:
                        value = tile[done:done + length]
                        turn = (part - k) * self.cols % self.lanes
                        if turn:
                            value = pltpu.roll(value, turn, 1)
                        terms.append(value[:, low:high])
                    self.blocks[dest] = sum(terms[1:], terms[0]) if terms else jnp.zeros((length, self.cols), f32)
                    done += length


def filter_own_body(frames, height, width, videos, near, piece, *refs):
    acts, refs = refs[:frames * videos], refs[frames * videos:]
    grads, (_, blocks, packs) = refs[:videos], refs[videos:]
    parts = FilterParts(frames, height, width, videos, near, piece, packs, blocks, grads[0].shape[1], acts[0].shape[0])
    parts.pack(grads)
    far, lanes = blocks.shape[0], blocks.shape[3]
    first = lax.axis_index("ctx") == 0
    if piece * videos > parts.rows:
        blocks[:, :, piece - TILE:] = jnp.zeros((far, near, TILE, lanes), f32)
    for step in range(TAPS):
        pairs = [(t, t + TAPS - 1 - step) for t in range(frames) if t + TAPS - 1 - step < frames]
        parts.put(step, parts.product(acts, pairs) if pairs else None)
        if step < TAPS - 1:
            @pl.when(first)
            def _(step=step):
                extra = [parts.product(acts, [(0, frame)]) for frame in range(TAPS - 1 - step)]
                parts.put(step, functools.reduce(lambda a, b: a + b, extra), blocks)


def filter_grad_body(frames, height, width, videos, near, piece, *refs):
    acts, refs = refs[:frames * videos], refs[frames * videos:]
    beyond, refs = refs[:videos], refs[videos:]
    smalls, base, refs = refs[:videos], refs[videos], refs[videos + 1:]
    own_far, own_line, small_out, line_send, *sends, packs, blocks = refs
    parts = FilterParts(frames, height, width, videos, near, piece, packs, blocks, beyond[0].shape[1], acts[0].shape[0])
    parts.pack(beyond)
    far, lanes = blocks.shape[0], blocks.shape[3]
    if piece * videos > parts.rows:
        blocks[:, :, piece - TILE:] = jnp.zeros((far, near, TILE, lanes), f32)
    for step in range(TAPS):
        pairs = [(t, t + TAPS - 1 - step - frames) for t in range(frames) if t + TAPS - 1 - step >= frames]
        parts.put(step, parts.product(acts, pairs) if pairs else None, base)
    device = lax.axis_index("ctx")
    line, place = device // near, device % near
    small = functools.reduce(lambda a, b: a + b, [ref[...] for ref in smalls])
    small_out[...] = small
    own_line[...] = blocks[line]
    for k in range(near):
        line_send[k * piece:(k + 1) * piece] = blocks[line ^ 1, k].astype(bf16)
    line_send[near * piece:near * piece + small.shape[0]] = small.astype(bf16)
    for k in range(far - 2):
        own_far[k] = blocks[line ^ (k + 2), place]
    for turn, send in enumerate(sends, 1):
        for k in range(far - 2):
            send[k * piece:(k + 1) * piece] = blocks[line ^ (k + 2), place ^ turn].astype(bf16)
        send[(far - 2) * piece:(far - 2) * piece + small.shape[0]] = small.astype(bf16)


def first_sum_body(near, far, entries, *refs):
    own_far, own_line, small, line_got, refs = *refs[:4], refs[4:]
    plane_got, refs = refs[:near - 1], refs[near - 1:]
    kept, small_out, refs = *refs[:2], refs[2:]
    plane_sends, line_sends, total = refs[:near - 1], refs[near - 1:-1], refs[-1]
    piece = own_line.shape[1]
    count = small.shape[0]
    place = lax.axis_index("ctx") % near
    got = [ref[(far - 2) * piece:(far - 2) * piece + count].astype(f32) for ref in plane_got]
    row = lax.broadcasted_iota(jnp.int32, small.shape, 0)
    summed = jnp.where(row < entries, functools.reduce(lambda a, b: a + b, got, small[...]), got[0])
    next_line = line_got[near * piece:near * piece + count]
    small_out[...] = jnp.where(row < entries, summed + next_line.astype(f32), summed)
    for k, send in enumerate(line_sends):
        send[0:piece] = functools.reduce(
            lambda a, b: a + b[k * piece:(k + 1) * piece].astype(f32), plane_got, own_far[k]).astype(bf16)
        send[piece:piece + count] = summed.astype(bf16)
    for k in range(near):
        total[k] = own_line[k] + line_got[k * piece:(k + 1) * piece].astype(f32)
    kept[...] = total[place]
    for turn, send in enumerate(plane_sends, 1):
        send[0:piece] = total[place ^ turn].astype(bf16)
        send[piece:piece + count] = next_line


def last_sum_body(near, far, entries, *refs):
    kept, small, lat_own, refs = *refs[:3], refs[3:]
    line_got, plane_got, refs = refs[:far - 2], refs[far - 2:near + far - 3], refs[near + far - 3:]
    filter_grad, mod_grads, vector_grads, latent_grad = refs
    piece, lanes = kept.shape
    count = small.shape[0]
    total = functools.reduce(lambda a, b: a + b[0:piece].astype(f32), line_got + plane_got, kept[...])
    cols, rows = filter_grad.shape
    turned = total.T
    for part in range(lanes // cols):
        first, last = part * piece, min(rows, (part + 1) * piece)
        if first < last:
            filter_grad[:, first:last] = turned[part * cols:(part + 1) * cols, :last - first]
    got = [ref[piece:piece + count].astype(f32) for ref in line_got + plane_got]
    summed = functools.reduce(lambda a, b: a + b, got, small[...])
    split, length = mod_grads.shape[0], mod_grads.shape[0] + vector_grads.shape[0]
    for k in range(mod_grads.shape[1] // lanes):
        mod_grads[:, k * lanes:(k + 1) * lanes] = summed[k * length:k * length + split]
        vector_grads[:, k * lanes:(k + 1) * lanes] = summed[k * length + split:(k + 1) * length]
    cells, depth = lat_own.shape
    here = lax.axis_index("vid")
    for video in range(lax.axis_size("vid")):
        @pl.when(here == video)
        def _(video=video):
            latent_grad[...] = lat_own[...] + small[entries:entries + cells, video * depth:(video + 1) * depth]


def local(features, grad_out, mean, rstd, latent, gamma, beta, ws, bs, wt, bt, kernel):
    _, frames, height, width, chans = features.shape
    outs = grad_out.shape[-1]
    depth, length = latent.shape[2:]
    count, videos = lax.axis_size("ctx"), lax.axis_size("vid")
    near = math.gcd(count, NEAR)
    far = count // near
    pixels = height * width
    size = frames * pixels
    rows, cols = TAPS**3 * chans // count, outs // videos
    piece = -(-rows // (TILE * videos)) * TILE
    gamma, beta, bs, bt = (value.reshape(1, chans) for value in (gamma, beta, bs, bt))
    feats = features.reshape(size, chans)
    grads = grad_out.reshape(size, outs)

    def along_ctx(value, target):
        return lax.ppermute(value, "ctx", [(s, target(s)) for s in range(count)])

    def others(value):
        return [value] + [
            lax.ppermute(value, "vid", [(s, (s + turn) % videos) for s in range(videos)])
            for turn in range(1, videos)]

    def plane_got(values):
        return [along_ctx(value, lambda s: s ^ turn) for turn, value in enumerate(values, 1)]

    def line_got(values, first):
        turns = range(first, first + len(values))
        got = {turn: along_ctx(values[turn - first], lambda s: s ^ (turn * near)) for turn in reversed(turns)}
        return [got[turn] for turn in turns]

    beyond = lax.ppermute(grads, "ctx", [(s, s - 1) for s in range(1, count)])
    shifts = pltpu.VMEM((TAPS, frames, (height + 2) * width, outs), bf16)
    *acts, slope, normed, gain, tab, partial, latent, gamma, beta, ws, wt, grads_near, kernel = call(
        functools.partial(modulate_body, frames, height, width),
        [shaped((chans, pixels), bf16)] * frames
        + [shaped((size, chans)), shaped((size, chans)), shaped((pixels, chans)),
         shaped((length, chans)), shaped((size, chans))],
        (shifts,),
        name="modulate",
        far_args=tuple(range(12)),
        keep=(3, 4, 5, 6, 8, 10, 11),
    )(feats, mean, rstd, latent, gamma, beta, ws, bs, wt, bt, grads, kernel)
    acts_all = [value for act in acts for value in others(act)]
    grads_all = others(grads_near)
    beyond_all = others(beyond)
    cells = length // 2
    entries = (2 * depth + 4) * (chans // outs)
    count_small = -(-(entries + cells) // TILE) * TILE
    feats_grad, small, lat_own = call(
        functools.partial(input_grad_body, frames, height, width),
        (shaped((size, chans), bf16), shaped((count_small, outs)), shaped((cells, depth))),
        (shifts, pltpu.VMEM((size, chans), f32)),
        name="input_grad",
    )(beyond, kernel, partial, slope, normed, gain, tab, latent, ws, wt, gamma, beta)
    smalls = others(small)
    banks = -(-TAPS // min(videos, TAPS))
    packs = pltpu.VMEM((videos, banks, frames, (height + 2) * width, outs), bf16)
    blocks, = call(
        functools.partial(filter_own_body, frames, height, width, videos, near, piece),
        (shaped((far, near, piece, outs)),),
        (packs,),
        name="filter_own",
    )(*acts_all, *grads_all, lat_own)
    own_far, own_line, small, line_send, *plane_sends = call(
        functools.partial(filter_grad_body, frames, height, width, videos, near, piece),
        [shaped((far - 2, piece, outs)), shaped((near, piece, outs)),
         shaped((count_small, outs)), shaped((near * piece + count_small, outs), bf16)]
        + [shaped(((far - 2) * piece + count_small, outs), bf16)] * (near - 1),
        (packs, pltpu.VMEM(blocks.shape, f32)),
        name="filter_grad",
    )(*acts_all, *beyond_all, *smalls, blocks)
    line_in = line_got([line_send], 1)
    plane_in = plane_got(plane_sends)
    kept, small, *sends = call(
        functools.partial(first_sum_body, near, far, entries),
        [shaped((piece, outs)), shaped((count_small, outs))]
        + [shaped((piece + count_small, outs), bf16)] * (near + far - 3),
        (pltpu.VMEM((near, piece, outs), f32),),
        name="first_sum",
    )(own_far, own_line, small, *line_in, *plane_in)
    line_in = line_got(sends[near - 1:], 2)
    plane_in = plane_got(sends[:near - 1])
    filter_grad, mod_grads, vector_grads, latent_grad = call(
        functools.partial(last_sum_body, near, far, entries),
        (shaped((cols, rows)), shaped((2 * depth, chans)), shaped((4, chans)), shaped((cells, depth))),
        name="last_sum",
    )(kept, small, lat_own, *line_in[::-1], *plane_in)
    return (
        feats_grad.reshape(features.shape),
        filter_grad.T,
        mod_grads.reshape(2, depth, chans),
        vector_grads,
        latent_grad.T[None, None],
    )


def solution(mesh):
    split = P("vid", "ctx", None, None, None)
    return jax.shard_map(
        local,
        mesh=mesh,
        in_specs=(split, split, P("vid", None), P("vid", None), P("vid", None, None, None)) + (P(),) * 7,
        out_specs=(split, P("ctx", "vid"), P(), P(), P("vid", "ctx", None, None)),
        check_vma=False,
    )
```

```python
import functools
import math

import jax
import jax.numpy as jnp
from jax import lax
from jax.experimental import pallas as pl
from jax.experimental.pallas import tpu as pltpu
from jax.sharding import PartitionSpec as P

NEAR = 4
CELL = 4
TAPS = 3
TILE = 16

f32 = jnp.float32
bf16 = jnp.bfloat16
dot = functools.partial(lax.dot_general, preferred_element_type=f32)
exact = functools.partial(dot, precision=lax.Precision.HIGHEST)
ROWS_COLS = (((1,), (0,)), ((), ()))
ROWS_ROWS = (((1,), (1,)), ((), ()))
COLS_COLS = (((0,), (0,)), ((), ()))


def call(body, outs, scratch=(), name=None, far_args=(), keep=(), work=1000):
    outs = list(outs)
    lost = [k for k in far_args if k not in keep]

    def run(*args):
        args = [pltpu.with_memory_space_constraint(arg, pltpu.HBM) if k in far_args else arg
                for k, arg in enumerate(args)]

        def full(*refs):
            refs = list(refs)
            sems = refs.pop()
            buffers = {k: refs.pop() for k in lost[::-1]}
            first = len(args) + len(outs)
            buffers.update({k: refs.pop(first) for k in keep})
            moves = [pltpu.make_async_copy(refs[k], buffers[k], sems.at[at]) for at, k in enumerate(far_args)]
            for move in moves:
                move.start()
            for k in far_args:
                refs[k] = buffers[k]
            for move in moves:
                move.wait()
            body(*refs)

        return pl.pallas_call(
            full if far_args else body,
            out_shape=outs + [shaped(args[k].shape, args[k].dtype) for k in keep],
            in_specs=[pl.BlockSpec(memory_space=pltpu.HBM if k in far_args else pltpu.VMEM) for k in range(len(args))],
            scratch_shapes=list(scratch) + [pltpu.VMEM(args[k].shape, args[k].dtype) for k in lost]
            + ([pltpu.SemaphoreType.DMA((len(far_args),))] if far_args else []),
            name=name,
            cost_estimate=pl.CostEstimate(flops=work, bytes_accessed=work, transcendentals=0),
            compiler_params=pltpu.CompilerParams(vmem_limit_bytes=28 * 2**20),
        )(*args)

    return run


def shaped(shape, kind=f32):
    return jax.ShapeDtypeStruct(shape, kind)


def cell_matrix(height, width, cells):
    pixel = lax.broadcasted_iota(jnp.int32, (height * width, cells), 0)
    cell = lax.broadcasted_iota(jnp.int32, (height * width, cells), 1)
    place = (pixel // width) // CELL * (width // CELL) + pixel % width // CELL
    return jnp.where(place == cell, 1.0, 0.0).astype(f32)


def modulate_body(frames, height, width, feats, mean, rstd, latent, gamma, beta, ws, bs, wt, bt, grads, weights, *refs):
    acts, (slope, normed_out, gain_out, tab_out, partial, shifted) = refs[:frames], refs[frames:]
    chans = feats.shape[1]
    groups = mean.shape[1]
    pixels = height * width
    lat = latent[0, lax.axis_index("ctx") * frames // CELL]
    group = lax.broadcasted_iota(jnp.int32, (groups, chans), 0)
    chan = lax.broadcasted_iota(jnp.int32, (groups, chans), 1)
    member = jnp.where(chan // (chans // groups) == group, 1.0, 0.0).astype(f32)
    mean_chan = exact(mean[...], member, ROWS_COLS)
    rstd_chan = exact(rstd[...], member, ROWS_COLS)
    scale_tab = exact(lat, ws[...], COLS_COLS) + bs[...]
    shift_tab = exact(lat, wt[...], COLS_COLS) + bt[...]
    tab_out[...] = scale_tab
    cells = cell_matrix(height, width, lat.shape[1])
    scale_map = exact(cells, scale_tab, ROWS_COLS)
    shift_map = exact(cells, shift_tab, ROWS_COLS)
    gain_out[...] = scale_map * (gamma[...] * rstd_chan)
    for frame in range(frames):
        at = pl.ds(frame * pixels, pixels)
        normed = (feats[at, :].astype(f32) - mean_chan) * rstd_chan
        modulated = (normed * gamma[...] + beta[...]) * scale_map + shift_map
        squashed = jax.nn.sigmoid(modulated)
        normed_out[at, :] = normed
        slope[at, :] = squashed * (1.0 + modulated * (1.0 - squashed))
        acts[frame][...] = (modulated * squashed).T.astype(bf16)
    conv_own_body(frames, height, width, grads, weights, partial, shifted)


def column_shifts(value, width):
    column = lax.broadcasted_iota(jnp.int32, value.shape, 0) % width
    rows = value.shape[0]
    return (
        jnp.where(column == width - 1, 0.0, pltpu.roll(value, rows - 1, 0)),
        value,
        jnp.where(column == 0, 0.0, pltpu.roll(value, 1, 0)),
    )


def clear_borders(padded, width):
    lead = padded.shape[:-2]
    length, lanes = padded.shape[-2:]
    edge = jnp.zeros(lead + (width, lanes), padded.dtype)
    every = (slice(None),) * len(lead)
    padded[every + (slice(0, width),)] = edge
    padded[every + (slice(length - width, length),)] = edge


def put_shifts(shifted, source, frames, pixels, width):
    clear_borders(shifted, width)
    for col, value in enumerate(column_shifts(source[...].astype(f32), width)):
        for frame in range(frames):
            shifted[col, frame, width:width + pixels] = value[frame * pixels:(frame + 1) * pixels].astype(bf16)


def taps_of(weights, step, chans):
    return jnp.concatenate(
        [weights[(step * TAPS * TAPS + k) * chans:(step * TAPS * TAPS + k + 1) * chans, :]
         for k in range(TAPS * TAPS)], axis=1)


def shifted_rows(shifted, frame_list, pixels, width):
    def window(frame, row, col):
        start = (TAPS - 1 - row) * width
        return shifted[col, frame, start:start + pixels]

    return jnp.concatenate(
        [jnp.concatenate([window(frame, k // TAPS, k % TAPS) for k in range(TAPS * TAPS)], axis=1)
         for frame in frame_list], axis=0)


def add_rows(total, term, first):
    if first == 0 and term.shape[0] == total.shape[0]:
        total[...] += term
    else:
        total[first:first + term.shape[0]] += term


def conv_own_body(frames, height, width, grads, weights, total, shifted):
    pixels = height * width
    chans = total.shape[1]
    put_shifts(shifted, grads, frames, pixels, width)
    total[...] = jnp.zeros_like(total)
    for step in range(TAPS):
        pairs = [(t, t + TAPS - 1 - step) for t in range(frames) if t + TAPS - 1 - step < frames]
        if pairs:
            rows = shifted_rows(shifted, [frame for _, frame in pairs], pixels, width)
            add_rows(total, dot(rows, taps_of(weights, step, chans), ROWS_ROWS), pairs[0][0] * pixels)

    @pl.when(lax.axis_index("ctx") == 0)
    def _():
        for step in range(TAPS - 1):
            for frame in range(TAPS - 1 - step):
                rows = shifted_rows(shifted, [frame], pixels, width)
                add_rows(total, dot(rows, taps_of(weights, step, chans), ROWS_ROWS), 0)


def input_grad_body(frames, height, width, beyond, weights, partial, slope, normed, gain, tab, latent,
                    ws, wt, gamma, beta, feats_grad, small, lat_own, shifted, total):
    pixels = height * width
    chans = gain.shape[1]
    device = lax.axis_index("ctx")
    put_shifts(shifted, beyond, frames, pixels, width)
    total[...] = partial[...]
    for step in range(TAPS):
        pairs = [(t, t + TAPS - 1 - step - frames) for t in range(frames) if t + TAPS - 1 - step >= frames]
        if pairs:
            rows = shifted_rows(shifted, [frame for _, frame in pairs], pixels, width)
            add_rows(total, dot(rows, taps_of(weights, step, chans), ROWS_ROWS), pairs[0][0] * pixels)

    pooled_shift = jnp.zeros((pixels, chans), f32)
    pooled_norm = jnp.zeros((pixels, chans), f32)
    for frame in range(frames):
        at = pl.ds(frame * pixels, pixels)
        pre = total[at, :] * slope[at, :]
        feats_grad[at, :] = (pre * gain[...]).astype(bf16)
        pooled_shift += pre
        pooled_norm += pre * normed[at, :]
    lat = latent[0, device * frames // CELL]
    depth, length = lat.shape
    bands = []
    for field in (pooled_norm, pooled_shift):
        for top in range(0, height, CELL):
            rows = [field[(top + k) * width:(top + k + 1) * width] for k in range(CELL)]
            bands.append(functools.reduce(lambda a, b: a + b, rows))
    across = cell_matrix(1, width, width // CELL)
    pooled = exact(across, jnp.concatenate(bands, axis=1), COLS_COLS)
    pools = [pooled[:, k * chans:(k + 1) * chans] for k in range(len(bands))]
    norm_pool = jnp.concatenate(pools[:len(pools) // 2], axis=0)
    shift_pool = jnp.concatenate(pools[len(pools) // 2:], axis=0)
    scale_pool = norm_pool * gamma[...] + shift_pool * beta[...]
    both = jnp.concatenate([scale_pool, shift_pool], axis=1)
    mods = exact(lat, both, ROWS_COLS)
    parts = [mods[:, :chans], mods[:, chans:]]
    for field in (norm_pool * tab[...], shift_pool * tab[...], scale_pool, shift_pool):
        parts.append(jnp.sum(field, axis=0, keepdims=True))
    lanes = small.shape[1]
    small[small.shape[0] - TILE:] = jnp.zeros((TILE, lanes), f32)
    at = 0
    for k in range(chans // lanes):
        for part in parts:
            small[at:at + part.shape[0]] = part[:, k * lanes:(k + 1) * lanes]
            at += part.shape[0]
    latent_sum = exact(both, jnp.concatenate([ws[...], wt[...]], axis=1), ROWS_ROWS)
    first, second = latent_sum[:length // 2], latent_sum[length // 2:]
    even = device % 2 == 0
    lat_own[...] = jnp.where(even, first, second)
    lat_far = jnp.where(even, second, first)
    here = lax.axis_index("vid")
    for video in range(lax.axis_size("vid")):
        @pl.when(here == video)
        def _(video=video):
            small[at:at + length // 2, video * depth:(video + 1) * depth] = lat_far


class FilterParts:
    def __init__(self, frames, height, width, videos, near, piece, packs, blocks, lanes, chans):
        self.frames, self.pixels, self.width, self.videos, self.near = frames, height * width, width, videos, near
        self.piece, self.packs, self.blocks, self.lanes, self.chans = piece, packs, blocks, lanes, chans
        self.cols = lanes // videos
        self.per = min(videos, TAPS)
        self.banks = -(-TAPS // self.per)
        self.slots = [(row, bank) for row in range(TAPS) for bank in range(self.banks)]
        self.rows = TAPS**3 * chans // (blocks.shape[0] * near)

    def pack(self, sources):
        clear_borders(self.packs, self.width)
        lane = lax.broadcasted_iota(jnp.int32, (1, self.lanes), 1)
        turn = lax.rem(self.lanes - lax.axis_index("vid") * self.cols, self.lanes)
        for video, source in enumerate(sources):
            moved = column_shifts(pltpu.roll(source[...].astype(f32), turn, 1), self.width)
            for bank in range(self.banks):
                packed = moved[bank * self.per]
                for k in range(1, min(self.per, TAPS - bank * self.per)):
                    other = pltpu.roll(moved[bank * self.per + k], k * self.cols, 1)
                    packed = jnp.where(lane >= k * self.cols, other, packed)
                packed = packed.astype(bf16)
                for frame in range(self.frames):
                    self.packs[video, bank, frame, self.width:self.width + self.pixels] = (
                        packed[frame * self.pixels:(frame + 1) * self.pixels])

    def product(self, acts, pairs):
        def window(video, frame, row, bank):
            start = (TAPS - 1 - row) * self.width
            return self.packs[video, bank, frame, start:start + self.pixels]

        left = jnp.concatenate(
            [acts[t * self.videos + video][...] for video in range(self.videos) for t, _ in pairs], axis=1)
        right = jnp.concatenate(
            [jnp.concatenate([window(video, frame, row, bank) for row, bank in self.slots], axis=1)
             for video in range(self.videos) for _, frame in pairs], axis=0)
        return dot(left, right, ROWS_COLS)

    def put(self, step, result, base=None):
        for place, (row, bank) in enumerate(self.slots):
            tile = None if result is None else result[:, place * self.lanes:(place + 1) * self.lanes]
            for k in range(min(self.per, TAPS - bank * self.per)):
                tap = (step * TAPS + row) * TAPS + bank * self.per + k
                done = 0
                while done < self.chans:
                    index = tap * self.chans + done
                    owner, inside = index // self.rows, index % self.rows
                    part, at = inside // self.piece, inside % self.piece
                    length = min(self.chans - done, self.rows - inside, self.piece - at)
                    low, high = part * self.cols, (part + 1) * self.cols
                    dest = (owner // self.near, owner % self.near, slice(at, at + length), slice(low, high))
                    terms = [] if base is None else [base[dest]]
                    if tile is not None:
                        value = tile[done:done + length]
                        turn = (part - k) * self.cols % self.lanes
                        if turn:
                            value = pltpu.roll(value, turn, 1)
                        terms.append(value[:, low:high])
                    self.blocks[dest] = sum(terms[1:], terms[0]) if terms else jnp.zeros((length, self.cols), f32)
                    done += length


def filter_own_body(frames, height, width, videos, near, piece, *refs):
    acts, refs = refs[:frames * videos], refs[frames * videos:]
    grads, (_, blocks, packs) = refs[:videos], refs[videos:]
    parts = FilterParts(frames, height, width, videos, near, piece, packs, blocks, grads[0].shape[1], acts[0].shape[0])
    parts.pack(grads)
    far, lanes = blocks.shape[0], blocks.shape[3]
    first = lax.axis_index("ctx") == 0
    if piece * videos > parts.rows:
        blocks[:, :, piece - TILE:] = jnp.zeros((far, near, TILE, lanes), f32)
    for step in range(TAPS):
        pairs = [(t, t + TAPS - 1 - step) for t in range(frames) if t + TAPS - 1 - step < frames]
        parts.put(step, parts.product(acts, pairs) if pairs else None)
        if step < TAPS - 1:
            @pl.when(first)
            def _(step=step):
                extra = [parts.product(acts, [(0, frame)]) for frame in range(TAPS - 1 - step)]
                parts.put(step, functools.reduce(lambda a, b: a + b, extra), blocks)


def filter_grad_body(frames, height, width, videos, near, piece, *refs):
    acts, refs = refs[:frames * videos], refs[frames * videos:]
    beyond, refs = refs[:videos], refs[videos:]
    smalls, base, refs = refs[:videos], refs[videos], refs[videos + 1:]
    own_far, own_line, small_out, line_send, *sends, packs, blocks = refs
    parts = FilterParts(frames, height, width, videos, near, piece, packs, blocks, beyond[0].shape[1], acts[0].shape[0])
    parts.pack(beyond)
    far, lanes = blocks.shape[0], blocks.shape[3]
    if piece * videos > parts.rows:
        blocks[:, :, piece - TILE:] = jnp.zeros((far, near, TILE, lanes), f32)
    for step in range(TAPS):
        pairs = [(t, t + TAPS - 1 - step - frames) for t in range(frames) if t + TAPS - 1 - step >= frames]
        parts.put(step, parts.product(acts, pairs) if pairs else None, base)
    device = lax.axis_index("ctx")
    line, place = device // near, device % near
    small = functools.reduce(lambda a, b: a + b, [ref[...] for ref in smalls])
    small_out[...] = small
    own_line[...] = blocks[line]
    for k in range(near):
        line_send[k * piece:(k + 1) * piece] = blocks[line ^ 1, k].astype(bf16)
    line_send[near * piece:near * piece + small.shape[0]] = small.astype(bf16)
    for k in range(far - 2):
        own_far[k] = blocks[line ^ (k + 2), place]
    for turn, send in enumerate(sends, 1):
        for k in range(far - 2):
            send[k * piece:(k + 1) * piece] = blocks[line ^ (k + 2), place ^ turn].astype(bf16)
        send[(far - 2) * piece:(far - 2) * piece + small.shape[0]] = small.astype(bf16)


def first_sum_body(near, far, entries, *refs):
    own_far, own_line, small, line_got, refs = *refs[:4], refs[4:]
    plane_got, refs = refs[:near - 1], refs[near - 1:]
    kept, small_out, refs = *refs[:2], refs[2:]
    plane_sends, line_sends, total = refs[:near - 1], refs[near - 1:-1], refs[-1]
    piece = own_line.shape[1]
    count = small.shape[0]
    place = lax.axis_index("ctx") % near
    got = [ref[(far - 2) * piece:(far - 2) * piece + count].astype(f32) for ref in plane_got]
    row = lax.broadcasted_iota(jnp.int32, small.shape, 0)
    summed = jnp.where(row < entries, functools.reduce(lambda a, b: a + b, got, small[...]), got[0])
    next_line = line_got[near * piece:near * piece + count]
    small_out[...] = jnp.where(row < entries, summed + next_line.astype(f32), summed)
    for k, send in enumerate(line_sends):
        send[0:piece] = functools.reduce(
            lambda a, b: a + b[k * piece:(k + 1) * piece].astype(f32), plane_got, own_far[k]).astype(bf16)
        send[piece:piece + count] = summed.astype(bf16)
    for k in range(near):
        total[k] = own_line[k] + line_got[k * piece:(k + 1) * piece].astype(f32)
    kept[...] = total[place]
    for turn, send in enumerate(plane_sends, 1):
        send[0:piece] = total[place ^ turn].astype(bf16)
        send[piece:piece + count] = next_line


def last_sum_body(near, far, entries, *refs):
    kept, small, lat_own, refs = *refs[:3], refs[3:]
    line_got, plane_got, refs = refs[:far - 2], refs[far - 2:near + far - 3], refs[near + far - 3:]
    filter_grad, mod_grads, vector_grads, latent_grad = refs
    piece, lanes = kept.shape
    count = small.shape[0]
    total = functools.reduce(lambda a, b: a + b[0:piece].astype(f32), line_got + plane_got, kept[...])
    cols, rows = filter_grad.shape
    turned = total.T
    for part in range(lanes // cols):
        first, last = part * piece, min(rows, (part + 1) * piece)
        if first < last:
            filter_grad[:, first:last] = turned[part * cols:(part + 1) * cols, :last - first]
    got = [ref[piece:piece + count].astype(f32) for ref in line_got + plane_got]
    summed = functools.reduce(lambda a, b: a + b, got, small[...])
    split, length = mod_grads.shape[0], mod_grads.shape[0] + vector_grads.shape[0]
    for k in range(mod_grads.shape[1] // lanes):
        mod_grads[:, k * lanes:(k + 1) * lanes] = summed[k * length:k * length + split]
        vector_grads[:, k * lanes:(k + 1) * lanes] = summed[k * length + split:(k + 1) * length]
    cells, depth = lat_own.shape
    here = lax.axis_index("vid")
    for video in range(lax.axis_size("vid")):
        @pl.when(here == video)
        def _(video=video):
            latent_grad[...] = lat_own[...] + small[entries:entries + cells, video * depth:(video + 1) * depth]


def local(features, grad_out, mean, rstd, latent, gamma, beta, ws, bs, wt, bt, kernel):
    _, frames, height, width, chans = features.shape
    outs = grad_out.shape[-1]
    depth, length = latent.shape[2:]
    count, videos = lax.axis_size("ctx"), lax.axis_size("vid")
    near = math.gcd(count, NEAR)
    far = count // near
    pixels = height * width
    size = frames * pixels
    rows, cols = TAPS**3 * chans // count, outs // videos
    piece = -(-rows // (TILE * videos)) * TILE
    gamma, beta, bs, bt = (value.reshape(1, chans) for value in (gamma, beta, bs, bt))
    feats = features.reshape(size, chans)
    grads = grad_out.reshape(size, outs)

    def along_ctx(value, target):
        return lax.ppermute(value, "ctx", [(s, target(s)) for s in range(count)])

    def others(value):
        return [value] + [
            lax.ppermute(value, "vid", [(s, (s + turn) % videos) for s in range(videos)])
            for turn in range(1, videos)]

    def plane_got(values):
        return [along_ctx(value, lambda s: s ^ turn) for turn, value in enumerate(values, 1)]

    def line_got(values, first):
        turns = range(first, first + len(values))
        got = {turn: along_ctx(values[turn - first], lambda s: s ^ (turn * near)) for turn in reversed(turns)}
        return [got[turn] for turn in turns]

    beyond = lax.ppermute(grads, "ctx", [(s, s - 1) for s in range(1, count)])
    shifts = pltpu.VMEM((TAPS, frames, (height + 2) * width, outs), bf16)
    *acts, slope, normed, gain, tab, partial, latent, gamma, beta, ws, wt, grads_near, kernel = call(
        functools.partial(modulate_body, frames, height, width),
        [shaped((chans, pixels), bf16)] * frames
        + [shaped((size, chans)), shaped((size, chans)), shaped((pixels, chans)),
         shaped((length, chans)), shaped((size, chans))],
        (shifts,),
        name="modulate",
        far_args=tuple(range(12)),
        keep=(3, 4, 5, 6, 8, 10, 11),
    )(feats, mean, rstd, latent, gamma, beta, ws, bs, wt, bt, grads, kernel)
    acts_all = [value for act in acts for value in others(act)]
    grads_all = others(grads_near)
    beyond_all = others(beyond)
    cells = length // 2
    entries = (2 * depth + 4) * (chans // outs)
    count_small = -(-(entries + cells) // TILE) * TILE
    feats_grad, small, lat_own = call(
        functools.partial(input_grad_body, frames, height, width),
        (shaped((size, chans), bf16), shaped((count_small, outs)), shaped((cells, depth))),
        (shifts, pltpu.VMEM((size, chans), f32)),
        name="input_grad",
    )(beyond, kernel, partial, slope, normed, gain, tab, latent, ws, wt, gamma, beta)
    smalls = others(small)
    banks = -(-TAPS // min(videos, TAPS))
    packs = pltpu.VMEM((videos, banks, frames, (height + 2) * width, outs), bf16)
    blocks, = call(
        functools.partial(filter_own_body, frames, height, width, videos, near, piece),
        (shaped((far, near, piece, outs)),),
        (packs,),
        name="filter_own",
    )(*acts_all, *grads_all, lat_own)
    own_far, own_line, small, line_send, *plane_sends = call(
        functools.partial(filter_grad_body, frames, height, width, videos, near, piece),
        [shaped((far - 2, piece, outs)), shaped((near, piece, outs)),
         shaped((count_small, outs)), shaped((near * piece + count_small, outs), bf16)]
        + [shaped(((far - 2) * piece + count_small, outs), bf16)] * (near - 1),
        (packs, pltpu.VMEM(blocks.shape, f32)),
        name="filter_grad",
    )(*acts_all, *beyond_all, *smalls, blocks)
    line_in = line_got([line_send], 1)
    plane_in = plane_got(plane_sends)
    kept, small, *sends = call(
        functools.partial(first_sum_body, near, far, entries),
        [shaped((piece, outs)), shaped((count_small, outs))]
        + [shaped((piece + count_small, outs), bf16)] * (near + far - 3),
        (pltpu.VMEM((near, piece, outs), f32),),
        name="first_sum",
    )(own_far, own_line, small, *line_in, *plane_in)
    line_in = line_got(sends[near - 1:], 2)
    plane_in = plane_got(sends[:near - 1])
    filter_grad, mod_grads, vector_grads, latent_grad = call(
        functools.partial(last_sum_body, near, far, entries),
        (shaped((cols, rows)), shaped((2 * depth, chans)), shaped((4, chans)), shaped((cells, depth))),
        name="last_sum",
    )(kept, small, lat_own, *line_in[::-1], *plane_in[::-1])
    return (
        feats_grad.reshape(features.shape),
        filter_grad.T,
        mod_grads.reshape(2, depth, chans),
        vector_grads,
        latent_grad.T[None, None],
    )


def solution(mesh):
    split = P("vid", "ctx", None, None, None)
    return jax.shard_map(
        local,
        mesh=mesh,
        in_specs=(split, split, P("vid", None), P("vid", None), P("vid", None, None, None)) + (P(),) * 7,
        out_specs=(split, P("ctx", "vid"), P(), P(), P("vid", "ctx", None, None)),
        check_vma=False,
    )
```

```python
import functools
import math

import jax
import jax.numpy as jnp
from jax import lax
from jax.experimental import pallas as pl
from jax.experimental.pallas import tpu as pltpu
from jax.sharding import PartitionSpec as P

NEAR = 4
CELL = 4
TAPS = 3
TILE = 16

f32 = jnp.float32
bf16 = jnp.bfloat16
dot = functools.partial(lax.dot_general, preferred_element_type=f32)
exact = functools.partial(dot, precision=lax.Precision.HIGHEST)
ROWS_COLS = (((1,), (0,)), ((), ()))
ROWS_ROWS = (((1,), (1,)), ((), ()))
COLS_COLS = (((0,), (0,)), ((), ()))


def call(body, outs, scratch=(), name=None, far_args=(), keep=(), work=1000):
    outs = list(outs)
    lost = [k for k in far_args if k not in keep]

    def run(*args):
        args = [pltpu.with_memory_space_constraint(arg, pltpu.HBM) if k in far_args else arg
                for k, arg in enumerate(args)]

        def full(*refs):
            refs = list(refs)
            sems = refs.pop()
            buffers = {k: refs.pop() for k in lost[::-1]}
            first = len(args) + len(outs)
            buffers.update({k: refs.pop(first) for k in keep})
            moves = [pltpu.make_async_copy(refs[k], buffers[k], sems.at[at]) for at, k in enumerate(far_args)]
            for move in moves:
                move.start()
            for k in far_args:
                refs[k] = buffers[k]
            for move in moves:
                move.wait()
            body(*refs)

        return pl.pallas_call(
            full if far_args else body,
            out_shape=outs + [shaped(args[k].shape, args[k].dtype) for k in keep],
            in_specs=[pl.BlockSpec(memory_space=pltpu.HBM if k in far_args else pltpu.VMEM) for k in range(len(args))],
            scratch_shapes=list(scratch) + [pltpu.VMEM(args[k].shape, args[k].dtype) for k in lost]
            + ([pltpu.SemaphoreType.DMA((len(far_args),))] if far_args else []),
            name=name,
            cost_estimate=pl.CostEstimate(flops=work, bytes_accessed=work, transcendentals=0),
            compiler_params=pltpu.CompilerParams(vmem_limit_bytes=28 * 2**20),
        )(*args)

    return run


def shaped(shape, kind=f32):
    return jax.ShapeDtypeStruct(shape, kind)


def cell_matrix(height, width, cells):
    pixel = lax.broadcasted_iota(jnp.int32, (height * width, cells), 0)
    cell = lax.broadcasted_iota(jnp.int32, (height * width, cells), 1)
    place = (pixel // width) // CELL * (width // CELL) + pixel % width // CELL
    return jnp.where(place == cell, 1.0, 0.0).astype(f32)


def modulate_body(frames, height, width, feats, mean, rstd, latent, gamma, beta, ws, bs, wt, bt, grads, weights, *refs):
    acts, (slope, normed_out, gain_out, tab_out, partial, shifted) = refs[:frames], refs[frames:]
    chans = feats.shape[1]
    groups = mean.shape[1]
    pixels = height * width
    lat = latent[0, lax.axis_index("ctx") * frames // CELL]
    group = lax.broadcasted_iota(jnp.int32, (groups, chans), 0)
    chan = lax.broadcasted_iota(jnp.int32, (groups, chans), 1)
    member = jnp.where(chan // (chans // groups) == group, 1.0, 0.0).astype(f32)
    mean_chan = exact(mean[...], member, ROWS_COLS)
    rstd_chan = exact(rstd[...], member, ROWS_COLS)
    scale_tab = exact(lat, ws[...], COLS_COLS) + bs[...]
    shift_tab = exact(lat, wt[...], COLS_COLS) + bt[...]
    tab_out[...] = scale_tab
    cells = cell_matrix(height, width, lat.shape[1])
    scale_map = exact(cells, scale_tab, ROWS_COLS)
    shift_map = exact(cells, shift_tab, ROWS_COLS)
    gain_out[...] = scale_map * (gamma[...] * rstd_chan)
    for frame in range(frames):
        at = pl.ds(frame * pixels, pixels)
        normed = (feats[at, :].astype(f32) - mean_chan) * rstd_chan
        modulated = (normed * gamma[...] + beta[...]) * scale_map + shift_map
        squashed = jax.nn.sigmoid(modulated)
        normed_out[at, :] = normed
        slope[at, :] = squashed * (1.0 + modulated * (1.0 - squashed))
        acts[frame][...] = (modulated * squashed).T.astype(bf16)
    conv_own_body(frames, height, width, grads, weights, partial, shifted)


def column_shifts(value, width):
    column = lax.broadcasted_iota(jnp.int32, value.shape, 0) % width
    rows = value.shape[0]
    return (
        jnp.where(column == width - 1, 0.0, pltpu.roll(value, rows - 1, 0)),
        value,
        jnp.where(column == 0, 0.0, pltpu.roll(value, 1, 0)),
    )


def clear_borders(padded, width):
    lead = padded.shape[:-2]
    length, lanes = padded.shape[-2:]
    edge = jnp.zeros(lead + (width, lanes), padded.dtype)
    every = (slice(None),) * len(lead)
    padded[every + (slice(0, width),)] = edge
    padded[every + (slice(length - width, length),)] = edge


def put_shifts(shifted, source, frames, pixels, width):
    clear_borders(shifted, width)
    for col, value in enumerate(column_shifts(source[...].astype(f32), width)):
        for frame in range(frames):
            shifted[col, frame, width:width + pixels] = value[frame * pixels:(frame + 1) * pixels].astype(bf16)


def taps_of(weights, step, chans):
    return jnp.concatenate(
        [weights[(step * TAPS * TAPS + k) * chans:(step * TAPS * TAPS + k + 1) * chans, :]
         for k in range(TAPS * TAPS)], axis=1)


def shifted_rows(shifted, frame_list, pixels, width):
    def window(frame, row, col):
        start = (TAPS - 1 - row) * width
        return shifted[col, frame, start:start + pixels]

    return jnp.concatenate(
        [jnp.concatenate([window(frame, k // TAPS, k % TAPS) for k in range(TAPS * TAPS)], axis=1)
         for frame in frame_list], axis=0)


def add_rows(total, term, first):
    if first == 0 and term.shape[0] == total.shape[0]:
        total[...] += term
    else:
        total[first:first + term.shape[0]] += term


def conv_own_body(frames, height, width, grads, weights, total, shifted):
    pixels = height * width
    chans = total.shape[1]
    put_shifts(shifted, grads, frames, pixels, width)
    total[...] = jnp.zeros_like(total)
    for step in range(TAPS):
        pairs = [(t, t + TAPS - 1 - step) for t in range(frames) if t + TAPS - 1 - step < frames]
        if pairs:
            rows = shifted_rows(shifted, [frame for _, frame in pairs], pixels, width)
            add_rows(total, dot(rows, taps_of(weights, step, chans), ROWS_ROWS), pairs[0][0] * pixels)

    @pl.when(lax.axis_index("ctx") == 0)
    def _():
        for step in range(TAPS - 1):
            for frame in range(TAPS - 1 - step):
                rows = shifted_rows(shifted, [frame], pixels, width)
                add_rows(total, dot(rows, taps_of(weights, step, chans), ROWS_ROWS), 0)


def input_grad_body(frames, height, width, beyond, weights, partial, slope, normed, gain, tab, latent,
                    ws, wt, gamma, beta, feats_grad, small, lat_own, shifted, total):
    pixels = height * width
    chans = gain.shape[1]
    device = lax.axis_index("ctx")
    put_shifts(shifted, beyond, frames, pixels, width)
    total[...] = partial[...]
    for step in range(TAPS):
        pairs = [(t, t + TAPS - 1 - step - frames) for t in range(frames) if t + TAPS - 1 - step >= frames]
        if pairs:
            rows = shifted_rows(shifted, [frame for _, frame in pairs], pixels, width)
            add_rows(total, dot(rows, taps_of(weights, step, chans), ROWS_ROWS), pairs[0][0] * pixels)

    pooled_shift = jnp.zeros((pixels, chans), f32)
    pooled_norm = jnp.zeros((pixels, chans), f32)
    for frame in range(frames):
        at = pl.ds(frame * pixels, pixels)
        pre = total[at, :] * slope[at, :]
        feats_grad[at, :] = (pre * gain[...]).astype(bf16)
        pooled_shift += pre
        pooled_norm += pre * normed[at, :]
    lat = latent[0, device * frames // CELL]
    depth, length = lat.shape
    bands = []
    for field in (pooled_norm, pooled_shift):
        for top in range(0, height, CELL):
            rows = [field[(top + k) * width:(top + k + 1) * width] for k in range(CELL)]
            bands.append(functools.reduce(lambda a, b: a + b, rows))
    across = cell_matrix(1, width, width // CELL)
    pooled = exact(across, jnp.concatenate(bands, axis=1), COLS_COLS)
    pools = [pooled[:, k * chans:(k + 1) * chans] for k in range(len(bands))]
    norm_pool = jnp.concatenate(pools[:len(pools) // 2], axis=0)
    shift_pool = jnp.concatenate(pools[len(pools) // 2:], axis=0)
    scale_pool = norm_pool * gamma[...] + shift_pool * beta[...]
    both = jnp.concatenate([scale_pool, shift_pool], axis=1)
    mods = exact(lat, both, ROWS_COLS)
    parts = [mods[:, :chans], mods[:, chans:]]
    for field in (norm_pool * tab[...], shift_pool * tab[...], scale_pool, shift_pool):
        parts.append(jnp.sum(field, axis=0, keepdims=True))
    lanes = small.shape[1]
    small[small.shape[0] - TILE:] = jnp.zeros((TILE, lanes), f32)
    at = 0
    for k in range(chans // lanes):
        for part in parts:
            small[at:at + part.shape[0]] = part[:, k * lanes:(k + 1) * lanes]
            at += part.shape[0]
    latent_sum = exact(both, jnp.concatenate([ws[...], wt[...]], axis=1), ROWS_ROWS)
    first, second = latent_sum[:length // 2], latent_sum[length // 2:]
    even = device % 2 == 0
    lat_own[...] = jnp.where(even, first, second)
    lat_far = jnp.where(even, second, first)
    here = lax.axis_index("vid")
    for video in range(lax.axis_size("vid")):
        @pl.when(here == video)
        def _(video=video):
            small[at:at + length // 2, video * depth:(video + 1) * depth] = lat_far


class FilterParts:
    def __init__(self, frames, height, width, videos, near, piece, packs, blocks, lanes, chans):
        self.frames, self.pixels, self.width, self.videos, self.near = frames, height * width, width, videos, near
        self.piece, self.packs, self.blocks, self.lanes, self.chans = piece, packs, blocks, lanes, chans
        self.cols = lanes // videos
        self.per = min(videos, TAPS)
        self.banks = -(-TAPS // self.per)
        self.slots = [(row, bank) for row in range(TAPS) for bank in range(self.banks)]
        self.rows = TAPS**3 * chans // (blocks.shape[0] * near)

    def pack(self, sources):
        clear_borders(self.packs, self.width)
        lane = lax.broadcasted_iota(jnp.int32, (1, self.lanes), 1)
        turn = lax.rem(self.lanes - lax.axis_index("vid") * self.cols, self.lanes)
        for video, source in enumerate(sources):
            moved = column_shifts(pltpu.roll(source[...].astype(f32), turn, 1), self.width)
            for bank in range(self.banks):
                packed = moved[bank * self.per]
                for k in range(1, min(self.per, TAPS - bank * self.per)):
                    other = pltpu.roll(moved[bank * self.per + k], k * self.cols, 1)
                    packed = jnp.where(lane >= k * self.cols, other, packed)
                packed = packed.astype(bf16)
                for frame in range(self.frames):
                    self.packs[video, bank, frame, self.width:self.width + self.pixels] = (
                        packed[frame * self.pixels:(frame + 1) * self.pixels])

    def product(self, acts, pairs):
        def window(video, frame, row, bank):
            start = (TAPS - 1 - row) * self.width
            return self.packs[video, bank, frame, start:start + self.pixels]

        left = jnp.concatenate(
            [acts[t * self.videos + video][...] for video in range(self.videos) for t, _ in pairs], axis=1)
        right = jnp.concatenate(
            [jnp.concatenate([window(video, frame, row, bank) for row, bank in self.slots], axis=1)
             for video in range(self.videos) for _, frame in pairs], axis=0)
        return dot(left, right, ROWS_COLS)

    def put(self, step, result, base=None):
        for place, (row, bank) in enumerate(self.slots):
            tile = None if result is None else result[:, place * self.lanes:(place + 1) * self.lanes]
            for k in range(min(self.per, TAPS - bank * self.per)):
                tap = (step * TAPS + row) * TAPS + bank * self.per + k
                done = 0
                while done < self.chans:
                    index = tap * self.chans + done
                    owner, inside = index // self.rows, index % self.rows
                    part, at = inside // self.piece, inside % self.piece
                    length = min(self.chans - done, self.rows - inside, self.piece - at)
                    low, high = part * self.cols, (part + 1) * self.cols
                    dest = (owner // self.near, owner % self.near, slice(at, at + length), slice(low, high))
                    terms = [] if base is None else [base[dest]]
                    if tile is not None:
                        value = tile[done:done + length]
                        turn = (part - k) * self.cols % self.lanes
                        if turn:
                            value = pltpu.roll(value, turn, 1)
                        terms.append(value[:, low:high])
                    self.blocks[dest] = sum(terms[1:], terms[0]) if terms else jnp.zeros((length, self.cols), f32)
                    done += length


def filter_own_body(frames, height, width, videos, near, piece, *refs):
    acts, refs = refs[:frames * videos], refs[frames * videos:]
    grads, (_, blocks, packs) = refs[:videos], refs[videos:]
    parts = FilterParts(frames, height, width, videos, near, piece, packs, blocks, grads[0].shape[1], acts[0].shape[0])
    parts.pack(grads)
    far, lanes = blocks.shape[0], blocks.shape[3]
    first = lax.axis_index("ctx") == 0
    if piece * videos > parts.rows:
        blocks[:, :, piece - TILE:] = jnp.zeros((far, near, TILE, lanes), f32)
    for step in range(TAPS):
        pairs = [(t, t + TAPS - 1 - step) for t in range(frames) if t + TAPS - 1 - step < frames]
        if pairs:
            parts.put(step, parts.product(acts, pairs))
        if step < TAPS - 1:
            @pl.when(first)
            def _(step=step, pairs=pairs):
                extra = [parts.product(acts, [(0, frame)]) for frame in range(TAPS - 1 - step)]
                parts.put(step, functools.reduce(lambda a, b: a + b, extra), blocks if pairs else None)


def filter_grad_body(frames, height, width, videos, near, piece, *refs):
    acts, refs = refs[:frames * videos], refs[frames * videos:]
    beyond, refs = refs[:videos], refs[videos:]
    smalls, base, refs = refs[:videos], refs[videos], refs[videos + 1:]
    own_far, own_line, small_out, line_send, *sends, packs, blocks = refs
    parts = FilterParts(frames, height, width, videos, near, piece, packs, blocks, beyond[0].shape[1], acts[0].shape[0])
    parts.pack(beyond)
    far, lanes = blocks.shape[0], blocks.shape[3]
    if piece * videos > parts.rows:
        blocks[:, :, piece - TILE:] = jnp.zeros((far, near, TILE, lanes), f32)
    for step in range(TAPS):
        pairs = [(t, t + TAPS - 1 - step - frames) for t in range(frames) if t + TAPS - 1 - step >= frames]
        result = parts.product(acts, pairs) if pairs else None
        if TAPS - 1 - step < frames:
            parts.put(step, result, base)
        else:
            first = lax.axis_index("ctx") == 0
            pl.when(first)(functools.partial(parts.put, step, result, base))
            pl.when(jnp.logical_not(first))(functools.partial(parts.put, step, result))
    device = lax.axis_index("ctx")
    line, place = device // near, device % near
    small = functools.reduce(lambda a, b: a + b, [ref[...] for ref in smalls])
    small_out[...] = small
    own_line[...] = blocks[line]
    for k in range(near):
        line_send[k * piece:(k + 1) * piece] = blocks[line ^ 1, k].astype(bf16)
    line_send[near * piece:near * piece + small.shape[0]] = small.astype(bf16)
    for k in range(far - 2):
        own_far[k] = blocks[line ^ (k + 2), place]
    for turn, send in enumerate(sends, 1):
        for k in range(far - 2):
            send[k * piece:(k + 1) * piece] = blocks[line ^ (k + 2), place ^ turn].astype(bf16)
        send[(far - 2) * piece:(far - 2) * piece + small.shape[0]] = small.astype(bf16)


def first_sum_body(near, far, entries, *refs):
    own_far, own_line, small, line_got, refs = *refs[:4], refs[4:]
    plane_got, refs = refs[:near - 1], refs[near - 1:]
    kept, small_out, refs = *refs[:2], refs[2:]
    plane_sends, line_sends, total = refs[:near - 1], refs[near - 1:-1], refs[-1]
    piece = own_line.shape[1]
    count = small.shape[0]
    place = lax.axis_index("ctx") % near
    got = [ref[(far - 2) * piece:(far - 2) * piece + count].astype(f32) for ref in plane_got]
    row = lax.broadcasted_iota(jnp.int32, small.shape, 0)
    summed = jnp.where(row < entries, functools.reduce(lambda a, b: a + b, got, small[...]), got[0])
    next_line = line_got[near * piece:near * piece + count]
    small_out[...] = jnp.where(row < entries, summed + next_line.astype(f32), summed)
    for k, send in enumerate(line_sends):
        send[0:piece] = functools.reduce(
            lambda a, b: a + b[k * piece:(k + 1) * piece].astype(f32), plane_got, own_far[k]).astype(bf16)
        send[piece:piece + count] = summed.astype(bf16)
    for k in range(near):
        total[k] = own_line[k] + line_got[k * piece:(k + 1) * piece].astype(f32)
    kept[...] = total[place]
    for turn, send in enumerate(plane_sends, 1):
        send[0:piece] = total[place ^ turn].astype(bf16)
        send[piece:piece + count] = next_line


def last_sum_body(near, far, entries, *refs):
    kept, small, lat_own, refs = *refs[:3], refs[3:]
    line_got, plane_got, refs = refs[:far - 2], refs[far - 2:near + far - 3], refs[near + far - 3:]
    filter_grad, mod_grads, vector_grads, latent_grad = refs
    piece, lanes = kept.shape
    count = small.shape[0]
    total = functools.reduce(lambda a, b: a + b[0:piece].astype(f32), line_got + plane_got, kept[...])
    cols, rows = filter_grad.shape
    turned = total.T
    for part in range(lanes // cols):
        first, last = part * piece, min(rows, (part + 1) * piece)
        if first < last:
            filter_grad[:, first:last] = turned[part * cols:(part + 1) * cols, :last - first]
    got = [ref[piece:piece + count].astype(f32) for ref in line_got + plane_got]
    summed = functools.reduce(lambda a, b: a + b, got, small[...])
    split, length = mod_grads.shape[0], mod_grads.shape[0] + vector_grads.shape[0]
    for k in range(mod_grads.shape[1] // lanes):
        mod_grads[:, k * lanes:(k + 1) * lanes] = summed[k * length:k * length + split]
        vector_grads[:, k * lanes:(k + 1) * lanes] = summed[k * length + split:(k + 1) * length]
    cells, depth = lat_own.shape
    here = lax.axis_index("vid")
    for video in range(lax.axis_size("vid")):
        @pl.when(here == video)
        def _(video=video):
            latent_grad[...] = lat_own[...] + small[entries:entries + cells, video * depth:(video + 1) * depth]


def local(features, grad_out, mean, rstd, latent, gamma, beta, ws, bs, wt, bt, kernel):
    _, frames, height, width, chans = features.shape
    outs = grad_out.shape[-1]
    depth, length = latent.shape[2:]
    count, videos = lax.axis_size("ctx"), lax.axis_size("vid")
    near = math.gcd(count, NEAR)
    far = count // near
    pixels = height * width
    size = frames * pixels
    rows, cols = TAPS**3 * chans // count, outs // videos
    piece = -(-rows // (TILE * videos)) * TILE
    gamma, beta, bs, bt = (value.reshape(1, chans) for value in (gamma, beta, bs, bt))
    feats = features.reshape(size, chans)
    grads = grad_out.reshape(size, outs)

    def along_ctx(value, target):
        return lax.ppermute(value, "ctx", [(s, target(s)) for s in range(count)])

    def others(value):
        return [value] + [
            lax.ppermute(value, "vid", [(s, (s + turn) % videos) for s in range(videos)])
            for turn in range(1, videos)]

    def plane_got(values):
        return [along_ctx(value, lambda s: s ^ turn) for turn, value in enumerate(values, 1)]

    def line_got(values, first):
        turns = range(first, first + len(values))
        got = {turn: along_ctx(values[turn - first], lambda s: s ^ (turn * near)) for turn in reversed(turns)}
        return [got[turn] for turn in turns]

    beyond = lax.ppermute(grads, "ctx", [(s, s - 1) for s in range(1, count)])
    shifts = pltpu.VMEM((TAPS, frames, (height + 2) * width, outs), bf16)
    *acts, slope, normed, gain, tab, partial, latent, gamma, beta, ws, wt, grads_near, kernel = call(
        functools.partial(modulate_body, frames, height, width),
        [shaped((chans, pixels), bf16)] * frames
        + [shaped((size, chans)), shaped((size, chans)), shaped((pixels, chans)),
         shaped((length, chans)), shaped((size, chans))],
        (shifts,),
        name="modulate",
        far_args=tuple(range(12)),
        keep=(3, 4, 5, 6, 8, 10, 11),
    )(feats, mean, rstd, latent, gamma, beta, ws, bs, wt, bt, grads, kernel)
    acts_all = [value for act in acts for value in others(act)]
    grads_all = others(grads_near)
    beyond_all = others(beyond)
    cells = length // 2
    entries = (2 * depth + 4) * (chans // outs)
    count_small = -(-(entries + cells) // TILE) * TILE
    feats_grad, small, lat_own = call(
        functools.partial(input_grad_body, frames, height, width),
        (shaped((size, chans), bf16), shaped((count_small, outs)), shaped((cells, depth))),
        (shifts, pltpu.VMEM((size, chans), f32)),
        name="input_grad",
    )(beyond, kernel, partial, slope, normed, gain, tab, latent, ws, wt, gamma, beta)
    smalls = others(small)
    banks = -(-TAPS // min(videos, TAPS))
    packs = pltpu.VMEM((videos, banks, frames, (height + 2) * width, outs), bf16)
    blocks, = call(
        functools.partial(filter_own_body, frames, height, width, videos, near, piece),
        (shaped((far, near, piece, outs)),),
        (packs,),
        name="filter_own",
    )(*acts_all, *grads_all, lat_own)
    own_far, own_line, small, line_send, *plane_sends = call(
        functools.partial(filter_grad_body, frames, height, width, videos, near, piece),
        [shaped((far - 2, piece, outs)), shaped((near, piece, outs)),
         shaped((count_small, outs)), shaped((near * piece + count_small, outs), bf16)]
        + [shaped(((far - 2) * piece + count_small, outs), bf16)] * (near - 1),
        (packs, pltpu.VMEM(blocks.shape, f32)),
        name="filter_grad",
    )(*acts_all, *beyond_all, *smalls, blocks)
    line_in = line_got([line_send], 1)
    plane_in = plane_got(plane_sends)
    kept, small, *sends = call(
        functools.partial(first_sum_body, near, far, entries),
        [shaped((piece, outs)), shaped((count_small, outs))]
        + [shaped((piece + count_small, outs), bf16)] * (near + far - 3),
        (pltpu.VMEM((near, piece, outs), f32),),
        name="first_sum",
    )(own_far, own_line, small, *line_in, *plane_in)
    line_in = line_got(sends[near - 1:], 2)
    plane_in = plane_got(sends[:near - 1])
    filter_grad, mod_grads, vector_grads, latent_grad = call(
        functools.partial(last_sum_body, near, far, entries),
        (shaped((cols, rows)), shaped((2 * depth, chans)), shaped((4, chans)), shaped((cells, depth))),
        name="last_sum",
    )(kept, small, lat_own, *line_in, *plane_in[::-1])
    return (
        feats_grad.reshape(features.shape),
        filter_grad.T,
        mod_grads.reshape(2, depth, chans),
        vector_grads,
        latent_grad.T[None, None],
    )


def solution(mesh):
    split = P("vid", "ctx", None, None, None)
    return jax.shard_map(
        local,
        mesh=mesh,
        in_specs=(split, split, P("vid", None), P("vid", None), P("vid", None, None, None)) + (P(),) * 7,
        out_specs=(split, P("ctx", "vid"), P(), P(), P("vid", "ctx", None, None)),
        check_vma=False,
    )
```

```python
import functools
import math

import jax
import jax.numpy as jnp
from jax import lax
from jax.experimental import pallas as pl
from jax.experimental.pallas import tpu as pltpu
from jax.sharding import PartitionSpec as P

NEAR = 4
CELL = 4
TAPS = 3
TILE = 16

f32 = jnp.float32
bf16 = jnp.bfloat16
dot = functools.partial(lax.dot_general, preferred_element_type=f32)
exact = functools.partial(dot, precision=lax.Precision.HIGHEST)
ROWS_COLS = (((1,), (0,)), ((), ()))
ROWS_ROWS = (((1,), (1,)), ((), ()))
COLS_COLS = (((0,), (0,)), ((), ()))


def call(body, outs, scratch=(), name=None, far_args=(), keep=(), work=1000):
    outs = list(outs)
    lost = [k for k in far_args if k not in keep]

    def run(*args):
        args = [pltpu.with_memory_space_constraint(arg, pltpu.HBM) if k in far_args else arg
                for k, arg in enumerate(args)]

        def full(*refs):
            refs = list(refs)
            sems = refs.pop()
            buffers = {k: refs.pop() for k in lost[::-1]}
            first = len(args) + len(outs)
            buffers.update({k: refs.pop(first) for k in keep})
            moves = [pltpu.make_async_copy(refs[k], buffers[k], sems.at[at]) for at, k in enumerate(far_args)]
            for move in moves:
                move.start()
            for k in far_args:
                refs[k] = buffers[k]
            for move in moves:
                move.wait()
            body(*refs)

        return pl.pallas_call(
            full if far_args else body,
            out_shape=outs + [shaped(args[k].shape, args[k].dtype) for k in keep],
            in_specs=[pl.BlockSpec(memory_space=pltpu.HBM if k in far_args else pltpu.VMEM) for k in range(len(args))],
            scratch_shapes=list(scratch) + [pltpu.VMEM(args[k].shape, args[k].dtype) for k in lost]
            + ([pltpu.SemaphoreType.DMA((len(far_args),))] if far_args else []),
            name=name,
            cost_estimate=pl.CostEstimate(flops=work, bytes_accessed=work, transcendentals=0),
            compiler_params=pltpu.CompilerParams(vmem_limit_bytes=28 * 2**20),
        )(*args)

    return run


def shaped(shape, kind=f32):
    return jax.ShapeDtypeStruct(shape, kind)


def cell_matrix(height, width, cells):
    pixel = lax.broadcasted_iota(jnp.int32, (height * width, cells), 0)
    cell = lax.broadcasted_iota(jnp.int32, (height * width, cells), 1)
    place = (pixel // width) // CELL * (width // CELL) + pixel % width // CELL
    return jnp.where(place == cell, 1.0, 0.0).astype(f32)


def modulate_body(frames, height, width, feats, mean, rstd, latent, gamma, beta, ws, bs, wt, bt, grads, weights, *refs):
    acts, (slope, normed_out, gain_out, tab_out, partial, shifted) = refs[:frames], refs[frames:]
    chans = feats.shape[1]
    groups = mean.shape[1]
    pixels = height * width
    lat = latent[0, lax.axis_index("ctx") * frames // CELL]
    group = lax.broadcasted_iota(jnp.int32, (groups, chans), 0)
    chan = lax.broadcasted_iota(jnp.int32, (groups, chans), 1)
    member = jnp.where(chan // (chans // groups) == group, 1.0, 0.0).astype(f32)
    mean_chan = exact(mean[...], member, ROWS_COLS)
    rstd_chan = exact(rstd[...], member, ROWS_COLS)
    scale_tab = exact(lat, ws[...], COLS_COLS) + bs[...]
    shift_tab = exact(lat, wt[...], COLS_COLS) + bt[...]
    tab_out[...] = scale_tab
    cells = cell_matrix(height, width, lat.shape[1])
    scale_map = exact(cells, scale_tab, ROWS_COLS)
    shift_map = exact(cells, shift_tab, ROWS_COLS)
    gain_out[...] = scale_map * (gamma[...] * rstd_chan)
    for frame in range(frames):
        at = pl.ds(frame * pixels, pixels)
        normed = (feats[at, :].astype(f32) - mean_chan) * rstd_chan
        modulated = (normed * gamma[...] + beta[...]) * scale_map + shift_map
        squashed = jax.nn.sigmoid(modulated)
        normed_out[at, :] = normed
        slope[at, :] = squashed * (1.0 + modulated * (1.0 - squashed))
        acts[frame][...] = (modulated * squashed).T.astype(bf16)
    conv_own_body(frames, height, width, grads, weights, partial, shifted)


def column_shifts(value, width):
    column = lax.broadcasted_iota(jnp.int32, value.shape, 0) % width
    rows = value.shape[0]
    return (
        jnp.where(column == width - 1, 0.0, pltpu.roll(value, rows - 1, 0)),
        value,
        jnp.where(column == 0, 0.0, pltpu.roll(value, 1, 0)),
    )


def clear_borders(padded, width):
    lead = padded.shape[:-2]
    length, lanes = padded.shape[-2:]
    edge = jnp.zeros(lead + (width, lanes), padded.dtype)
    every = (slice(None),) * len(lead)
    padded[every + (slice(0, width),)] = edge
    padded[every + (slice(length - width, length),)] = edge


def put_shifts(shifted, source, frames, pixels, width):
    clear_borders(shifted, width)
    for col, value in enumerate(column_shifts(source[...].astype(f32), width)):
        for frame in range(frames):
            shifted[col, frame, width:width + pixels] = value[frame * pixels:(frame + 1) * pixels].astype(bf16)


def taps_of(weights, step, chans):
    return jnp.concatenate(
        [weights[(step * TAPS * TAPS + k) * chans:(step * TAPS * TAPS + k + 1) * chans, :]
         for k in range(TAPS * TAPS)], axis=1)


def shifted_rows(shifted, frame_list, pixels, width):
    def window(frame, row, col):
        start = (TAPS - 1 - row) * width
        return shifted[col, frame, start:start + pixels]

    return jnp.concatenate(
        [jnp.concatenate([window(frame, k // TAPS, k % TAPS) for k in range(TAPS * TAPS)], axis=1)
         for frame in frame_list], axis=0)


def add_rows(total, term, first):
    if first == 0 and term.shape[0] == total.shape[0]:
        total[...] += term
    else:
        total[first:first + term.shape[0]] += term


def conv_own_body(frames, height, width, grads, weights, total, shifted):
    pixels = height * width
    chans = total.shape[1]
    put_shifts(shifted, grads, frames, pixels, width)
    total[...] = jnp.zeros_like(total)
    for step in range(TAPS):
        pairs = [(t, t + TAPS - 1 - step) for t in range(frames) if t + TAPS - 1 - step < frames]
        if pairs:
            rows = shifted_rows(shifted, [frame for _, frame in pairs], pixels, width)
            add_rows(total, dot(rows, taps_of(weights, step, chans), ROWS_ROWS), pairs[0][0] * pixels)

    @pl.when(lax.axis_index("ctx") == 0)
    def _():
        for step in range(TAPS - 1):
            for frame in range(TAPS - 1 - step):
                rows = shifted_rows(shifted, [frame], pixels, width)
                add_rows(total, dot(rows, taps_of(weights, step, chans), ROWS_ROWS), 0)


def input_grad_body(frames, height, width, beyond, weights, partial, slope, normed, gain, tab, latent,
                    ws, wt, gamma, beta, feats_grad, small, lat_own, shifted, total):
    pixels = height * width
    chans = gain.shape[1]
    device = lax.axis_index("ctx")
    put_shifts(shifted, beyond, frames, pixels, width)
    total[...] = partial[...]
    for step in range(TAPS):
        pairs = [(t, t + TAPS - 1 - step - frames) for t in range(frames) if t + TAPS - 1 - step >= frames]
        if pairs:
            rows = shifted_rows(shifted, [frame for _, frame in pairs], pixels, width)
            add_rows(total, dot(rows, taps_of(weights, step, chans), ROWS_ROWS), pairs[0][0] * pixels)

    pooled_shift = jnp.zeros((pixels, chans), f32)
    pooled_norm = jnp.zeros((pixels, chans), f32)
    for frame in range(frames):
        at = pl.ds(frame * pixels, pixels)
        pre = total[at, :] * slope[at, :]
        feats_grad[at, :] = (pre * gain[...]).astype(bf16)
        pooled_shift += pre
        pooled_norm += pre * normed[at, :]
    lat = latent[0, device * frames // CELL]
    depth, length = lat.shape
    bands = []
    for field in (pooled_norm, pooled_shift):
        for top in range(0, height, CELL):
            rows = [field[(top + k) * width:(top + k + 1) * width] for k in range(CELL)]
            bands.append(functools.reduce(lambda a, b: a + b, rows))
    across = cell_matrix(1, width, width // CELL)
    pooled = exact(across, jnp.concatenate(bands, axis=1), COLS_COLS)
    pools = [pooled[:, k * chans:(k + 1) * chans] for k in range(len(bands))]
    norm_pool = jnp.concatenate(pools[:len(pools) // 2], axis=0)
    shift_pool = jnp.concatenate(pools[len(pools) // 2:], axis=0)
    scale_pool = norm_pool * gamma[...] + shift_pool * beta[...]
    both = jnp.concatenate([scale_pool, shift_pool], axis=1)
    mods = exact(lat, both, ROWS_COLS)
    parts = [mods[:, :chans], mods[:, chans:]]
    for field in (norm_pool * tab[...], shift_pool * tab[...], scale_pool, shift_pool):
        parts.append(jnp.sum(field, axis=0, keepdims=True))
    lanes = small.shape[1]
    small[small.shape[0] - TILE:] = jnp.zeros((TILE, lanes), f32)
    at = 0
    for k in range(chans // lanes):
        for part in parts:
            small[at:at + part.shape[0]] = part[:, k * lanes:(k + 1) * lanes]
            at += part.shape[0]
    latent_sum = exact(both, jnp.concatenate([ws[...], wt[...]], axis=1), ROWS_ROWS)
    first, second = latent_sum[:length // 2], latent_sum[length // 2:]
    even = device % 2 == 0
    lat_own[...] = jnp.where(even, first, second)
    lat_far = jnp.where(even, second, first)
    here = lax.axis_index("vid")
    for video in range(lax.axis_size("vid")):
        @pl.when(here == video)
        def _(video=video):
            small[at:at + length // 2, video * depth:(video + 1) * depth] = lat_far


class FilterParts:
    def __init__(self, frames, height, width, videos, near, piece, packs, blocks, lanes, chans):
        self.frames, self.pixels, self.width, self.videos, self.near = frames, height * width, width, videos, near
        self.piece, self.packs, self.blocks, self.lanes, self.chans = piece, packs, blocks, lanes, chans
        self.cols = lanes // videos
        self.per = min(videos, TAPS)
        self.banks = -(-TAPS // self.per)
        self.slots = [(row, bank) for row in range(TAPS) for bank in range(self.banks)]
        self.rows = TAPS**3 * chans // (blocks.shape[0] * near)

    def pack(self, sources):
        clear_borders(self.packs, self.width)
        lane = lax.broadcasted_iota(jnp.int32, (1, self.lanes), 1)
        turn = lax.rem(self.lanes - lax.axis_index("vid") * self.cols, self.lanes)
        for video, source in enumerate(sources):
            moved = column_shifts(pltpu.roll(source[...].astype(f32), turn, 1), self.width)
            for bank in range(self.banks):
                packed = moved[bank * self.per]
                for k in range(1, min(self.per, TAPS - bank * self.per)):
                    other = pltpu.roll(moved[bank * self.per + k], k * self.cols, 1)
                    packed = jnp.where(lane >= k * self.cols, other, packed)
                packed = packed.astype(bf16)
                for frame in range(self.frames):
                    self.packs[video, bank, frame, self.width:self.width + self.pixels] = (
                        packed[frame * self.pixels:(frame + 1) * self.pixels])

    def product(self, acts, pairs):
        def window(video, frame, row, bank):
            start = (TAPS - 1 - row) * self.width
            return self.packs[video, bank, frame, start:start + self.pixels]

        left = jnp.concatenate(
            [acts[t * self.videos + video][...] for video in range(self.videos) for t, _ in pairs], axis=1)
        right = jnp.concatenate(
            [jnp.concatenate([window(video, frame, row, bank) for row, bank in self.slots], axis=1)
             for video in range(self.videos) for _, frame in pairs], axis=0)
        return dot(left, right, ROWS_COLS)

    def put(self, step, result, base=None):
        for place, (row, bank) in enumerate(self.slots):
            tile = None if result is None else result[:, place * self.lanes:(place + 1) * self.lanes]
            for k in range(min(self.per, TAPS - bank * self.per)):
                tap = (step * TAPS + row) * TAPS + bank * self.per + k
                done = 0
                while done < self.chans:
                    index = tap * self.chans + done
                    owner, inside = index // self.rows, index % self.rows
                    part, at = inside // self.piece, inside % self.piece
                    length = min(self.chans - done, self.rows - inside, self.piece - at)
                    low, high = part * self.cols, (part + 1) * self.cols
                    dest = (owner // self.near, owner % self.near, slice(at, at + length), slice(low, high))
                    terms = [] if base is None else [base[dest]]
                    if tile is not None:
                        value = tile[done:done + length]
                        turn = (part - k) * self.cols % self.lanes
                        if turn:
                            value = pltpu.roll(value, turn, 1)
                        terms.append(value[:, low:high])
                    self.blocks[dest] = sum(terms[1:], terms[0]) if terms else jnp.zeros((length, self.cols), f32)
                    done += length


def filter_own_body(frames, height, width, videos, near, piece, *refs):
    acts, refs = refs[:frames * videos], refs[frames * videos:]
    grads, (_, blocks, packs) = refs[:videos], refs[videos:]
    parts = FilterParts(frames, height, width, videos, near, piece, packs, blocks, grads[0].shape[1], acts[0].shape[0])
    parts.pack(grads)
    far, lanes = blocks.shape[0], blocks.shape[3]
    first = lax.axis_index("ctx") == 0
    if piece * videos > parts.rows:
        blocks[:, :, piece - TILE:] = jnp.zeros((far, near, TILE, lanes), f32)
    for step in range(TAPS):
        pairs = [(t, t + TAPS - 1 - step) for t in range(frames) if t + TAPS - 1 - step < frames]
        parts.put(step, parts.product(acts, pairs) if pairs else None)
        if step < TAPS - 1:
            @pl.when(first)
            def _(step=step):
                extra = [parts.product(acts, [(0, frame)]) for frame in range(TAPS - 1 - step)]
                parts.put(step, functools.reduce(lambda a, b: a + b, extra), blocks)


def filter_grad_body(frames, height, width, videos, near, piece, *refs):
    acts, refs = refs[:frames * videos], refs[frames * videos:]
    beyond, refs = refs[:videos], refs[videos:]
    smalls, base, refs = refs[:videos], refs[videos], refs[videos + 1:]
    own_far, own_line, small_out, line_send, *sends, packs, blocks = refs
    parts = FilterParts(frames, height, width, videos, near, piece, packs, blocks, beyond[0].shape[1], acts[0].shape[0])
    parts.pack(beyond)
    far, lanes = blocks.shape[0], blocks.shape[3]
    if piece * videos > parts.rows:
        blocks[:, :, piece - TILE:] = jnp.zeros((far, near, TILE, lanes), f32)
    for step in range(TAPS):
        pairs = [(t, t + TAPS - 1 - step - frames) for t in range(frames) if t + TAPS - 1 - step >= frames]
        parts.put(step, parts.product(acts, pairs) if pairs else None, base)
    device = lax.axis_index("ctx")
    line, place = device // near, device % near
    small = functools.reduce(lambda a, b: a + b, [ref[...] for ref in smalls])
    small_out[...] = small
    own_line[...] = blocks[line]
    for k in range(near):
        line_send[k * piece:(k + 1) * piece] = blocks[line ^ 1, k].astype(bf16)
    line_send[near * piece:near * piece + small.shape[0]] = small.astype(bf16)
    for k in range(far - 2):
        own_far[k] = blocks[line ^ (k + 2), place]
    for turn, send in enumerate(sends, 1):
        for k in range(far - 2):
            send[k * piece:(k + 1) * piece] = blocks[line ^ (k + 2), place ^ turn].astype(bf16)
        send[(far - 2) * piece:(far - 2) * piece + small.shape[0]] = small.astype(bf16)


def first_sum_body(near, far, entries, *refs):
    own_far, own_line, small, line_got, refs = *refs[:4], refs[4:]
    plane_got, refs = refs[:near - 1], refs[near - 1:]
    kept, small_out, refs = *refs[:2], refs[2:]
    plane_sends, line_sends, total = refs[:near - 1], refs[near - 1:-1], refs[-1]
    piece = own_line.shape[1]
    count = small.shape[0]
    place = lax.axis_index("ctx") % near
    got = [ref[(far - 2) * piece:(far - 2) * piece + count].astype(f32) for ref in plane_got]
    row = lax.broadcasted_iota(jnp.int32, small.shape, 0)
    summed = jnp.where(row < entries, functools.reduce(lambda a, b: a + b, got, small[...]), got[0])
    next_line = line_got[near * piece:near * piece + count]
    small_out[...] = jnp.where(row < entries, summed + next_line.astype(f32), summed)
    for k, send in enumerate(line_sends):
        send[0:piece] = functools.reduce(
            lambda a, b: a + b[k * piece:(k + 1) * piece].astype(f32), plane_got, own_far[k]).astype(bf16)
        send[piece:piece + count] = summed.astype(bf16)
    for k in range(near):
        total[k] = own_line[k] + line_got[k * piece:(k + 1) * piece].astype(f32)
    kept[...] = total[place]
    for turn, send in enumerate(plane_sends, 1):
        send[0:piece] = total[place ^ turn].astype(bf16)
        send[piece:piece + count] = next_line


def last_sum_body(near, far, entries, *refs):
    kept, small, lat_own, refs = *refs[:3], refs[3:]
    got, (filter_grad, mod_grads, vector_grads, latent_grad) = refs[:near + far - 3], refs[near + far - 3:]
    piece, lanes = kept.shape
    count = small.shape[0]
    total = functools.reduce(lambda a, b: a + b[0:piece].astype(f32), got, kept[...])
    cols, rows = filter_grad.shape
    turned = total.T
    for part in range(lanes // cols):
        first, last = part * piece, min(rows, (part + 1) * piece)
        if first < last:
            filter_grad[:, first:last] = turned[part * cols:(part + 1) * cols, :last - first]
    summed = functools.reduce(lambda a, b: a + b[piece:piece + count].astype(f32), got, small[...])
    split, length = mod_grads.shape[0], mod_grads.shape[0] + vector_grads.shape[0]
    for k in range(mod_grads.shape[1] // lanes):
        mod_grads[:, k * lanes:(k + 1) * lanes] = summed[k * length:k * length + split]
        vector_grads[:, k * lanes:(k + 1) * lanes] = summed[k * length + split:(k + 1) * length]
    cells, depth = lat_own.shape
    here = lax.axis_index("vid")
    for video in range(lax.axis_size("vid")):
        @pl.when(here == video)
        def _(video=video):
            latent_grad[...] = lat_own[...] + small[entries:entries + cells, video * depth:(video + 1) * depth]


def local(features, grad_out, mean, rstd, latent, gamma, beta, ws, bs, wt, bt, kernel):
    _, frames, height, width, chans = features.shape
    outs = grad_out.shape[-1]
    depth, length = latent.shape[2:]
    count, videos = lax.axis_size("ctx"), lax.axis_size("vid")
    near = math.gcd(count, NEAR)
    far = count // near
    pixels = height * width
    size = frames * pixels
    rows, cols = TAPS**3 * chans // count, outs // videos
    piece = -(-rows // (TILE * videos)) * TILE
    gamma, beta, bs, bt = (value.reshape(1, chans) for value in (gamma, beta, bs, bt))
    feats = features.reshape(size, chans)
    grads = grad_out.reshape(size, outs)

    def along_ctx(value, target):
        return lax.ppermute(value, "ctx", [(s, target(s)) for s in range(count)])

    def others(value):
        return [value] + [
            lax.ppermute(value, "vid", [(s, (s + turn) % videos) for s in range(videos)])
            for turn in range(1, videos)]

    def plane_got(values):
        return [along_ctx(value, lambda s: s ^ turn) for turn, value in enumerate(values, 1)]

    def line_got(values, first):
        turns = range(first, first + len(values))
        got = {turn: along_ctx(values[turn - first], lambda s: s ^ (turn * near)) for turn in reversed(turns)}
        return [got[turn] for turn in turns]

    beyond = lax.ppermute(grads, "ctx", [(s, s - 1) for s in range(1, count)])
    shifts = pltpu.VMEM((TAPS, frames, (height + 2) * width, outs), bf16)
    *acts, slope, normed, gain, tab, partial, latent, gamma, beta, ws, wt, grads_near, kernel = call(
        functools.partial(modulate_body, frames, height, width),
        [shaped((chans, pixels), bf16)] * frames
        + [shaped((size, chans)), shaped((size, chans)), shaped((pixels, chans)),
         shaped((length, chans)), shaped((size, chans))],
        (shifts,),
        name="modulate",
        far_args=tuple(range(12)),
        keep=(3, 4, 5, 6, 8, 10, 11),
    )(feats, mean, rstd, latent, gamma, beta, ws, bs, wt, bt, grads, kernel)
    acts_all = [value for act in acts for value in others(act)]
    grads_all = others(grads_near)
    beyond_all = others(beyond)
    cells = length // 2
    entries = (2 * depth + 4) * (chans // outs)
    count_small = -(-(entries + cells) // TILE) * TILE
    feats_grad, small, lat_own = call(
        functools.partial(input_grad_body, frames, height, width),
        (shaped((size, chans), bf16), shaped((count_small, outs)), shaped((cells, depth))),
        (shifts, pltpu.VMEM((size, chans), f32)),
        name="input_grad",
    )(beyond, kernel, partial, slope, normed, gain, tab, latent, ws, wt, gamma, beta)
    smalls = others(small)
    banks = -(-TAPS // min(videos, TAPS))
    packs = pltpu.VMEM((videos, banks, frames, (height + 2) * width, outs), bf16)
    blocks, = call(
        functools.partial(filter_own_body, frames, height, width, videos, near, piece),
        (shaped((far, near, piece, outs)),),
        (packs,),
        name="filter_own",
    )(*acts_all, *grads_all, lat_own)
    own_far, own_line, small, line_send, *plane_sends = call(
        functools.partial(filter_grad_body, frames, height, width, videos, near, piece),
        [shaped((far - 2, piece, outs)), shaped((near, piece, outs)),
         shaped((count_small, outs)), shaped((near * piece + count_small, outs), bf16)]
        + [shaped(((far - 2) * piece + count_small, outs), bf16)] * (near - 1),
        (packs, pltpu.VMEM(blocks.shape, f32)),
        name="filter_grad",
    )(*acts_all, *beyond_all, *smalls, blocks)
    line_in = line_got([line_send], 1)
    plane_in = plane_got(plane_sends)
    kept, small, *sends = call(
        functools.partial(first_sum_body, near, far, entries),
        [shaped((piece, outs)), shaped((count_small, outs))]
        + [shaped((piece + count_small, outs), bf16)] * (near + far - 3),
        (pltpu.VMEM((near, piece, outs), f32),),
        name="first_sum",
    )(own_far, own_line, small, *line_in, *plane_in)
    line_in = line_got(sends[near - 1:], 2)
    plane_in = plane_got(sends[:near - 1])
    filter_grad, mod_grads, vector_grads, latent_grad = call(
        functools.partial(last_sum_body, near, far, entries),
        (shaped((cols, rows)), shaped((2 * depth, chans)), shaped((4, chans)), shaped((cells, depth))),
        name="last_sum",
    )(kept, small, lat_own, *line_in[:1], *plane_in[:2], *line_in[1:], *plane_in[2:])
    return (
        feats_grad.reshape(features.shape),
        filter_grad.T,
        mod_grads.reshape(2, depth, chans),
        vector_grads,
        latent_grad.T[None, None],
    )


def solution(mesh):
    split = P("vid", "ctx", None, None, None)
    return jax.shard_map(
        local,
        mesh=mesh,
        in_specs=(split, split, P("vid", None), P("vid", None), P("vid", None, None, None)) + (P(),) * 7,
        out_specs=(split, P("ctx", "vid"), P(), P(), P("vid", "ctx", None, None)),
        check_vma=False,
    )
```

```python
import functools
import math

import jax
import jax.numpy as jnp
from jax import lax
from jax.experimental import pallas as pl
from jax.experimental.pallas import tpu as pltpu
from jax.sharding import PartitionSpec as P

NEAR = 4
CELL = 4
TAPS = 3
TILE = 16

f32 = jnp.float32
bf16 = jnp.bfloat16
dot = functools.partial(lax.dot_general, preferred_element_type=f32)
exact = functools.partial(dot, precision=lax.Precision.HIGHEST)
ROWS_COLS = (((1,), (0,)), ((), ()))
ROWS_ROWS = (((1,), (1,)), ((), ()))
COLS_COLS = (((0,), (0,)), ((), ()))


def call(body, outs, scratch=(), name=None, far_args=(), keep=(), work=1000):
    outs = list(outs)
    lost = [k for k in far_args if k not in keep]

    def run(*args):
        args = [pltpu.with_memory_space_constraint(arg, pltpu.HBM) if k in far_args else arg
                for k, arg in enumerate(args)]

        def full(*refs):
            refs = list(refs)
            sems = refs.pop()
            buffers = {k: refs.pop() for k in lost[::-1]}
            first = len(args) + len(outs)
            buffers.update({k: refs.pop(first) for k in keep})
            moves = [pltpu.make_async_copy(refs[k], buffers[k], sems.at[at]) for at, k in enumerate(far_args)]
            for move in moves:
                move.start()
            for k in far_args:
                refs[k] = buffers[k]
            for move in moves:
                move.wait()
            body(*refs)

        return pl.pallas_call(
            full if far_args else body,
            out_shape=outs + [shaped(args[k].shape, args[k].dtype) for k in keep],
            in_specs=[pl.BlockSpec(memory_space=pltpu.HBM if k in far_args else pltpu.VMEM) for k in range(len(args))],
            scratch_shapes=list(scratch) + [pltpu.VMEM(args[k].shape, args[k].dtype) for k in lost]
            + ([pltpu.SemaphoreType.DMA((len(far_args),))] if far_args else []),
            name=name,
            cost_estimate=pl.CostEstimate(flops=work, bytes_accessed=work, transcendentals=0),
            compiler_params=pltpu.CompilerParams(vmem_limit_bytes=28 * 2**20),
        )(*args)

    return run


def shaped(shape, kind=f32):
    return jax.ShapeDtypeStruct(shape, kind)


def cell_matrix(height, width, cells):
    pixel = lax.broadcasted_iota(jnp.int32, (height * width, cells), 0)
    cell = lax.broadcasted_iota(jnp.int32, (height * width, cells), 1)
    place = (pixel // width) // CELL * (width // CELL) + pixel % width // CELL
    return jnp.where(place == cell, 1.0, 0.0).astype(f32)


def modulate_body(frames, height, width, feats, mean, rstd, latent, gamma, beta, ws, bs, wt, bt, grads, weights, *refs):
    acts, (slope, normed_out, gain_out, tab_out, partial, shifted) = refs[:frames], refs[frames:]
    chans = feats.shape[1]
    groups = mean.shape[1]
    pixels = height * width
    lat = latent[0, lax.axis_index("ctx") * frames // CELL]
    group = lax.broadcasted_iota(jnp.int32, (groups, chans), 0)
    chan = lax.broadcasted_iota(jnp.int32, (groups, chans), 1)
    member = jnp.where(chan // (chans // groups) == group, 1.0, 0.0).astype(f32)
    mean_chan = exact(mean[...], member, ROWS_COLS)
    rstd_chan = exact(rstd[...], member, ROWS_COLS)
    scale_tab = exact(lat, ws[...], COLS_COLS) + bs[...]
    shift_tab = exact(lat, wt[...], COLS_COLS) + bt[...]
    tab_out[...] = scale_tab
    cells = cell_matrix(height, width, lat.shape[1])
    scale_map = exact(cells, scale_tab, ROWS_COLS)
    shift_map = exact(cells, shift_tab, ROWS_COLS)
    gain_out[...] = scale_map * (gamma[...] * rstd_chan)
    for frame in range(frames):
        at = pl.ds(frame * pixels, pixels)
        normed = (feats[at, :].astype(f32) - mean_chan) * rstd_chan
        modulated = (normed * gamma[...] + beta[...]) * scale_map + shift_map
        squashed = jax.nn.sigmoid(modulated)
        normed_out[at, :] = normed
        slope[at, :] = squashed * (1.0 + modulated * (1.0 - squashed))
        acts[frame][...] = (modulated * squashed).T.astype(bf16)
    conv_own_body(frames, height, width, grads, weights, partial, shifted)


def column_shifts(value, width):
    column = lax.broadcasted_iota(jnp.int32, value.shape, 0) % width
    rows = value.shape[0]
    return (
        jnp.where(column == width - 1, 0.0, pltpu.roll(value, rows - 1, 0)),
        value,
        jnp.where(column == 0, 0.0, pltpu.roll(value, 1, 0)),
    )


def clear_borders(padded, width):
    lead = padded.shape[:-2]
    length, lanes = padded.shape[-2:]
    edge = jnp.zeros(lead + (width, lanes), padded.dtype)
    every = (slice(None),) * len(lead)
    padded[every + (slice(0, width),)] = edge
    padded[every + (slice(length - width, length),)] = edge


def put_shifts(shifted, source, frames, pixels, width):
    clear_borders(shifted, width)
    for col, value in enumerate(column_shifts(source[...].astype(f32), width)):
        for frame in range(frames):
            shifted[col, frame, width:width + pixels] = value[frame * pixels:(frame + 1) * pixels].astype(bf16)


def taps_of(weights, step, chans):
    return jnp.concatenate(
        [weights[(step * TAPS * TAPS + k) * chans:(step * TAPS * TAPS + k + 1) * chans, :]
         for k in range(TAPS * TAPS)], axis=1)


def shifted_rows(shifted, frame_list, pixels, width):
    def window(frame, row, col):
        start = (TAPS - 1 - row) * width
        return shifted[col, frame, start:start + pixels]

    return jnp.concatenate(
        [jnp.concatenate([window(frame, k // TAPS, k % TAPS) for k in range(TAPS * TAPS)], axis=1)
         for frame in frame_list], axis=0)


def add_rows(total, term, first):
    if first == 0 and term.shape[0] == total.shape[0]:
        total[...] += term
    else:
        total[first:first + term.shape[0]] += term


def conv_own_body(frames, height, width, grads, weights, total, shifted):
    pixels = height * width
    chans = total.shape[1]
    put_shifts(shifted, grads, frames, pixels, width)
    total[...] = jnp.zeros_like(total)
    for step in range(TAPS):
        pairs = [(t, t + TAPS - 1 - step) for t in range(frames) if t + TAPS - 1 - step < frames]
        if pairs:
            rows = shifted_rows(shifted, [frame for _, frame in pairs], pixels, width)
            add_rows(total, dot(rows, taps_of(weights, step, chans), ROWS_ROWS), pairs[0][0] * pixels)

    @pl.when(lax.axis_index("ctx") == 0)
    def _():
        for step in range(TAPS - 1):
            for frame in range(TAPS - 1 - step):
                rows = shifted_rows(shifted, [frame], pixels, width)
                add_rows(total, dot(rows, taps_of(weights, step, chans), ROWS_ROWS), 0)


def input_grad_body(frames, height, width, beyond, weights, partial, slope, normed, gain, tab, latent,
                    ws, wt, gamma, beta, feats_grad, small, lat_own, shifted, total):
    pixels = height * width
    chans = gain.shape[1]
    device = lax.axis_index("ctx")
    put_shifts(shifted, beyond, frames, pixels, width)
    filled = False
    for step in range(TAPS):
        pairs = [(t, t + TAPS - 1 - step - frames) for t in range(frames) if t + TAPS - 1 - step >= frames]
        if pairs:
            rows = shifted_rows(shifted, [frame for _, frame in pairs], pixels, width)
            term = dot(rows, taps_of(weights, step, chans), ROWS_ROWS)
            if not filled and len(pairs) < frames:
                total[...] = partial[...]
            if filled or len(pairs) < frames:
                add_rows(total, term, pairs[0][0] * pixels)
            else:
                total[...] = partial[...] + term
            filled = True

    pooled_shift = jnp.zeros((pixels, chans), f32)
    pooled_norm = jnp.zeros((pixels, chans), f32)
    for frame in range(frames):
        at = pl.ds(frame * pixels, pixels)
        pre = total[at, :] * slope[at, :]
        feats_grad[at, :] = (pre * gain[...]).astype(bf16)
        pooled_shift += pre
        pooled_norm += pre * normed[at, :]
    lat = latent[0, device * frames // CELL]
    depth, length = lat.shape
    bands = []
    for field in (pooled_norm, pooled_shift):
        for top in range(0, height, CELL):
            rows = [field[(top + k) * width:(top + k + 1) * width] for k in range(CELL)]
            bands.append(functools.reduce(lambda a, b: a + b, rows))
    across = cell_matrix(1, width, width // CELL)
    pooled = exact(across, jnp.concatenate(bands, axis=1), COLS_COLS)
    pools = [pooled[:, k * chans:(k + 1) * chans] for k in range(len(bands))]
    norm_pool = jnp.concatenate(pools[:len(pools) // 2], axis=0)
    shift_pool = jnp.concatenate(pools[len(pools) // 2:], axis=0)
    scale_pool = norm_pool * gamma[...] + shift_pool * beta[...]
    both = jnp.concatenate([scale_pool, shift_pool], axis=1)
    mods = exact(lat, both, ROWS_COLS)
    parts = [mods[:, :chans], mods[:, chans:]]
    for field in (norm_pool * tab[...], shift_pool * tab[...], scale_pool, shift_pool):
        parts.append(jnp.sum(field, axis=0, keepdims=True))
    lanes = small.shape[1]
    small[small.shape[0] - TILE:] = jnp.zeros((TILE, lanes), f32)
    at = 0
    for k in range(chans // lanes):
        for part in parts:
            small[at:at + part.shape[0]] = part[:, k * lanes:(k + 1) * lanes]
            at += part.shape[0]
    latent_sum = exact(both, jnp.concatenate([ws[...], wt[...]], axis=1), ROWS_ROWS)
    first, second = latent_sum[:length // 2], latent_sum[length // 2:]
    even = device % 2 == 0
    lat_own[...] = jnp.where(even, first, second)
    lat_far = jnp.where(even, second, first)
    here = lax.axis_index("vid")
    for video in range(lax.axis_size("vid")):
        @pl.when(here == video)
        def _(video=video):
            small[at:at + length // 2, video * depth:(video + 1) * depth] = lat_far


class FilterParts:
    def __init__(self, frames, height, width, videos, near, piece, packs, blocks, lanes, chans):
        self.frames, self.pixels, self.width, self.videos, self.near = frames, height * width, width, videos, near
        self.piece, self.packs, self.blocks, self.lanes, self.chans = piece, packs, blocks, lanes, chans
        self.cols = lanes // videos
        self.per = min(videos, TAPS)
        self.banks = -(-TAPS // self.per)
        self.slots = [(row, bank) for row in range(TAPS) for bank in range(self.banks)]
        self.rows = TAPS**3 * chans // (blocks.shape[0] * near)

    def pack(self, sources):
        clear_borders(self.packs, self.width)
        lane = lax.broadcasted_iota(jnp.int32, (1, self.lanes), 1)
        turn = lax.rem(self.lanes - lax.axis_index("vid") * self.cols, self.lanes)
        for video, source in enumerate(sources):
            moved = column_shifts(pltpu.roll(source[...].astype(f32), turn, 1), self.width)
            for bank in range(self.banks):
                packed = moved[bank * self.per]
                for k in range(1, min(self.per, TAPS - bank * self.per)):
                    other = pltpu.roll(moved[bank * self.per + k], k * self.cols, 1)
                    packed = jnp.where(lane >= k * self.cols, other, packed)
                packed = packed.astype(bf16)
                for frame in range(self.frames):
                    self.packs[video, bank, frame, self.width:self.width + self.pixels] = (
                        packed[frame * self.pixels:(frame + 1) * self.pixels])

    def product(self, acts, pairs):
        def window(video, frame, row, bank):
            start = (TAPS - 1 - row) * self.width
            return self.packs[video, bank, frame, start:start + self.pixels]

        left = jnp.concatenate(
            [acts[t * self.videos + video][...] for video in range(self.videos) for t, _ in pairs], axis=1)
        right = jnp.concatenate(
            [jnp.concatenate([window(video, frame, row, bank) for row, bank in self.slots], axis=1)
             for video in range(self.videos) for _, frame in pairs], axis=0)
        return dot(left, right, ROWS_COLS)

    def put(self, step, result, base=None, present=None):
        for place, (row, bank) in enumerate(self.slots):
            tile = None if result is None else result[:, place * self.lanes:(place + 1) * self.lanes]
            for k in range(min(self.per, TAPS - bank * self.per)):
                tap = (step * TAPS + row) * TAPS + bank * self.per + k
                done = 0
                while done < self.chans:
                    index = tap * self.chans + done
                    owner, inside = index // self.rows, index % self.rows
                    part, at = inside // self.piece, inside % self.piece
                    length = min(self.chans - done, self.rows - inside, self.piece - at)
                    low, high = part * self.cols, (part + 1) * self.cols
                    dest = (owner // self.near, owner % self.near, slice(at, at + length), slice(low, high))
                    terms = [] if base is None else [base[dest]]
                    if present is not None:
                        terms = [jnp.where(present, terms[0], 0.0)]
                    if tile is not None:
                        value = tile[done:done + length]
                        turn = (part - k) * self.cols % self.lanes
                        if turn:
                            value = pltpu.roll(value, turn, 1)
                        terms.append(value[:, low:high])
                    self.blocks[dest] = sum(terms[1:], terms[0]) if terms else jnp.zeros((length, self.cols), f32)
                    done += length


def filter_own_body(frames, height, width, videos, near, piece, *refs):
    acts, refs = refs[:frames * videos], refs[frames * videos:]
    grads, (_, blocks, packs) = refs[:videos], refs[videos:]
    parts = FilterParts(frames, height, width, videos, near, piece, packs, blocks, grads[0].shape[1], acts[0].shape[0])
    parts.pack(grads)
    far, lanes = blocks.shape[0], blocks.shape[3]
    first = lax.axis_index("ctx") == 0
    if piece * videos > parts.rows:
        blocks[:, :, piece - TILE:] = jnp.zeros((far, near, TILE, lanes), f32)
    for step in range(TAPS):
        pairs = [(t, t + TAPS - 1 - step) for t in range(frames) if t + TAPS - 1 - step < frames]
        if pairs:
            parts.put(step, parts.product(acts, pairs))
        if step < TAPS - 1:
            @pl.when(first)
            def _(step=step, pairs=pairs):
                extra = [parts.product(acts, [(0, frame)]) for frame in range(TAPS - 1 - step)]
                parts.put(step, functools.reduce(lambda a, b: a + b, extra), blocks if pairs else None)


def filter_grad_body(frames, height, width, videos, near, piece, *refs):
    acts, refs = refs[:frames * videos], refs[frames * videos:]
    beyond, refs = refs[:videos], refs[videos:]
    smalls, base, refs = refs[:videos], refs[videos], refs[videos + 1:]
    own_far, own_line, small_out, line_send, *sends, packs, blocks = refs
    parts = FilterParts(frames, height, width, videos, near, piece, packs, blocks, beyond[0].shape[1], acts[0].shape[0])
    parts.pack(beyond)
    far, lanes = blocks.shape[0], blocks.shape[3]
    if piece * videos > parts.rows:
        blocks[:, :, piece - TILE:] = jnp.zeros((far, near, TILE, lanes), f32)
    for step in range(TAPS):
        pairs = [(t, t + TAPS - 1 - step - frames) for t in range(frames) if t + TAPS - 1 - step >= frames]
        present = None if TAPS - 1 - step < frames else lax.axis_index("ctx") == 0
        parts.put(step, parts.product(acts, pairs) if pairs else None, base, present)
    device = lax.axis_index("ctx")
    line, place = device // near, device % near
    small = functools.reduce(lambda a, b: a + b, [ref[...] for ref in smalls])
    small_out[...] = small
    own_line[...] = blocks[line]
    for k in range(near):
        line_send[k * piece:(k + 1) * piece] = blocks[line ^ 1, k].astype(bf16)
    line_send[near * piece:near * piece + small.shape[0]] = small.astype(bf16)
    for k in range(far - 2):
        own_far[k] = blocks[line ^ (k + 2), place]
    for turn, send in enumerate(sends, 1):
        for k in range(far - 2):
            send[k * piece:(k + 1) * piece] = blocks[line ^ (k + 2), place ^ turn].astype(bf16)
        send[(far - 2) * piece:(far - 2) * piece + small.shape[0]] = small.astype(bf16)


def first_sum_body(near, far, entries, *refs):
    own_far, own_line, small, line_got, refs = *refs[:4], refs[4:]
    plane_got, refs = refs[:near - 1], refs[near - 1:]
    kept, small_out, refs = *refs[:2], refs[2:]
    plane_sends, line_sends, total = refs[:near - 1], refs[near - 1:-1], refs[-1]
    piece = own_line.shape[1]
    count = small.shape[0]
    place = lax.axis_index("ctx") % near
    got = [ref[(far - 2) * piece:(far - 2) * piece + count].astype(f32) for ref in plane_got]
    row = lax.broadcasted_iota(jnp.int32, small.shape, 0)
    summed = jnp.where(row < entries, functools.reduce(lambda a, b: a + b, got, small[...]), got[0])
    next_line = line_got[near * piece:near * piece + count]
    small_out[...] = jnp.where(row < entries, summed + next_line.astype(f32), summed)
    for k, send in enumerate(line_sends):
        send[0:piece] = functools.reduce(
            lambda a, b: a + b[k * piece:(k + 1) * piece].astype(f32), plane_got, own_far[k]).astype(bf16)
        send[piece:piece + count] = summed.astype(bf16)
    for k in range(near):
        total[k] = own_line[k] + line_got[k * piece:(k + 1) * piece].astype(f32)
    kept[...] = total[place]
    for turn, send in enumerate(plane_sends, 1):
        send[0:piece] = total[place ^ turn].astype(bf16)
        send[piece:piece + count] = next_line


def last_sum_body(near, far, entries, *refs):
    kept, small, lat_own, refs = *refs[:3], refs[3:]
    got, (filter_grad, mod_grads, vector_grads, latent_grad) = refs[:near + far - 3], refs[near + far - 3:]
    piece, lanes = kept.shape
    count = small.shape[0]
    total = functools.reduce(lambda a, b: a + b[0:piece].astype(f32), got, kept[...])
    cols, rows = filter_grad.shape
    turned = total.T
    for part in range(lanes // cols):
        first, last = part * piece, min(rows, (part + 1) * piece)
        if first < last:
            filter_grad[:, first:last] = turned[part * cols:(part + 1) * cols, :last - first]
    summed = functools.reduce(lambda a, b: a + b[piece:piece + count].astype(f32), got, small[...])
    split, length = mod_grads.shape[0], mod_grads.shape[0] + vector_grads.shape[0]
    for k in range(mod_grads.shape[1] // lanes):
        mod_grads[:, k * lanes:(k + 1) * lanes] = summed[k * length:k * length + split]
        vector_grads[:, k * lanes:(k + 1) * lanes] = summed[k * length + split:(k + 1) * length]
    cells, depth = lat_own.shape
    here = lax.axis_index("vid")
    for video in range(lax.axis_size("vid")):
        @pl.when(here == video)
        def _(video=video):
            latent_grad[...] = lat_own[...] + small[entries:entries + cells, video * depth:(video + 1) * depth]


def local(features, grad_out, mean, rstd, latent, gamma, beta, ws, bs, wt, bt, kernel):
    _, frames, height, width, chans = features.shape
    outs = grad_out.shape[-1]
    depth, length = latent.shape[2:]
    count, videos = lax.axis_size("ctx"), lax.axis_size("vid")
    near = math.gcd(count, NEAR)
    far = count // near
    pixels = height * width
    size = frames * pixels
    rows, cols = TAPS**3 * chans // count, outs // videos
    piece = -(-rows // (TILE * videos)) * TILE
    gamma, beta, bs, bt = (value.reshape(1, chans) for value in (gamma, beta, bs, bt))
    feats = features.reshape(size, chans)
    grads = grad_out.reshape(size, outs)

    def along_ctx(value, target):
        return lax.ppermute(value, "ctx", [(s, target(s)) for s in range(count)])

    def others(value):
        return [value] + [
            lax.ppermute(value, "vid", [(s, (s + turn) % videos) for s in range(videos)])
            for turn in range(1, videos)]

    def plane_got(values):
        return [along_ctx(value, lambda s: s ^ turn) for turn, value in enumerate(values, 1)]

    def line_got(values, first):
        turns = range(first, first + len(values))
        got = {turn: along_ctx(values[turn - first], lambda s: s ^ (turn * near)) for turn in reversed(turns)}
        return [got[turn] for turn in turns]

    beyond = lax.ppermute(grads, "ctx", [(s, s - 1) for s in range(1, count)])
    shifts = pltpu.VMEM((TAPS, frames, (height + 2) * width, outs), bf16)
    *acts, slope, normed, gain, tab, partial, latent, gamma, beta, ws, wt, grads_near, kernel = call(
        functools.partial(modulate_body, frames, height, width),
        [shaped((chans, pixels), bf16)] * frames
        + [shaped((size, chans)), shaped((size, chans)), shaped((pixels, chans)),
         shaped((length, chans)), shaped((size, chans))],
        (shifts,),
        name="modulate",
        far_args=tuple(range(12)),
        keep=(3, 4, 5, 6, 8, 10, 11),
    )(feats, mean, rstd, latent, gamma, beta, ws, bs, wt, bt, grads, kernel)
    acts_all = [value for act in acts for value in others(act)]
    grads_all = others(grads_near)
    beyond_all = others(beyond)
    cells = length // 2
    entries = (2 * depth + 4) * (chans // outs)
    count_small = -(-(entries + cells) // TILE) * TILE
    feats_grad, small, lat_own = call(
        functools.partial(input_grad_body, frames, height, width),
        (shaped((size, chans), bf16), shaped((count_small, outs)), shaped((cells, depth))),
        (shifts, pltpu.VMEM((size, chans), f32)),
        name="input_grad",
    )(beyond, kernel, partial, slope, normed, gain, tab, latent, ws, wt, gamma, beta)
    smalls = others(small)
    banks = -(-TAPS // min(videos, TAPS))
    packs = pltpu.VMEM((videos, banks, frames, (height + 2) * width, outs), bf16)
    blocks, = call(
        functools.partial(filter_own_body, frames, height, width, videos, near, piece),
        (shaped((far, near, piece, outs)),),
        (packs,),
        name="filter_own",
    )(*acts_all, *grads_all, lat_own)
    own_far, own_line, small, line_send, *plane_sends = call(
        functools.partial(filter_grad_body, frames, height, width, videos, near, piece),
        [shaped((far - 2, piece, outs)), shaped((near, piece, outs)),
         shaped((count_small, outs)), shaped((near * piece + count_small, outs), bf16)]
        + [shaped(((far - 2) * piece + count_small, outs), bf16)] * (near - 1),
        (packs, pltpu.VMEM(blocks.shape, f32)),
        name="filter_grad",
    )(*acts_all, *beyond_all, *smalls, blocks)
    line_in = line_got([line_send], 1)
    plane_in = plane_got(plane_sends)
    kept, small, *sends = call(
        functools.partial(first_sum_body, near, far, entries),
        [shaped((piece, outs)), shaped((count_small, outs))]
        + [shaped((piece + count_small, outs), bf16)] * (near + far - 3),
        (pltpu.VMEM((near, piece, outs), f32),),
        name="first_sum",
    )(own_far, own_line, small, *line_in, *plane_in)
    line_in = line_got(sends[near - 1:], 2)
    plane_in = plane_got(sends[:near - 1])
    filter_grad, mod_grads, vector_grads, latent_grad = call(
        functools.partial(last_sum_body, near, far, entries),
        (shaped((cols, rows)), shaped((2 * depth, chans)), shaped((4, chans)), shaped((cells, depth))),
        name="last_sum",
    )(kept, small, lat_own, *line_in[:1], *plane_in[:2], *line_in[1:], *plane_in[2:])
    return (
        feats_grad.reshape(features.shape),
        filter_grad.T,
        mod_grads.reshape(2, depth, chans),
        vector_grads,
        latent_grad.T[None, None],
    )


def solution(mesh):
    split = P("vid", "ctx", None, None, None)
    return jax.shard_map(
        local,
        mesh=mesh,
        in_specs=(split, split, P("vid", None), P("vid", None), P("vid", None, None, None)) + (P(),) * 7,
        out_specs=(split, P("ctx", "vid"), P(), P(), P("vid", "ctx", None, None)),
        check_vma=False,
    )
```
